128 devices in a mesh: row: 2 (over y_hi), inst: 4 (over x), mesh: 16 (over y_lo, z, core).
Axes of the slice: x: 4, y: 4 (y_hi: 2, y_lo: 2; y = y_hi * 2 + y_lo), z: 4, core: 2. Of those that a mesh axis runs over, the one named last changes fastest.
Arguments:
- state: float32 [2, 8, 6, 128, 64, 128], P('row', 'inst', None, 'mesh'), may hold values from -6 to 6
- viscosity: float32 [2, 128, 64, 128], P('row', 'mesh'), may hold values from 0.05 to 0.5
- blade_counts: int32 [2], replicated, may hold values from 20 to 79
- mode_orders: int32 [8], replicated, may hold values from 1 to 63
Outputs:
- new_state: float32 [2, 8, 6, 128, 64, 128], P('row', 'inst', None, 'mesh')
- residual: float32 [2, 8, 6, 128, 64, 128], P('row', 'inst', None, 'mesh')
The draws below stay inside these ranges and needn't reach their ends.
All inputs are finite; a program needn't handle non-finite values.
Results may differ from the reference program's by a relative error of at most 0.0001.
Values sent between devices are 32-bit elements; how exact they have to be, the bound alone decides.
No kernel may reach another device: no remote copies, remote signals or barrier semaphores. Data moves between devices by JAX's collectives and lax.ppermute only.
A program may use at most 128 MiB of HBM per device.

```python
import math
import jax
import jax.numpy as jnp
from jax import lax

NV = 6
NA = 64
NR = 128
NMODE = 8
INST = 8
NP = 128


def set_ends(entries, rng, low, high):
    index_at = [jax.random.randint(jax.random.fold_in(rng, axis), (), 0, length) for axis, length in enumerate(entries.shape)]
    main_axis = entries.shape.index(max(entries.shape))
    next_to = index_at[:main_axis] + [(index_at[main_axis] + 1) % entries.shape[main_axis]] + index_at[main_axis + 1:]
    return entries.at[tuple(index_at)].set(low).at[tuple(next_to)].set(high)


def levels(stream_key, extent, pieces, smallest, top_value):
    def one(axis_at, shards_of):
        draws = jax.random.uniform(jax.random.fold_in(jax.random.fold_in(stream_key, 6), axis_at), (shards_of,), jnp.float32, smallest / len(pieces), top_value / len(pieces))
        return jnp.repeat(jnp.exp(draws), extent[axis_at] // shards_of).reshape((-1,) + (1,) * (len(extent) - axis_at - 1))

    factor_of = one(*pieces[0])
    for cut in pieces[1:]:
        factor_of = factor_of * one(*cut)
    return factor_of


def normal_values(own_key, dims, width, reach, split=(), dtype=jnp.bfloat16):
    gain = levels(own_key, dims, split, -0.22, 0.18) if split else 1.0
    entries = jax.random.normal(own_key, dims, jnp.float32) * width * gain
    return jnp.minimum(jnp.maximum(entries, -reach), reach).astype(dtype)


def setup_inputs(seed: int = 0) -> dict:
    splits = jax.random.split(jax.random.key(seed), 5)
    state = normal_values(splits[0], (2, INST, NV, NP, NA, NR), 1.0, 6.0, ((0, 2), (1, 4), (3, 16)), jnp.float32)
    viscosity = jnp.clip(jnp.exp(math.log(0.5) - 2.3025851 * jax.random.uniform(splits[1], (2, NP, NA, NR), jnp.float32) ** levels(splits[1], (2, NP, NA, NR), ((0, 2), (1, 16)), -0.2, 0.2)), 0.05, 0.5)
    blade_counts = jax.random.randint(splits[2], (2,), 20, 80).astype(jnp.int32)
    mode_orders = set_ends(jax.random.randint(splits[3], (NMODE,), 1, NP // 2), jax.random.fold_in(splits[3], 1), 1, (NP // 2) - 1).astype(jnp.int32)
    return {"state": state, "viscosity": viscosity, "blade_counts": blade_counts, "mode_orders": mode_orders}


def spectral_matrix(count):
    idx = jnp.arange(count).astype(jnp.float32)
    diff = idx[:, None] - idx[None, :]
    safe = jnp.where(diff == 0.0, 1.0, diff)
    value = 0.5 * jnp.cos(math.pi * safe) * jnp.cos(math.pi * safe / count) / jnp.sin(math.pi * safe / count)
    return jnp.where(diff == 0.0, 0.0, value).astype(jnp.float32)

def shift_matrix(count, lag):
    idx = jnp.arange(count).astype(jnp.float32)
    delta = idx[:, None] - idx[None, :] - lag
    orders = jnp.arange(1, count // 2).astype(jnp.float32)
    total = 1.0 + 2.0 * lax.optimization_barrier(jnp.sum(jnp.cos(2.0 * math.pi * orders[None, None, :] * delta[:, :, None] / count), axis=2))
    total = total + jnp.cos(math.pi * delta)
    return (total / count).astype(jnp.float32)

def rotate(field, angle):
    cosine = jnp.cos(angle)
    sine = jnp.sin(angle)
    first = field[:, 2]
    second = field[:, 3]
    return jnp.concatenate([field[:, :2], (cosine * first - sine * second)[:, None], (sine * first + cosine * second)[:, None], field[:, 4:]], 1)

def bases(positions, orders, total):
    phase = 2.0 * math.pi * positions.astype(jnp.float32)[:, None] * orders.astype(jnp.float32)[None, :] / total
    ones = jnp.ones((positions.shape[0], 1), jnp.float32)
    synth = jnp.concatenate([ones, jnp.cos(phase), jnp.sin(phase)], 1)
    scale = jnp.concatenate([jnp.ones((1,), jnp.float32) / total, jnp.full((orders.shape[0] * 2,), 2.0 / total, jnp.float32)])
    return (synth * scale[None, :], synth)

def smooth(field):
    length = field.shape[-2]
    steps = jnp.arange(1, length + 1).astype(jnp.float32)
    basis = math.sqrt(2.0 / (length + 1)) * jnp.sin(math.pi * steps[:, None] * steps[None, :] / (length + 1))
    eigen = 2.0 - jnp.cos(math.pi * steps / (length + 1))
    inverse = jnp.dot(basis / eigen[None, :], basis.T, precision=lax.Precision.HIGHEST)
    return jnp.einsum('ab,ncpbr->ncpar', inverse, field, precision=lax.Precision.HIGHEST)

def stencil(padded, field, nu, source):
    lap = padded[:, :, 2:, 1:-1, 1:-1] + padded[:, :, :-2, 1:-1, 1:-1]
    lap = lap + padded[:, :, 1:-1, 2:, 1:-1] + padded[:, :, 1:-1, :-2, 1:-1]
    lap = lap + padded[:, :, 1:-1, 1:-1, 2:] + padded[:, :, 1:-1, 1:-1, :-2]
    lap = lap - 6.0 * field
    return nu * lap - 1.0 * (field - padded[:, :, 1:-1, :-2, 1:-1]) - 0.5 * (field - padded[:, :, :-2, 1:-1, 1:-1]) - source

def reference(state, viscosity, blade_counts, mode_orders):
    hi = lax.Precision.HIGHEST
    count = state.shape[1]
    total = state.shape[3]
    length = state.shape[4]
    spectral = spectral_matrix(count)
    analysis, synth = bases(jnp.arange(total), mode_orders, total)
    news = []
    residuals = []
    for which in range(2):
        other_row = 1 - which
        field = state[which]
        nu = viscosity[which][None, None]
        ratio = blade_counts[other_row].astype(jnp.float32) / blade_counts[which].astype(jnp.float32)
        angle = 2.0 * math.pi / blade_counts[which].astype(jnp.float32)
        low = rotate(jnp.einsum('nm,mcar->ncar', shift_matrix(count, ratio), field[:, :, total - 1], precision=hi), -angle)
        high = rotate(jnp.einsum('nm,mcar->ncar', shift_matrix(count, -ratio), field[:, :, 0], precision=hi), angle)
        padded = jnp.concatenate([low[:, :, None], field, high[:, :, None]], 2)
        plane = state[other_row][:, :, :, 0 if which == 0 else length - 1, :]
        coeffs = jnp.einsum('ncpr,pk->nckr', plane, analysis, precision=hi)
        ghost = jnp.einsum('nckr,pk->ncpr', coeffs, synth, precision=hi)
        ghost = jnp.pad(ghost, ((0, 0), (0, 0), (1, 1), (0, 0)))
        zeros = jnp.zeros_like(ghost)
        front = zeros if which == 0 else ghost
        back = ghost if which == 0 else zeros
        padded = jnp.concatenate([front[:, :, :, None], padded, back[:, :, :, None]], 3)
        padded = jnp.pad(padded, ((0, 0), (0, 0), (0, 0), (0, 0), (1, 1)))
        source = ratio * jnp.einsum('nm,mcpar->ncpar', spectral, field, precision=hi)
        res = stencil(padded, field, nu, source)
        residuals.append(res)
        news.append(field + 0.2 * smooth(res))
    return (jnp.stack(news), jnp.stack(residuals))
```

```python
import functools
import math

import numpy as np

import jax
import jax.numpy as jnp
from jax import lax
from jax.experimental import pallas as pl
from jax.experimental.pallas import tpu as pltpu
from jax.sharding import PartitionSpec as P

INST = 8
MODES = 24
LIMIT = 12 * 1024 * 1024
VMEM = pl.BlockSpec(memory_space=pltpu.VMEM)
SMEM = pl.BlockSpec(memory_space=pltpu.SMEM)
ANY = pl.BlockSpec(memory_space=pl.ANY)
HBM = pl.BlockSpec(memory_space=pltpu.HBM)
D1 = -0.5 / math.tan(math.pi / 8)
D2 = 0.5 / math.tan(math.pi / 4)
D3 = -0.5 / math.tan(3 * math.pi / 8)


def shaped(*dims):
    return jax.ShapeDtypeStruct(dims, jnp.float32)


def cost():
    return pl.CostEstimate(flops=1, bytes_accessed=1, transcendentals=0)


def inverse_parts(length):
    steps = np.arange(1, length + 1).astype(np.float64)
    basis = math.sqrt(2.0 / (length + 1)) * np.sin(
        math.pi * steps[:, None] * steps[None, :] / (length + 1)
    )
    eigen = 2.0 - np.cos(math.pi * steps / (length + 1))
    inverse = (0.2 * (basis / eigen[None, :]) @ basis.T).astype(np.float32)
    high = inverse.astype(jnp.bfloat16)
    low = (inverse - high.astype(np.float32)).astype(jnp.bfloat16)
    return np.concatenate([high, low, high], axis=1)


def split_bf16(x):
    high = x.astype(jnp.bfloat16)
    return high, (x - high.astype(jnp.float32)).astype(jnp.bfloat16)


def params():
    return pltpu.CompilerParams(vmem_limit_bytes=LIMIT)


def pack_kernel(planes, with_edges, field, *rest):
    sems = rest[-1]
    copies = []

    def copy(source, target):
        one = pltpu.make_async_copy(source, target, sems.at[len(copies)])
        one.start()
        copies.append(one)

    outs = rest[-6:-1] if with_edges else rest[-4:-1]
    for k, out in zip((1, 3, 2), outs):
        place = lax.rem(lax.axis_index("inst") + k, 4) * 16
        rows = pl.ds(pl.multiple_of(place, 16), 16)
        done = 0
        for start, size in planes:
            copy(field.at[:, start : start + size, rows, :], out.at[:, done : done + size])
            done += size
    if with_edges:
        copy(field.at[:, field.shape[1] - 1], outs[3])
        copy(field.at[:, 0], outs[4])
    for one in copies:
        one.wait()


def pack(field, planes, with_edges, after=()):
    blocks, _, rows, lanes = field.shape
    size = sum(size for _, size in planes)
    quarters = [shaped(blocks, size, rows // 4, lanes)] * 3
    edges = [shaped(blocks, rows, lanes)] * 2 if with_edges else []
    out_shape = tuple(quarters + edges)
    return pl.pallas_call(
        functools.partial(pack_kernel, planes, with_edges),
        out_shape=out_shape,
        in_specs=[HBM] + [VMEM] * len(after),
        out_specs=(VMEM,) * len(out_shape),
        scratch_shapes=[pltpu.SemaphoreType.DMA((8,))],
        compiler_params=params(),
        cost_estimate=cost(),
    )(pltpu.with_memory_space_constraint(field, pltpu.HBM), *after)


def turns(position, mode, orders, total):
    order = jnp.zeros(mode.shape, jnp.int32)
    count = orders.shape[0]
    for j in range(count):
        order = jnp.where((mode == 1 + j) | (mode == 1 + count + j), orders[j], order)
    phase = lax.rem(position * order, total).astype(jnp.float32) * (2.0 * math.pi / total)
    value = jnp.where(mode <= count, jnp.cos(phase), jnp.sin(phase))
    return jnp.where(mode <= 2 * count, value, 0.0)


def harmonics_kernel(total, where, orders, after, field, out):
    blocks, planes, _, lanes = field.shape
    mode = lax.broadcasted_iota(jnp.int32, (MODES, planes), 0)
    position = lax.broadcasted_iota(jnp.int32, (MODES, planes), 1) + where[0]
    basis = turns(position, mode, orders, total) * jnp.where(mode == 0, 1.0 / total, 2.0 / total)
    for b in range(blocks):
        edge = jnp.where(where[1] == 0, field[b, :, 7, :], field[b, :, 0, :])
        out[:, b * lanes : (b + 1) * lanes] = jnp.dot(
            basis, edge, precision=lax.Precision.HIGHEST, preferred_element_type=jnp.float32
        )


def read_all(refs, *at):
    own, up, down, far = refs
    return [r[(slot, *at)] for r in (own, up, far, down) for slot in range(2)]


def mix_kernel(scalars, plane, own_low, own_high, up, down, far, out):
    weight = [scalars[k] for k in range(INST)]
    cosine, sine = scalars[INST], scalars[INST + 1]
    at = plane[0]
    is_low = at == 0

    def mixed(var):
        own = [jnp.where(is_low, own_low[s, var, 0], own_high[s, var, 0]) for s in range(2)]
        u = own + [r[s, var, at] for r in (up, far, down) for s in range(2)]
        sums = []
        for a in range(INST):
            total = weight[a % INST] * u[0]
            for b in range(1, INST):
                total = total + weight[(a - b) % INST] * u[b]
            sums.append(total)
        return sums

    for var in (0, 1, 4, 5):
        for a, value in enumerate(mixed(var)):
            out[a, var] = value
    v, w = mixed(2), mixed(3)
    for a in range(INST):
        out[a, 2] = cosine * v[a] - sine * w[a]
        out[a, 3] = sine * v[a] + cosine * w[a]


def source_kernel(rims, scalars, *refs):
    outs, refs = refs[-4:], refs[:-4]
    if rims:
        ghost, nu = refs[-2:]
        refs = refs[:-2]
    up, down, far = refs[-3:]
    own = refs[:-3]
    ratio = scalars[0]
    c1, c2, c3 = (ratio * D1, ratio * D2, ratio * D3)
    out_own, out_up, out_down, out_far = outs
    order = (out_own, out_up, out_far, out_down)
    for var in range(up.shape[1]):
        for p in range(up.shape[2]):
            u = [own[p][s, var, 0] for s in range(2)]
            u += [r[s, var, p] for r in (up, far, down) for s in range(2)]
            near = [u[(n - 1) % INST] - u[(n + 1) % INST] for n in range(INST)]
            second = [c2 * (u[(n - 2) % INST] - u[(n + 2) % INST]) for n in range(4)]
            if rims:
                factor = (nu[0] + 0.5) * scalars[1] if p == 0 else nu[1] * scalars[2]
            for n in range(INST):
                s = c1 * near[n] - c3 * near[(n + 4) % INST]
                s = s + second[n] if n < 4 else s - second[n - 4]
                if rims:
                    s = s - factor * ghost[n, var]
                order[n // 2][n % 2, var, p] = s


def stencil_kernel(nu, low, high, field, out):
    blocks, planes, rows, lanes = field.shape
    lane = lax.broadcasted_iota(jnp.int32, (rows, lanes), 1)
    row = lax.broadcasted_iota(jnp.int32, (rows, lanes), 0)
    for b in range(blocks):
        for p in range(planes):
            u = field[b, p]
            before = low[b] if p == 0 else field[b, p - 1]
            after = high[b] if p == planes - 1 else field[b, p + 1]
            left = jnp.where(lane == 0, 0.0, pltpu.roll(u, 1, 1))
            right = jnp.where(lane == lanes - 1, 0.0, pltpu.roll(u, lanes - 1, 1))
            above = jnp.where(row == 0, 0.0, pltpu.roll(u, 1, 0))
            below = jnp.where(row == rows - 1, 0.0, pltpu.roll(u, rows - 1, 0))
            lap = (before + after) + (above + below) + (left + right) - 6.0 * u
            out[b, p] = nu[p] * lap - (u - above) - 0.5 * (u - before)


def edge_kernel(total, where, orders, coeffs, facing, out):
    planes, blocks, rows, lanes = out.shape
    mode = lax.broadcasted_iota(jnp.int32, (planes, MODES), 1)
    position = lax.broadcasted_iota(jnp.int32, (planes, MODES), 0) + where[0]
    ghost = jnp.dot(
        turns(position, mode, orders, total),
        coeffs[...],
        precision=lax.Precision.HIGHEST,
        preferred_element_type=jnp.float32,
    )
    hit = lax.broadcasted_iota(jnp.int32, (rows, lanes), 0) == (1 - where[1]) * (rows - 1)
    for b in range(blocks):
        value = facing[...] * ghost[:, b * lanes : (b + 1) * lanes]
        for p in range(planes):
            out[p, b] = jnp.where(hit, value[p : p + 1], 0.0)


def final_kernel(places, inverse, edge, field, pre, own, up, down, far, *rest):
    new, residual = rest[-2:]
    count, _, rows, lanes = field.shape
    tile = pl.ds(pl.multiple_of(places[4], 8), 8)
    for j in range(count):
        for k, piece in enumerate((own, up, down, far)):
            at = pl.ds(pl.multiple_of(places[k], 16), 16)
            residual[j, 0, at] = pre[j, 0, at] - piece[j, 0]
        residual[j, 0, tile] = residual[j, 0, tile] + edge[0, j]
    for j in range(0, count, 2):
        high, low = split_bf16(jnp.concatenate([residual[j, 0], residual[j + 1, 0]], 1))
        change = jnp.dot(
            inverse[...],
            jnp.concatenate([high, high, low], 0),
            preferred_element_type=jnp.float32,
        )
        new[j, 0] = field[j, 0] + change[:, :lanes]
        new[j + 1, 0] = field[j + 1, 0] + change[:, lanes:]


def lag_weights(lag):
    delta = jnp.arange(INST).astype(jnp.float32) - lag
    total = 1.0 + jnp.cos(math.pi * delta)
    for k in range(1, INST // 2):
        total = total + 2.0 * jnp.cos(2.0 * math.pi * k / INST * delta)
    return total / INST


def local(state, viscosity, blade_counts, mode_orders):
    _, local_inst, variables, planes, rows, lanes = state.shape
    quarter = rows // 4
    blocks = local_inst * variables
    mesh_count = lax.axis_size("mesh")
    total = planes * mesh_count
    which = lax.axis_index("row")
    inst = lax.axis_index("inst")
    mesh_idx = lax.axis_index("mesh")
    counts = blade_counts.astype(jnp.float32)
    ratio = counts[1 - which] / counts[which]
    angle = 2.0 * math.pi / counts[which]
    field = state.reshape(blocks, planes, rows, lanes)
    nu = viscosity[0]
    first = mesh_idx == 0
    last = mesh_idx == mesh_count - 1
    places = (quarter * ((inst + jnp.array([0, 1, 3, 2])) % 4)).astype(jnp.int32)
    where = jnp.stack([mesh_idx * planes, which]).astype(jnp.int32)

    def along(x, step):
        return lax.ppermute(x, "inst", [(j, (j + step) % 4) for j in range(4)])

    def in_hbm(*arrays):
        return [pltpu.with_memory_space_constraint(x, pltpu.HBM) for x in arrays]

    def exchange(up, down, far):
        from_down, from_up, from_far = along(up, 1), along(down, 3), along(far, 2)
        return from_up, from_down, from_far

    mid_out = pack(field, ((1, planes - 2),), False)
    mid_in = exchange(*mid_out)
    *rim_out, top, bottom = pack(field, ((0, 1), (planes - 1, 1)), True, after=mid_out[:1])
    rim_in = exchange(*rim_out)

    low = lax.ppermute(top, "mesh", [(j, j + 1) for j in range(mesh_count - 1)])
    high = lax.ppermute(bottom, "mesh", [(j + 1, j) for j in range(mesh_count - 1)])

    def own_spec(plane, vars_at_once):
        return pl.BlockSpec(
            (2, vars_at_once, 1, quarter, lanes),
            lambda b, places: (0, b, plane, places[0] // quarter, 0),
        )

    split = (local_inst, variables)
    parted = field.reshape(*split, planes, rows, lanes)

    whole = shaped(*field.shape)
    at_once = 2
    slab = pl.BlockSpec((at_once, planes, rows, lanes), lambda b: (b, 0, 0, 0))
    plane = pl.BlockSpec((at_once, rows, lanes), lambda b: (b, 0, 0))
    pre = pl.pallas_call(
        stencil_kernel,
        grid=(blocks // at_once,),
        out_shape=pltpu.HBM(field.shape, jnp.float32),
        in_specs=[pl.BlockSpec((planes, rows, lanes), lambda b: (0, 0, 0)), plane, plane, slab],
        out_specs=slab,
        compiler_params=params(),
        cost_estimate=cost(),
    )(nu, *in_hbm(low, high), field)

    weights = lag_weights(jnp.where(first, -ratio, ratio))
    turn = jnp.where(first, angle, -angle)
    ghost_shape = shaped(INST, variables, quarter, lanes)

    def mixer(places, *refs):
        mix_kernel(*refs[:-2], refs[-1])

    ghost_out = pl.pallas_call(
        mixer,
        out_shape=ghost_shape,
        grid_spec=pltpu.PrefetchScalarGridSpec(
            num_scalar_prefetch=1,
            grid=(1,),
            in_specs=[SMEM, SMEM, own_spec(0, variables), own_spec(planes - 1, variables)]
            + [pl.BlockSpec((2, variables, 2, quarter, lanes), lambda b, places: (0, 0, 0, 0, 0))] * 3
            + [VMEM],
            out_specs=pl.BlockSpec(ghost_shape.shape, lambda b, places: (0, 0, 0, 0)),
        ),
        compiler_params=params(),
        cost_estimate=cost(),
    )(
        places,
        jnp.concatenate([weights, jnp.stack([jnp.cos(turn), jnp.sin(turn)])]),
        jnp.where(first, 0, 1).astype(jnp.int32)[None],
        parted,
        parted,
        *in_hbm(*(x.reshape(*split, 2, quarter, lanes) for x in rim_in)),
        mid_out[0],
    )
    ghost = lax.ppermute(ghost_out, "mesh", [(mesh_count - 1, 0), (0, mesh_count - 1)])

    edge_rows = pl.BlockSpec(
        (blocks, planes, 8, lanes),
        lambda b, where, orders: (0, 0, (1 - where[1]) * (rows // 8 - 1), 0),
    )
    harmonics = pl.pallas_call(
        functools.partial(harmonics_kernel, total),
        out_shape=shaped(MODES, blocks * lanes),
        grid_spec=pltpu.PrefetchScalarGridSpec(
            num_scalar_prefetch=2,
            grid=(1,),
            in_specs=[VMEM, edge_rows],
            out_specs=pl.BlockSpec((MODES, blocks * lanes), lambda b, where, orders: (0, 0)),
        ),
        compiler_params=params(),
        cost_estimate=cost(),
    )(where, mode_orders, low, field)
    def crossing(flip):
        return [
            (r * mesh_count + m, (1 - r) * mesh_count + (m ^ flip))
            for r in range(2)
            for m in range(mesh_count)
        ]

    def doubled(x, flip):
        return x + lax.ppermute(x, "mesh", [(m, m ^ flip) for m in range(mesh_count)])

    two_ways = [lax.ppermute(harmonics, ("row", "mesh"), crossing(flip)) for flip in (0, 1)]
    harmonics = doubled(two_ways[0] + two_ways[1], 2)
    early = harmonics
    harmonics = doubled(doubled(harmonics, 4), 8)

    scalars = jnp.stack([ratio, first.astype(jnp.float32), last.astype(jnp.float32)])

    def sources(own_planes, part, gathered, rims, after=()):
        at_once, size = 3, len(own_planes)
        piece_in = pl.BlockSpec(
            (2, at_once, size, quarter, lanes), lambda b, places: (0, b, part, 0, 0)
        )
        piece = pl.BlockSpec((2, at_once, size, quarter, lanes), lambda b, places: (0, b, 0, 0, 0))
        rim_specs = [
            pl.BlockSpec((INST, at_once, quarter, lanes), lambda b, places: (0, b, 0, 0)),
            pl.BlockSpec((2, quarter, lanes), lambda b, places: (0, 0, 0)),
        ]

        def kernel(places, *refs):
            inputs, outputs = refs[: -4 - len(after)], refs[-4:]
            source_kernel(bool(rims), *inputs, *outputs)

        outs = pl.pallas_call(
            kernel,
            out_shape=(pltpu.HBM((*split, size, quarter, lanes), jnp.float32),) * 4,
            grid_spec=pltpu.PrefetchScalarGridSpec(
                num_scalar_prefetch=1,
                grid=(variables // at_once,),
                in_specs=[SMEM]
                + [own_spec(plane, at_once) for plane in own_planes]
                + [piece_in] * 3
                + rim_specs[: len(rims)]
                + [ANY] * len(after),
                out_specs=(piece,) * 4,
            ),
            compiler_params=params(),
            cost_estimate=cost(),
        )(
            places,
            scalars,
            *([parted] * size),
            *in_hbm(*(x.reshape(*split, -1, quarter, lanes) for x in gathered)),
            *in_hbm(*rims[:1]),
            *rims[1:],
            *after,
        )
        own, up, down, far = (x.reshape(blocks, size, quarter, lanes) for x in outs)
        return (own, *exchange(up, down, far))

    one_source = sources((1, 2, 3, 4), 0, mid_in, (), after=in_hbm(pre))
    two_source = sources((5, 6), 2, mid_in, ())

    rim_nu = lax.dynamic_slice(nu[:: planes - 1], (0, places[0], 0), (2, quarter, lanes))
    rim_source = sources((0, planes - 1), 0, rim_in, (ghost, rim_nu), after=in_hbm(*one_source[1:]))

    facing = jnp.where(which == 0, nu[:, rows - 1], nu[:, 0] + 1.0)
    edge = pl.pallas_call(
        functools.partial(edge_kernel, total),
        out_shape=shaped(planes, blocks, 8, lanes),
        in_specs=[SMEM, SMEM, VMEM, VMEM],
        out_specs=VMEM,
        compiler_params=params(),
        cost_estimate=cost(),
    )(where, mode_orders, harmonics, facing)

    inverse = jnp.asarray(inverse_parts(rows))
    with_facing = jnp.concatenate([places, jnp.where(which == 0, rows - 8, 0).astype(jnp.int32)[None]])
    new, residual = None, pre
    for base, stride, size, group in (
        (1, 1, 4, one_source),
        (5, 1, 2, two_source),
        (0, planes - 1, 2, rim_source),
    ):
        slab = pl.BlockSpec(
            (blocks, 1, rows, lanes),
            functools.partial(lambda base, stride, g: (0, base + stride * g, 0, 0), base, stride),
        )
        tiles = pl.BlockSpec(
            (1, blocks, 8, lanes),
            functools.partial(lambda base, stride, g: (base + stride * g, 0, 0, 0), base, stride),
        )
        part = pl.BlockSpec((blocks, 1, quarter, lanes), lambda g: (0, g, 0, 0))
        kept = [] if new is None else [new]
        new, residual = pl.pallas_call(
            final_kernel,
            grid=(size,),
            out_shape=(whole, whole),
            in_specs=[SMEM, pl.BlockSpec(inverse.shape, lambda g: (0, 0)), tiles, slab, slab]
            + [part] * 4
            + [ANY] * len(kept),
            out_specs=(slab, slab),
            input_output_aliases={4: 1, **({9: 0} if kept else {})},
            compiler_params=params(),
            cost_estimate=cost(),
        )(with_facing, inverse, edge, field, residual, *in_hbm(*group), *kept)
    return (new.reshape(state.shape), residual.reshape(state.shape))


def solution(mesh):
    spread = P("row", "inst", None, "mesh", None, None)
    return jax.shard_map(
        local,
        mesh=mesh,
        in_specs=(spread, P("row", "mesh", None, None), P(), P()),
        out_specs=(spread, spread),
        check_vma=False,
    )
```

```python
import functools
import math

import numpy as np

import jax
import jax.numpy as jnp
from jax import lax
from jax.experimental import pallas as pl
from jax.experimental.pallas import tpu as pltpu
from jax.sharding import PartitionSpec as P

INST = 8
MODES = 24
LIMIT = 10 * 1024 * 1024
VMEM = pl.BlockSpec(memory_space=pltpu.VMEM)
SMEM = pl.BlockSpec(memory_space=pltpu.SMEM)
ANY = pl.BlockSpec(memory_space=pl.ANY)
HBM = pl.BlockSpec(memory_space=pltpu.HBM)
D1 = -0.5 / math.tan(math.pi / 8)
D2 = 0.5 / math.tan(math.pi / 4)
D3 = -0.5 / math.tan(3 * math.pi / 8)


def shaped(*dims):
    return jax.ShapeDtypeStruct(dims, jnp.float32)


def cost():
    return pl.CostEstimate(flops=1, bytes_accessed=1, transcendentals=0)


def inverse_parts(length):
    steps = np.arange(1, length + 1).astype(np.float64)
    basis = math.sqrt(2.0 / (length + 1)) * np.sin(
        math.pi * steps[:, None] * steps[None, :] / (length + 1)
    )
    eigen = 2.0 - np.cos(math.pi * steps / (length + 1))
    inverse = (0.2 * (basis / eigen[None, :]) @ basis.T).astype(np.float32)
    high = inverse.astype(jnp.bfloat16)
    low = (inverse - high.astype(np.float32)).astype(jnp.bfloat16)
    return np.concatenate([high, low, high], axis=1)


def split_bf16(x):
    high = x.astype(jnp.bfloat16)
    return high, (x - high.astype(jnp.float32)).astype(jnp.bfloat16)


def params():
    return pltpu.CompilerParams(vmem_limit_bytes=LIMIT)


def pack_kernel(planes, field, *rest):
    sems = rest[-1]
    copies = []

    def copy(source, target):
        one = pltpu.make_async_copy(source, target, sems.at[len(copies)])
        one.start()
        copies.append(one)

    outs = rest[:3]
    for k, out in zip((1, 3, 2), outs):
        place = lax.rem(lax.axis_index("inst") + k, 4) * 16
        rows = pl.ds(pl.multiple_of(place, 16), 16)
        done = 0
        for start, size in planes:
            for b in range(0, field.shape[0], 4):
                copy(
                    field.at[b : b + 4, start : start + size, rows, :],
                    out.at[b : b + 4, done : done + size],
                )
            done += size
    for one in copies:
        one.wait()


def edges_kernel(field, after, top, bottom, sems):
    copies = [
        pltpu.make_async_copy(field.at[b, plane], out.at[b], sems.at[k, b])
        for k, (plane, out) in enumerate(((field.shape[1] - 1, top), (0, bottom)))
        for b in range(field.shape[0])
    ]
    for one in copies:
        one.start()
    for one in copies:
        one.wait()


def pack(field, planes):
    blocks, _, rows, lanes = field.shape
    size = sum(size for _, size in planes)
    return pl.pallas_call(
        functools.partial(pack_kernel, planes),
        out_shape=(shaped(blocks, size, rows // 4, lanes),) * 3,
        in_specs=[HBM],
        out_specs=(VMEM,) * 3,
        scratch_shapes=[pltpu.SemaphoreType.DMA((32,))],
        compiler_params=params(),
        cost_estimate=cost(),
    )(pltpu.with_memory_space_constraint(field, pltpu.HBM))


def turns(position, mode, orders, total):
    order = jnp.zeros(mode.shape, jnp.int32)
    count = orders.shape[0]
    for j in range(count):
        order = jnp.where((mode == 1 + j) | (mode == 1 + count + j), orders[j], order)
    phase = lax.rem(position * order, total).astype(jnp.float32) * (2.0 * math.pi / total)
    value = jnp.where(mode <= count, jnp.cos(phase), jnp.sin(phase))
    return jnp.where(mode <= 2 * count, value, 0.0)


def harmonics_kernel(total, where, orders, after, field, out):
    blocks, planes, _, lanes = field.shape
    mode = lax.broadcasted_iota(jnp.int32, (MODES, planes), 0)
    position = lax.broadcasted_iota(jnp.int32, (MODES, planes), 1) + where[0]
    basis = turns(position, mode, orders, total) * jnp.where(mode == 0, 1.0 / total, 2.0 / total)
    for b in range(blocks):
        edge = jnp.where(where[1] == 0, field[b, :, 7, :], field[b, :, 0, :])
        out[:, b * lanes : (b + 1) * lanes] = jnp.dot(
            basis, edge, precision=lax.Precision.HIGHEST, preferred_element_type=jnp.float32
        )


def read_all(refs, *at):
    own, up, down, far = refs
    return [r[(slot, *at)] for r in (own, up, far, down) for slot in range(2)]


def mix_kernel(scalars, plane, own_low, own_high, up, down, far, out):
    weight = [scalars[k] for k in range(INST)]
    cosine, sine = scalars[INST], scalars[INST + 1]
    at = plane[0]
    is_low = at == 1

    def mixed(var):
        own = [jnp.where(is_low, own_low[s, var, 0], own_high[s, var, 0]) for s in range(2)]
        u = own + [r[s, var, at] for r in (up, far, down) for s in range(2)]
        sums = []
        for a in range(INST):
            total = weight[a % INST] * u[0]
            for b in range(1, INST):
                total = total + weight[(a - b) % INST] * u[b]
            sums.append(total)
        return sums

    for var in (0, 1, 4, 5):
        for a, value in enumerate(mixed(var)):
            out[a, var] = value
    v, w = mixed(2), mixed(3)
    for a in range(INST):
        out[a, 2] = cosine * v[a] - sine * w[a]
        out[a, 3] = sine * v[a] + cosine * w[a]


def source_kernel(rims, scalars, *refs):
    if rims:
        outs, refs = refs[-4:], refs[:-4]
    else:
        outs, refs = refs[-1:], refs[:-1]
    if rims:
        ghost, nu = refs[-2:]
        refs = refs[:-2]
    up, down, far = refs[-3:]
    own = refs[:-3]
    ratio = scalars[0]
    c1, c2, c3 = (ratio * D1, ratio * D2, ratio * D3)
    if rims:
        out_own, out_up, out_down, out_far = outs
        order = (out_own, out_up, out_far, out_down)
    else:
        inst = lax.axis_index("inst")
        order = [outs[0].at[lax.rem(inst + k, 4)] for k in range(4)]
    for var in range(up.shape[1]):
        for p in range(up.shape[2]):
            u = [own[p][s, var, 0] for s in range(2)]
            u += [r[s, var, p] for r in (up, far, down) for s in range(2)]
            near = [u[(n - 1) % INST] - u[(n + 1) % INST] for n in range(INST)]
            second = [c2 * (u[(n - 2) % INST] - u[(n + 2) % INST]) for n in range(4)]
            for n in range(INST):
                s = c1 * near[n] - c3 * near[(n + 4) % INST]
                s = s + second[n] if n < 4 else s - second[n - 4]
                order[n // 2][n % 2, var, p] = s
    if not rims:
        return

    def add_ghost(p, factor):
        for var in range(up.shape[1]):
            for n in range(INST):
                at = (n % 2, var, p)
                order[n // 2][at] = order[n // 2][at] - factor * ghost[n, var]

    @pl.when(scalars[1] > 0.5)
    def _():
        add_ghost(3, nu[0] + 0.5)

    @pl.when(scalars[2] > 0.5)
    def _():
        add_ghost(2, nu[1])


def stencil_kernel(nu, low, high, field, out):
    blocks, planes, rows, lanes = field.shape
    lane = lax.broadcasted_iota(jnp.int32, (rows, lanes), 1)
    row = lax.broadcasted_iota(jnp.int32, (rows, lanes), 0)
    for b in range(blocks):
        for p in range(planes):
            u = field[b, p]
            before = low[b] if p == 0 else field[b, p - 1]
            after = high[b] if p == planes - 1 else field[b, p + 1]
            left = jnp.where(lane == 0, 0.0, pltpu.roll(u, 1, 1))
            right = jnp.where(lane == lanes - 1, 0.0, pltpu.roll(u, lanes - 1, 1))
            above = jnp.where(row == 0, 0.0, pltpu.roll(u, 1, 0))
            below = jnp.where(row == rows - 1, 0.0, pltpu.roll(u, rows - 1, 0))
            lap = (before + after) + (above + below) + (left + right) - 6.0 * u
            out[b, p] = nu[p] * lap - (u - above) - 0.5 * (u - before)


def edge_kernel(total, where, orders, coeffs, facing, out):
    planes, blocks, rows, lanes = out.shape
    mode = lax.broadcasted_iota(jnp.int32, (planes, MODES), 1)
    position = lax.broadcasted_iota(jnp.int32, (planes, MODES), 0) + where[0]
    ghost = jnp.dot(
        turns(position, mode, orders, total),
        coeffs[...],
        precision=lax.Precision.HIGHEST,
        preferred_element_type=jnp.float32,
    )
    hit = lax.broadcasted_iota(jnp.int32, (rows, lanes), 0) == (1 - where[1]) * (rows - 1)
    for b in range(blocks):
        value = facing[...] * ghost[:, b * lanes : (b + 1) * lanes]
        for p in range(planes):
            out[p, b] = jnp.where(hit, value[p : p + 1], 0.0)


def final_kernel(base, planes, places, inverse, edge, field, pre, *rest):
    new, residual = rest[-2:]
    count, _, rows, lanes = new.shape
    pieces = rest[:4] if rest[0].shape[0] == count else [rest[0].at[j] for j in range(4)]
    plane = lax.rem(base + pl.program_id(0), planes)
    tile = pl.ds(pl.multiple_of(places[4], 8), 8)
    for j in range(count):
        for k, piece in enumerate(pieces):
            if rest[0].shape[0] == count:
                at = pl.ds(pl.multiple_of(places[k], 16), 16)
            else:
                at = pl.ds(16 * k, 16)
            residual[j, 0, at] = pre[j, plane, at] - piece[j, 0]
        residual[j, 0, tile] = residual[j, 0, tile] + edge[0, j]
    for j in range(0, count, 2):
        high, low = split_bf16(jnp.concatenate([residual[j, 0], residual[j + 1, 0]], 1))
        change = jnp.dot(
            inverse[...],
            jnp.concatenate([high, high, low], 0),
            preferred_element_type=jnp.float32,
        )
        new[j, 0] = field[j, plane] + change[:, :lanes]
        new[j + 1, 0] = field[j + 1, plane] + change[:, lanes:]


def lag_weights(lag):
    delta = jnp.arange(INST).astype(jnp.float32) - lag
    total = 1.0 + jnp.cos(math.pi * delta)
    for k in range(1, INST // 2):
        total = total + 2.0 * jnp.cos(2.0 * math.pi * k / INST * delta)
    return total / INST


def local(state, viscosity, blade_counts, mode_orders):
    _, local_inst, variables, planes, rows, lanes = state.shape
    quarter = rows // 4
    blocks = local_inst * variables
    mesh_count = lax.axis_size("mesh")
    total = planes * mesh_count
    which = lax.axis_index("row")
    inst = lax.axis_index("inst")
    mesh_idx = lax.axis_index("mesh")
    counts = blade_counts.astype(jnp.float32)
    ratio = counts[1 - which] / counts[which]
    angle = 2.0 * math.pi / counts[which]
    field = state.reshape(blocks, planes, rows, lanes)
    nu = viscosity[0]
    first = mesh_idx == 0
    last = mesh_idx == mesh_count - 1
    places = (quarter * ((inst + jnp.array([0, 1, 3, 2])) % 4)).astype(jnp.int32)
    where = jnp.stack([mesh_idx * planes, which, last]).astype(jnp.int32)

    def along(x, step):
        return lax.ppermute(x, "inst", [(j, (j + step) % 4) for j in range(4)])

    def in_hbm(*arrays):
        return [pltpu.with_memory_space_constraint(x, pltpu.HBM) for x in arrays]

    def exchange(up, down, far):
        from_down, from_up, from_far = along(up, 1), along(down, 3), along(far, 2)
        return from_up, from_down, from_far

    packed = pack(field, ((1, planes - 1), (0, 1)))
    gathered = exchange(*packed)

    top, bottom = pl.pallas_call(
        edges_kernel,
        out_shape=(shaped(blocks, rows, lanes),) * 2,
        in_specs=[HBM, VMEM],
        out_specs=(VMEM,) * 2,
        scratch_shapes=[pltpu.SemaphoreType.DMA((2, blocks))],
        compiler_params=params(),
        cost_estimate=cost(),
    )(pltpu.with_memory_space_constraint(field, pltpu.HBM), packed[0])
    low = lax.ppermute(top, "mesh", [(j, j + 1) for j in range(mesh_count - 1)])
    high = lax.ppermute(bottom, "mesh", [(j + 1, j) for j in range(mesh_count - 1)])

    def own_spec(plane, vars_at_once):
        return pl.BlockSpec(
            (2, vars_at_once, 1, quarter, lanes),
            lambda b, places: (0, b, plane, places[0] // quarter, 0),
        )

    split = (local_inst, variables)
    parted = field.reshape(*split, planes, rows, lanes)

    whole = shaped(*field.shape)
    at_once = 2
    slab = pl.BlockSpec((at_once, planes, rows, lanes), lambda b: (b, 0, 0, 0))
    plane = pl.BlockSpec((at_once, rows, lanes), lambda b: (b, 0, 0))
    pre = pl.pallas_call(
        stencil_kernel,
        grid=(blocks // at_once,),
        out_shape=pltpu.HBM(field.shape, jnp.float32),
        in_specs=[pl.BlockSpec((planes, rows, lanes), lambda b: (0, 0, 0)), plane, plane, slab],
        out_specs=slab,
        compiler_params=params(),
        cost_estimate=cost(),
    )(nu, *in_hbm(low, high), field)

    edge_rows = pl.BlockSpec(
        (blocks, planes, 8, lanes),
        lambda b, where, orders: (0, 0, (1 - where[1]) * (rows // 8 - 1), 0),
    )
    harmonics = pl.pallas_call(
        functools.partial(harmonics_kernel, total),
        out_shape=shaped(MODES, blocks * lanes),
        grid_spec=pltpu.PrefetchScalarGridSpec(
            num_scalar_prefetch=2,
            grid=(1,),
            in_specs=[ANY, edge_rows],
            out_specs=pl.BlockSpec((MODES, blocks * lanes), lambda b, where, orders: (0, 0)),
        ),
        compiler_params=params(),
        cost_estimate=cost(),
    )(where, mode_orders, *in_hbm(low), field)
    def crossing(flip):
        return [
            (r * mesh_count + m, (1 - r) * mesh_count + (m ^ flip))
            for r in range(2)
            for m in range(mesh_count)
        ]

    def doubled(x, flip):
        return x + lax.ppermute(x, "mesh", [(m, m ^ flip) for m in range(mesh_count)])

    two_ways = [lax.ppermute(harmonics, ("row", "mesh"), crossing(flip)) for flip in (0, 1)]
    harmonics = doubled(two_ways[0] + two_ways[1], 2)
    early = harmonics
    harmonics = doubled(doubled(harmonics, 4), 8)

    scalars = jnp.stack([ratio, first.astype(jnp.float32), last.astype(jnp.float32)])

    def sources(own_planes, part, gathered, rims, after=()):
        at_once, size = 3, len(own_planes)
        piece_in = pl.BlockSpec(
            (2, at_once, size, quarter, lanes), lambda b, places: (0, b, part // size, 0, 0)
        )
        piece = pl.BlockSpec((2, at_once, size, quarter, lanes), lambda b, places: (0, b, 0, 0, 0))
        rim_specs = [
            pl.BlockSpec((INST, at_once, quarter, lanes), lambda b, places: (0, b, 0, 0)),
            pl.BlockSpec((2, quarter, lanes), lambda b, places: (0, 0, 0)),
        ]

        count = 4 if rims else 1

        def kernel(places, *refs):
            inputs, outputs = refs[: -count - len(after)], refs[-count:]
            source_kernel(bool(rims), *inputs, *outputs)

        if not rims:
            out_shape = (pltpu.HBM((4, *split, size, quarter, lanes), jnp.float32),)
            out_specs = (
                pl.BlockSpec(
                    (4, 2, at_once, size, quarter, lanes), lambda b, places: (0, 0, b, 0, 0, 0)
                ),
            )
        else:
            out_shape = (pltpu.HBM((*split, size, quarter, lanes), jnp.float32),) * 4
            out_specs = (piece,) * 4
        outs = pl.pallas_call(
            kernel,
            out_shape=out_shape,
            grid_spec=pltpu.PrefetchScalarGridSpec(
                num_scalar_prefetch=1,
                grid=(variables // at_once,),
                in_specs=[SMEM]
                + [own_spec(plane, at_once) for plane in own_planes]
                + [piece_in] * 3
                + rim_specs[: len(rims)]
                + [ANY] * len(after),
                out_specs=out_specs,
            ),
            compiler_params=params(),
            cost_estimate=cost(),
        )(
            places,
            scalars,
            *([parted] * size),
            *in_hbm(*(x.reshape(*split, -1, quarter, lanes) for x in gathered)),
            *rims,
            *after,
        )
        if not rims:
            out = outs[0].reshape(4, blocks, size, quarter, lanes)
            return (lax.all_to_all(out, "inst", split_axis=0, concat_axis=0, tiled=True), out)
        own, up, down, far = (x.reshape(blocks, size, quarter, lanes) for x in outs)
        return (own, *exchange(up, down, far))

    one_source = sources(tuple(range(1, 5)), 0, gathered, (), after=(*in_hbm(pre), *two_ways,))

    weights = lag_weights(jnp.where(first, -ratio, ratio))
    turn = jnp.where(first, angle, -angle)
    ghost_shape = shaped(INST, variables, quarter, lanes)

    def mixer(places, *refs):
        mix_kernel(*refs[:-2], refs[-1])

    ghost_out = pl.pallas_call(
        mixer,
        out_shape=ghost_shape,
        grid_spec=pltpu.PrefetchScalarGridSpec(
            num_scalar_prefetch=1,
            grid=(1,),
            in_specs=[SMEM, SMEM, own_spec(0, variables), own_spec(planes - 1, variables)]
            + [pl.BlockSpec((2, variables, 2, quarter, lanes), lambda b, places: (0, 0, 3, 0, 0))] * 3
            + [ANY],
            out_specs=pl.BlockSpec(ghost_shape.shape, lambda b, places: (0, 0, 0, 0)),
        ),
        compiler_params=params(),
        cost_estimate=cost(),
    )(
        places,
        jnp.concatenate([weights, jnp.stack([jnp.cos(turn), jnp.sin(turn)])]),
        jnp.where(first, 1, 0).astype(jnp.int32)[None],
        parted,
        parted,
        *in_hbm(*(x.reshape(*split, planes, quarter, lanes) for x in gathered)),
        *in_hbm(one_source[1]),
    )
    ghost = lax.ppermute(ghost_out, "mesh", [(mesh_count - 1, 0), (0, mesh_count - 1)])

    rim_nu = lax.dynamic_slice(nu[:: planes - 1], (0, places[0], 0), (2, quarter, lanes))
    two_source = sources(
        (5, 6, 7, 0), 4, gathered, (*in_hbm(ghost), rim_nu)
    )

    facing = jnp.where(which == 0, nu[:, rows - 1], nu[:, 0] + 1.0)
    edge = pl.pallas_call(
        functools.partial(edge_kernel, total),
        out_shape=shaped(planes, blocks, 8, lanes),
        in_specs=[SMEM, SMEM, VMEM, VMEM],
        out_specs=VMEM,
        compiler_params=params(),
        cost_estimate=cost(),
    )(where, mode_orders, harmonics, facing)

    inverse = jnp.asarray(inverse_parts(rows))
    with_facing = jnp.concatenate([places, jnp.where(which == 0, rows - 8, 0).astype(jnp.int32)[None]])
    kept = ()
    for base, size, group in ((1, 4, one_source[:1]), (1 + 4, planes - 4, two_source)):
        slab = pl.BlockSpec(
            (blocks, 1, rows, lanes),
            functools.partial(lambda base, g: (0, (base + g) % planes, 0, 0), base),
        )
        tiles = pl.BlockSpec(
            (1, blocks, 8, lanes),
            functools.partial(lambda base, g: ((base + g) % planes, 0, 0, 0), base),
        )
        if len(group) == 4:
            part = pl.BlockSpec((blocks, 1, quarter, lanes), lambda g: (0, g, 0, 0))
        else:
            part = pl.BlockSpec((4, blocks, 1, quarter, lanes), lambda g: (0, 0, g, 0, 0))
        given = 5 + len(group)
        kept = pl.pallas_call(
            functools.partial(final_kernel, base, planes),
            grid=(size,),
            out_shape=(whole, whole),
            in_specs=[SMEM, pl.BlockSpec(inverse.shape, lambda g: (0, 0)), tiles, VMEM, VMEM]
            + [part] * len(group)
            + [ANY] * len(kept),
            out_specs=(slab, slab),
            input_output_aliases={given: 0, given + 1: 1} if kept else {},
            compiler_params=params(),
            cost_estimate=cost(),
        )(with_facing, inverse, edge, field, pre, *in_hbm(*group), *kept)
    new, residual = kept
    return (new.reshape(state.shape), residual.reshape(state.shape))


def solution(mesh):
    spread = P("row", "inst", None, "mesh", None, None)
    return jax.shard_map(
        local,
        mesh=mesh,
        in_specs=(spread, P("row", "mesh", None, None), P(), P()),
        out_specs=(spread, spread),
        check_vma=False,
    )
```

```python
import functools
import math

import numpy as np

import jax
import jax.numpy as jnp
from jax import lax
from jax.experimental import pallas as pl
from jax.experimental.pallas import tpu as pltpu
from jax.sharding import PartitionSpec as P

INST = 8
MODES = 24
LIMIT = 10 * 1024 * 1024
VMEM = pl.BlockSpec(memory_space=pltpu.VMEM)
SMEM = pl.BlockSpec(memory_space=pltpu.SMEM)
ANY = pl.BlockSpec(memory_space=pl.ANY)
HBM = pl.BlockSpec(memory_space=pltpu.HBM)
D1 = -0.5 / math.tan(math.pi / 8)
D2 = 0.5 / math.tan(math.pi / 4)
D3 = -0.5 / math.tan(3 * math.pi / 8)


def shaped(*dims):
    return jax.ShapeDtypeStruct(dims, jnp.float32)


def cost():
    return pl.CostEstimate(flops=1, bytes_accessed=1, transcendentals=0)


def inverse_parts(length):
    steps = np.arange(1, length + 1).astype(np.float64)
    basis = math.sqrt(2.0 / (length + 1)) * np.sin(
        math.pi * steps[:, None] * steps[None, :] / (length + 1)
    )
    eigen = 2.0 - np.cos(math.pi * steps / (length + 1))
    inverse = (0.2 * (basis / eigen[None, :]) @ basis.T).astype(np.float32)
    high = inverse.astype(jnp.bfloat16)
    low = (inverse - high.astype(np.float32)).astype(jnp.bfloat16)
    return np.concatenate([high, low, high], axis=1)


def split_bf16(x):
    high = x.astype(jnp.bfloat16)
    return high, (x - high.astype(jnp.float32)).astype(jnp.bfloat16)


def params():
    return pltpu.CompilerParams(vmem_limit_bytes=LIMIT)


def pack_kernel(planes, field, *rest):
    sems = rest[-1]
    copies = []

    def copy(source, target):
        one = pltpu.make_async_copy(source, target, sems.at[len(copies)])
        one.start()
        copies.append(one)

    outs = rest[:3]
    for k, out in zip((1, 3, 2), outs):
        place = lax.rem(lax.axis_index("inst") + k, 4) * 16
        rows = pl.ds(pl.multiple_of(place, 16), 16)
        done = 0
        for start, size in planes:
            for b in range(0, field.shape[0], 4):
                copy(
                    field.at[b : b + 4, start : start + size, rows, :],
                    out.at[b : b + 4, done : done + size],
                )
            done += size
    for one in copies:
        one.wait()


def edges_kernel(field, after, top, bottom, sems):
    copies = [
        pltpu.make_async_copy(field.at[b, plane], out.at[b], sems.at[k, b])
        for k, (plane, out) in enumerate(((field.shape[1] - 1, top), (0, bottom)))
        for b in range(field.shape[0])
    ]
    for one in copies:
        one.start()
    for one in copies:
        one.wait()


def pack(field, planes):
    blocks, _, rows, lanes = field.shape
    size = sum(size for _, size in planes)
    return pl.pallas_call(
        functools.partial(pack_kernel, planes),
        out_shape=(shaped(blocks, size, rows // 4, lanes),) * 3,
        in_specs=[HBM],
        out_specs=(VMEM,) * 3,
        scratch_shapes=[pltpu.SemaphoreType.DMA((32,))],
        compiler_params=params(),
        cost_estimate=cost(),
    )(pltpu.with_memory_space_constraint(field, pltpu.HBM))


def turns(position, mode, orders, total):
    order = jnp.zeros(mode.shape, jnp.int32)
    count = orders.shape[0]
    for j in range(count):
        order = jnp.where((mode == 1 + j) | (mode == 1 + count + j), orders[j], order)
    phase = lax.rem(position * order, total).astype(jnp.float32) * (2.0 * math.pi / total)
    value = jnp.where(mode <= count, jnp.cos(phase), jnp.sin(phase))
    return jnp.where(mode <= 2 * count, value, 0.0)


def harmonics_kernel(total, where, orders, after, field, out):
    blocks, planes, _, lanes = field.shape
    mode = lax.broadcasted_iota(jnp.int32, (MODES, planes), 0)
    position = lax.broadcasted_iota(jnp.int32, (MODES, planes), 1) + where[0]
    basis = turns(position, mode, orders, total) * jnp.where(mode == 0, 1.0 / total, 2.0 / total)
    for b in range(blocks):
        edge = jnp.where(where[1] == 0, field[b, :, 7, :], field[b, :, 0, :])
        out[:, b * lanes : (b + 1) * lanes] = jnp.dot(
            basis, edge, precision=lax.Precision.HIGHEST, preferred_element_type=jnp.float32
        )


def read_all(refs, *at):
    own, up, down, far = refs
    return [r[(slot, *at)] for r in (own, up, far, down) for slot in range(2)]


def mix_kernel(scalars, plane, own_low, own_high, up, down, far, out):
    weight = [scalars[k] for k in range(INST)]
    cosine, sine = scalars[INST], scalars[INST + 1]
    at = plane[0]
    is_low = at == 1

    def mixed(var):
        own = [jnp.where(is_low, own_low[s, var, 0], own_high[s, var, 0]) for s in range(2)]
        u = own + [r[s, var, at] for r in (up, far, down) for s in range(2)]
        sums = []
        for a in range(INST):
            total = weight[a % INST] * u[0]
            for b in range(1, INST):
                total = total + weight[(a - b) % INST] * u[b]
            sums.append(total)
        return sums

    for var in (0, 1, 4, 5):
        for a, value in enumerate(mixed(var)):
            out[a, var] = value
    v, w = mixed(2), mixed(3)
    for a in range(INST):
        out[a, 2] = cosine * v[a] - sine * w[a]
        out[a, 3] = sine * v[a] + cosine * w[a]


def source_kernel(rims, scalars, *refs):
    if rims:
        outs, refs = refs[-4:], refs[:-4]
    else:
        outs, refs = refs[-1:], refs[:-1]
    if rims:
        ghost, nu = refs[-2:]
        refs = refs[:-2]
    size = len(refs) // 4
    own, up, down, far = (refs[k * size : (k + 1) * size] for k in range(4))
    ratio = scalars[0]
    c1, c2, c3 = (ratio * D1, ratio * D2, ratio * D3)
    if rims:
        out_own, out_up, out_down, out_far = outs
        order = (out_own, out_up, out_far, out_down)
    else:
        inst = lax.axis_index("inst")
        order = [outs[0].at[lax.rem(inst + k, 4)] for k in range(4)]
    for var in range(up[0].shape[1]):
        for p in range(size):
            u = [own[p][s, var, 0] for s in range(2)]
            u += [r[p][s, var, 0] for r in (up, far, down) for s in range(2)]
            near = [u[(n - 1) % INST] - u[(n + 1) % INST] for n in range(INST)]
            second = [c2 * (u[(n - 2) % INST] - u[(n + 2) % INST]) for n in range(4)]
            for n in range(INST):
                s = c1 * near[n] - c3 * near[(n + 4) % INST]
                s = s + second[n] if n < 4 else s - second[n - 4]
                order[n // 2][n % 2, var, p] = s
    if not rims:
        return

    def add_ghost(p, factor):
        for var in range(up[0].shape[1]):
            for n in range(INST):
                at = (n % 2, var, p)
                order[n // 2][at] = order[n // 2][at] - factor * ghost[n, var]

    @pl.when(scalars[1] > 0.5)
    def _():
        add_ghost(2, nu[0] + 0.5)

    @pl.when(scalars[2] > 0.5)
    def _():
        add_ghost(1, nu[1])


def stencil_kernel(nu, low, high, field, out):
    blocks, planes, rows, lanes = field.shape
    lane = lax.broadcasted_iota(jnp.int32, (rows, lanes), 1)
    row = lax.broadcasted_iota(jnp.int32, (rows, lanes), 0)
    for b in range(blocks):
        for p in range(planes):
            u = field[b, p]
            before = low[b] if p == 0 else field[b, p - 1]
            after = high[b] if p == planes - 1 else field[b, p + 1]
            left = jnp.where(lane == 0, 0.0, pltpu.roll(u, 1, 1))
            right = jnp.where(lane == lanes - 1, 0.0, pltpu.roll(u, lanes - 1, 1))
            above = jnp.where(row == 0, 0.0, pltpu.roll(u, 1, 0))
            below = jnp.where(row == rows - 1, 0.0, pltpu.roll(u, rows - 1, 0))
            lap = (before + after) + (above + below) + (left + right) - 6.0 * u
            out[b, p] = nu[p] * lap - (u - above) - 0.5 * (u - before)


def edge_kernel(total, where, orders, coeffs, facing, out):
    planes, blocks, rows, lanes = out.shape
    mode = lax.broadcasted_iota(jnp.int32, (planes, MODES), 1)
    position = lax.broadcasted_iota(jnp.int32, (planes, MODES), 0) + where[0]
    ghost = jnp.dot(
        turns(position, mode, orders, total),
        coeffs[...],
        precision=lax.Precision.HIGHEST,
        preferred_element_type=jnp.float32,
    )
    hit = lax.broadcasted_iota(jnp.int32, (rows, lanes), 0) == (1 - where[1]) * (rows - 1)
    for b in range(blocks):
        value = facing[...] * ghost[:, b * lanes : (b + 1) * lanes]
        for p in range(planes):
            out[p, b] = jnp.where(hit, value[p : p + 1], 0.0)


def final_kernel(base, size, places, inverse, edge, field, pre, *rest):
    new, residual, new_held, residual_held, sems = rest[-5:]
    count, planes, rows, lanes = field.shape
    pieces = rest[:4] if rest[0].shape[0] == count else [rest[0].at[j] for j in range(4)]
    tile = pl.ds(pl.multiple_of(places[4], 8), 8)
    runs = [(0, base, min(size, planes - base))]
    if base + size > planes:
        runs.append((planes - base, 0, base + size - planes))
    copies = []
    for j in range(0, count, 2):
        for p in range(size):
            plane = (base + p) % planes
            for b in (j, j + 1):
                for k, piece in enumerate(pieces):
                    if rest[0].shape[0] == count:
                        at = pl.ds(pl.multiple_of(places[k], 16), 16)
                    else:
                        at = pl.ds(16 * k, 16)
                    residual_held[b, p, at] = pre[b, plane, at] - piece[b, p]
                residual_held[b, p, tile] = residual_held[b, p, tile] + edge[plane, b]
            high, low = split_bf16(
                jnp.concatenate([residual_held[j, p], residual_held[j + 1, p]], 1)
            )
            change = jnp.dot(
                inverse[...],
                jnp.concatenate([high, high, low], 0),
                preferred_element_type=jnp.float32,
            )
            new_held[j, p] = field[j, plane] + change[:, :lanes]
            new_held[j + 1, p] = field[j + 1, plane] + change[:, lanes:]
        for b in (j, j + 1):
            for held, out in ((residual_held, residual), (new_held, new)):
                for source, target, length in runs:
                    copies.append(
                        pltpu.make_async_copy(
                            held.at[b, source : source + length],
                            out.at[b, target : target + length],
                            sems.at[len(copies)],
                        )
                    )
                    copies[-1].start()
    for one in copies:
        one.wait()


def lag_weights(lag):
    delta = jnp.arange(INST).astype(jnp.float32) - lag
    total = 1.0 + jnp.cos(math.pi * delta)
    for k in range(1, INST // 2):
        total = total + 2.0 * jnp.cos(2.0 * math.pi * k / INST * delta)
    return total / INST


def local(state, viscosity, blade_counts, mode_orders):
    _, local_inst, variables, planes, rows, lanes = state.shape
    quarter = rows // 4
    blocks = local_inst * variables
    mesh_count = lax.axis_size("mesh")
    total = planes * mesh_count
    which = lax.axis_index("row")
    inst = lax.axis_index("inst")
    mesh_idx = lax.axis_index("mesh")
    counts = blade_counts.astype(jnp.float32)
    ratio = counts[1 - which] / counts[which]
    angle = 2.0 * math.pi / counts[which]
    field = state.reshape(blocks, planes, rows, lanes)
    nu = viscosity[0]
    first = mesh_idx == 0
    last = mesh_idx == mesh_count - 1
    places = (quarter * ((inst + jnp.array([0, 1, 3, 2])) % 4)).astype(jnp.int32)
    where = jnp.stack([mesh_idx * planes, which, last]).astype(jnp.int32)

    def along(x, step):
        return lax.ppermute(x, "inst", [(j, (j + step) % 4) for j in range(4)])

    def in_hbm(*arrays):
        return [pltpu.with_memory_space_constraint(x, pltpu.HBM) for x in arrays]

    def exchange(up, down, far):
        from_down, from_up, from_far = along(up, 1), along(down, 3), along(far, 2)
        return from_up, from_down, from_far

    packed = pack(field, ((1, planes - 1), (0, 1)))
    gathered = exchange(*packed)

    top, bottom = pl.pallas_call(
        edges_kernel,
        out_shape=(shaped(blocks, rows, lanes),) * 2,
        in_specs=[HBM, VMEM],
        out_specs=(VMEM,) * 2,
        scratch_shapes=[pltpu.SemaphoreType.DMA((2, blocks))],
        compiler_params=params(),
        cost_estimate=cost(),
    )(pltpu.with_memory_space_constraint(field, pltpu.HBM), packed[0])
    low = lax.ppermute(top, "mesh", [(j, j + 1) for j in range(mesh_count - 1)])
    high = lax.ppermute(bottom, "mesh", [(j + 1, j) for j in range(mesh_count - 1)])

    def own_spec(plane, vars_at_once):
        return pl.BlockSpec(
            (2, vars_at_once, 1, quarter, lanes),
            lambda b, places: (0, b, plane, places[0] // quarter, 0),
        )

    split = (local_inst, variables)
    parted = field.reshape(*split, planes, rows, lanes)

    whole = shaped(*field.shape)
    at_once = 2
    slab = pl.BlockSpec((at_once, planes, rows, lanes), lambda b: (b, 0, 0, 0))
    plane = pl.BlockSpec((at_once, rows, lanes), lambda b: (b, 0, 0))
    pre = pl.pallas_call(
        stencil_kernel,
        grid=(blocks // at_once,),
        out_shape=pltpu.HBM(field.shape, jnp.float32),
        in_specs=[pl.BlockSpec((planes, rows, lanes), lambda b: (0, 0, 0)), plane, plane, slab],
        out_specs=slab,
        compiler_params=params(),
        cost_estimate=cost(),
    )(nu, *in_hbm(low, high), field)

    edge_rows = pl.BlockSpec(
        (blocks, planes, 8, lanes),
        lambda b, where, orders: (0, 0, (1 - where[1]) * (rows // 8 - 1), 0),
    )
    harmonics = pl.pallas_call(
        functools.partial(harmonics_kernel, total),
        out_shape=shaped(MODES, blocks * lanes),
        grid_spec=pltpu.PrefetchScalarGridSpec(
            num_scalar_prefetch=2,
            grid=(1,),
            in_specs=[VMEM, edge_rows],
            out_specs=pl.BlockSpec((MODES, blocks * lanes), lambda b, where, orders: (0, 0)),
        ),
        compiler_params=params(),
        cost_estimate=cost(),
    )(where, mode_orders, packed[0], field)
    def crossing(flip):
        return [
            (r * mesh_count + m, (1 - r) * mesh_count + (m ^ flip))
            for r in range(2)
            for m in range(mesh_count)
        ]

    def doubled(x, flip):
        return x + lax.ppermute(x, "mesh", [(m, m ^ flip) for m in range(mesh_count)])

    two_ways = [lax.ppermute(harmonics, ("row", "mesh"), crossing(flip)) for flip in (0, 1)]
    harmonics = doubled(two_ways[0] + two_ways[1], 2)
    early = harmonics
    harmonics = doubled(doubled(harmonics, 4), 8)

    scalars = jnp.stack([ratio, first.astype(jnp.float32), last.astype(jnp.float32)])

    def sources(own_planes, part, gathered, rims, after=()):
        at_once, size = 3, len(own_planes)
        pieces_in = [
            pl.BlockSpec(
                (2, at_once, 1, quarter, lanes),
                functools.partial(lambda plane, b, places: (0, b, plane, 0, 0), part + p),
            )
            for _ in range(3)
            for p in range(size)
        ]
        piece = pl.BlockSpec((2, at_once, size, quarter, lanes), lambda b, places: (0, b, 0, 0, 0))
        rim_specs = [
            pl.BlockSpec((INST, at_once, quarter, lanes), lambda b, places: (0, b, 0, 0)),
            pl.BlockSpec((2, quarter, lanes), lambda b, places: (0, 0, 0)),
        ]

        count = 4 if rims else 1

        def kernel(places, *refs):
            inputs, outputs = refs[: -count - len(after)], refs[-count:]
            source_kernel(bool(rims), *inputs, *outputs)

        if not rims:
            out_shape = (pltpu.HBM((4, *split, size, quarter, lanes), jnp.float32),)
            out_specs = (
                pl.BlockSpec(
                    (4, 2, at_once, size, quarter, lanes), lambda b, places: (0, 0, b, 0, 0, 0)
                ),
            )
        else:
            out_shape = (pltpu.HBM((*split, size, quarter, lanes), jnp.float32),) * 4
            out_specs = (piece,) * 4
        outs = pl.pallas_call(
            kernel,
            out_shape=out_shape,
            grid_spec=pltpu.PrefetchScalarGridSpec(
                num_scalar_prefetch=1,
                grid=(variables // at_once,),
                in_specs=[SMEM]
                + [own_spec(plane, at_once) for plane in own_planes]
                + pieces_in
                + rim_specs[: len(rims)]
                + [ANY] * len(after),
                out_specs=out_specs,
            ),
            compiler_params=params(),
            cost_estimate=cost(),
        )(
            places,
            scalars,
            *([parted] * size),
            *in_hbm(*(x.reshape(*split, -1, quarter, lanes) for x in gathered for _ in range(size))),
            *rims,
            *after,
        )
        if not rims:
            out = outs[0].reshape(4, blocks, size, quarter, lanes)
            return (lax.all_to_all(out, "inst", split_axis=0, concat_axis=0, tiled=True), out)
        own, up, down, far = (x.reshape(blocks, size, quarter, lanes) for x in outs)
        return (own, *exchange(up, down, far))

    one_source = sources(tuple(range(1, 6)), 0, gathered, (), after=(*in_hbm(pre), early,))

    weights = lag_weights(jnp.where(first, -ratio, ratio))
    turn = jnp.where(first, angle, -angle)
    ghost_shape = shaped(INST, variables, quarter, lanes)

    def mixer(places, *refs):
        mix_kernel(*refs[:-2], refs[-1])

    ghost_out = pl.pallas_call(
        mixer,
        out_shape=ghost_shape,
        grid_spec=pltpu.PrefetchScalarGridSpec(
            num_scalar_prefetch=1,
            grid=(1,),
            in_specs=[SMEM, SMEM, own_spec(0, variables), own_spec(planes - 1, variables)]
            + [pl.BlockSpec((2, variables, 2, quarter, lanes), lambda b, places: (0, 0, 3, 0, 0))] * 3
            + [ANY],
            out_specs=pl.BlockSpec(ghost_shape.shape, lambda b, places: (0, 0, 0, 0)),
        ),
        compiler_params=params(),
        cost_estimate=cost(),
    )(
        places,
        jnp.concatenate([weights, jnp.stack([jnp.cos(turn), jnp.sin(turn)])]),
        jnp.where(first, 1, 0).astype(jnp.int32)[None],
        parted,
        parted,
        *in_hbm(*(x.reshape(*split, planes, quarter, lanes) for x in gathered)),
        *in_hbm(one_source[1]),
    )
    ghost = lax.ppermute(ghost_out, "mesh", [(mesh_count - 1, 0), (0, mesh_count - 1)])

    rim_nu = lax.dynamic_slice(nu[:: planes - 1], (0, places[0], 0), (2, quarter, lanes))
    two_source = sources(
        (6, 7, 0), 5, gathered, (*in_hbm(ghost), rim_nu)
    )

    facing = jnp.where(which == 0, nu[:, rows - 1], nu[:, 0] + 1.0)
    edge = pl.pallas_call(
        functools.partial(edge_kernel, total),
        out_shape=shaped(planes, blocks, 8, lanes),
        in_specs=[SMEM, SMEM, VMEM, VMEM],
        out_specs=VMEM,
        compiler_params=params(),
        cost_estimate=cost(),
    )(where, mode_orders, harmonics, facing)

    inverse = jnp.asarray(inverse_parts(rows))
    with_facing = jnp.concatenate([places, jnp.where(which == 0, rows - 8, 0).astype(jnp.int32)[None]])
    kept = ()
    for base, size, group in ((1, 5, one_source[:1]), (1 + 5, planes - 5, two_source)):
        given = 5 + len(group)
        kept = pl.pallas_call(
            functools.partial(final_kernel, base, size),
            out_shape=(pltpu.HBM(field.shape, jnp.float32),) * 2,
            in_specs=[SMEM] + [VMEM] * (4 + len(group)) + [HBM] * len(kept),
            out_specs=(HBM,) * 2,
            scratch_shapes=[pltpu.VMEM((blocks, size, rows, lanes), jnp.float32)] * 2
            + [pltpu.SemaphoreType.DMA((4 * blocks,))],
            input_output_aliases={given: 0, given + 1: 1} if kept else {},
            compiler_params=params(),
            cost_estimate=cost(),
        )(with_facing, inverse, edge, field, pre, *group, *kept)
    new, residual = kept
    return (new.reshape(state.shape), residual.reshape(state.shape))


def solution(mesh):
    spread = P("row", "inst", None, "mesh", None, None)
    return jax.shard_map(
        local,
        mesh=mesh,
        in_specs=(spread, P("row", "mesh", None, None), P(), P()),
        out_specs=(spread, spread),
        check_vma=False,
    )
```

```python
import functools
import math

import numpy as np

import jax
import jax.numpy as jnp
from jax import lax
from jax.experimental import pallas as pl
from jax.experimental.pallas import tpu as pltpu
from jax.sharding import PartitionSpec as P

INST = 8
MODES = 24
LIMIT = 10 * 1024 * 1024
VMEM = pl.BlockSpec(memory_space=pltpu.VMEM)
SMEM = pl.BlockSpec(memory_space=pltpu.SMEM)
ANY = pl.BlockSpec(memory_space=pl.ANY)
HBM = pl.BlockSpec(memory_space=pltpu.HBM)
D1 = -0.5 / math.tan(math.pi / 8)
D2 = 0.5 / math.tan(math.pi / 4)
D3 = -0.5 / math.tan(3 * math.pi / 8)


def shaped(*dims):
    return jax.ShapeDtypeStruct(dims, jnp.float32)


def cost():
    return pl.CostEstimate(flops=1, bytes_accessed=1, transcendentals=0)


def inverse_parts(length):
    steps = np.arange(1, length + 1).astype(np.float64)
    basis = math.sqrt(2.0 / (length + 1)) * np.sin(
        math.pi * steps[:, None] * steps[None, :] / (length + 1)
    )
    eigen = 2.0 - np.cos(math.pi * steps / (length + 1))
    inverse = (0.2 * (basis / eigen[None, :]) @ basis.T).astype(np.float32)
    high = inverse.astype(jnp.bfloat16)
    low = (inverse - high.astype(np.float32)).astype(jnp.bfloat16)
    return np.concatenate([high, low, high], axis=1)


def split_bf16(x):
    high = x.astype(jnp.bfloat16)
    return high, (x - high.astype(jnp.float32)).astype(jnp.bfloat16)


def params():
    return pltpu.CompilerParams(vmem_limit_bytes=LIMIT)


def pack_kernel(planes, field, *rest):
    sems = rest[-1]
    copies = []

    def copy(source, target):
        one = pltpu.make_async_copy(source, target, sems.at[len(copies)])
        one.start()
        copies.append(one)

    outs = rest[:3]
    for k, out in zip((1, 3, 2), outs):
        place = lax.rem(lax.axis_index("inst") + k, 4) * 16
        rows = pl.ds(pl.multiple_of(place, 16), 16)
        done = 0
        for start, size in planes:
            for b in range(0, field.shape[0], 4):
                copy(
                    field.at[b : b + 4, start : start + size, rows, :],
                    out.at[b : b + 4, done : done + size],
                )
            done += size
    for one in copies:
        one.wait()


def edges_kernel(field, after, top, bottom, own, sems):
    rows = pl.ds(pl.multiple_of(lax.axis_index("inst") * 16, 16), 16)
    copies = [
        pltpu.make_async_copy(field.at[b, plane], out.at[b], sems.at[k, b])
        for k, (plane, out) in enumerate(((field.shape[1] - 1, top), (0, bottom)))
        for b in range(field.shape[0])
    ]
    last = field.shape[1] - 1
    copies.append(
        pltpu.make_async_copy(field.at[:, 1:, rows, :], own.at[:, :last], sems.at[2, 0])
    )
    copies.append(
        pltpu.make_async_copy(field.at[:, :1, rows, :], own.at[:, last:], sems.at[2, 1])
    )
    for one in copies:
        one.start()
    for one in copies:
        one.wait()


def pack(field, planes):
    blocks, _, rows, lanes = field.shape
    size = sum(size for _, size in planes)
    return pl.pallas_call(
        functools.partial(pack_kernel, planes),
        out_shape=(shaped(blocks, size, rows // 4, lanes),) * 3,
        in_specs=[HBM],
        out_specs=(VMEM,) * 3,
        scratch_shapes=[pltpu.SemaphoreType.DMA((32,))],
        compiler_params=params(),
        cost_estimate=cost(),
    )(pltpu.with_memory_space_constraint(field, pltpu.HBM))


def turns(position, mode, orders, total):
    order = jnp.zeros(mode.shape, jnp.int32)
    count = orders.shape[0]
    for j in range(count):
        order = jnp.where((mode == 1 + j) | (mode == 1 + count + j), orders[j], order)
    phase = lax.rem(position * order, total).astype(jnp.float32) * (2.0 * math.pi / total)
    value = jnp.where(mode <= count, jnp.cos(phase), jnp.sin(phase))
    return jnp.where(mode <= 2 * count, value, 0.0)


def harmonics_kernel(total, orders, after, front, back, out):
    blocks, planes, _, lanes = front.shape
    mode = lax.broadcasted_iota(jnp.int32, (MODES, planes), 0)
    position = lax.broadcasted_iota(jnp.int32, (MODES, planes), 1) + lax.axis_index("mesh") * planes
    basis = turns(position, mode, orders, total) * jnp.where(mode == 0, 1.0 / total, 2.0 / total)
    rotor = lax.axis_index("row") == 0
    for b in range(blocks):
        edge = jnp.where(rotor, back[b, :, 7, :], front[b, :, 0, :])
        out[:, b * lanes : (b + 1) * lanes] = jnp.dot(
            basis, edge, precision=lax.Precision.HIGHEST, preferred_element_type=jnp.float32
        )


def mix_kernel(scalars, own, up, down, far, after, out):
    weight = [scalars[k] for k in range(INST)]
    cosine, sine = scalars[INST], scalars[INST + 1]
    at = jnp.where(lax.axis_index("mesh") == 0, 1, 0)

    def mixed(var):
        u = [r[s, var, at] for r in (own, up, far, down) for s in range(2)]
        sums = []
        for a in range(INST):
            total = weight[a % INST] * u[0]
            for b in range(1, INST):
                total = total + weight[(a - b) % INST] * u[b]
            sums.append(total)
        return sums

    for var in (0, 1, 4, 5):
        for a, value in enumerate(mixed(var)):
            out[a, var] = value
    v, w = mixed(2), mixed(3)
    for a in range(INST):
        out[a, 2] = cosine * v[a] - sine * w[a]
        out[a, 3] = sine * v[a] + cosine * w[a]


def source_kernel(rims, scalars, *refs):
    if rims:
        outs, refs = refs[-4:], refs[:-4]
    else:
        outs, refs = refs[-1:], refs[:-1]
    if rims:
        ghost, nu = refs[-2:]
        refs = refs[:-2]
    size = len(refs) // 4
    own, up, down, far = (refs[k * size : (k + 1) * size] for k in range(4))
    ratio = scalars[0]
    c1, c2, c3 = (ratio * D1, ratio * D2, ratio * D3)
    if rims:
        out_own, out_up, out_down, out_far = outs
        order = (out_own, out_up, out_far, out_down)
    else:
        inst = lax.axis_index("inst")
        order = [outs[0].at[lax.rem(inst + k, 4)] for k in range(4)]
    for var in range(up[0].shape[1]):
        for p in range(size):
            u = [own[p][s, var, 0] for s in range(2)]
            u += [r[p][s, var, 0] for r in (up, far, down) for s in range(2)]
            near = [u[(n - 1) % INST] - u[(n + 1) % INST] for n in range(INST)]
            second = [c2 * (u[(n - 2) % INST] - u[(n + 2) % INST]) for n in range(4)]
            for n in range(INST):
                s = c1 * near[n] - c3 * near[(n + 4) % INST]
                s = s + second[n] if n < 4 else s - second[n - 4]
                order[n // 2][n % 2, var, p] = s
    if not rims:
        return

    def add_ghost(p, factor):
        for var in range(up[0].shape[1]):
            for n in range(INST):
                at = (n % 2, var, p)
                order[n // 2][at] = order[n // 2][at] - factor * ghost[n, var]

    place = pl.ds(pl.multiple_of(lax.axis_index("inst") * 16, 16), 16)

    @pl.when(lax.axis_index("mesh") == 0)
    def _():
        add_ghost(size - 1, nu[0, place, :] + 0.5)

    @pl.when(lax.axis_index("mesh") == lax.axis_size("mesh") - 1)
    def _():
        add_ghost(size - 2, nu[nu.shape[0] - 1, place, :])


def stencil_kernel(nu, low, high, field, out):
    blocks, planes, rows, lanes = field.shape
    lane = lax.broadcasted_iota(jnp.int32, (rows, lanes), 1)
    row = lax.broadcasted_iota(jnp.int32, (rows, lanes), 0)
    for b in range(blocks):
        for p in range(planes):
            u = field[b, p]
            before = low[b] if p == 0 else field[b, p - 1]
            after = high[b] if p == planes - 1 else field[b, p + 1]
            left = jnp.where(lane == 0, 0.0, pltpu.roll(u, 1, 1))
            right = jnp.where(lane == lanes - 1, 0.0, pltpu.roll(u, lanes - 1, 1))
            above = jnp.where(row == 0, 0.0, pltpu.roll(u, 1, 0))
            below = jnp.where(row == rows - 1, 0.0, pltpu.roll(u, rows - 1, 0))
            lap = (before + after) + (above + below) + (left + right) - 6.0 * u
            out[b, p] = nu[p] * lap - (u - above) - 0.5 * (u - before)


def add_kernel(one, two, after, out):
    out[...] = one[...] + two[...]


def edge_kernel(total, orders, one, two, nu, out):
    planes, blocks, rows, lanes = out.shape
    mode = lax.broadcasted_iota(jnp.int32, (planes, MODES), 1)
    position = lax.broadcasted_iota(jnp.int32, (planes, MODES), 0) + lax.axis_index("mesh") * planes
    ghost = jnp.dot(
        turns(position, mode, orders, total),
        one[...] + two[...],
        precision=lax.Precision.HIGHEST,
        preferred_element_type=jnp.float32,
    )
    rotor = lax.axis_index("row") == 0
    hit = lax.broadcasted_iota(jnp.int32, (rows, lanes), 0) == jnp.where(rotor, rows - 1, 0)
    for p in range(planes):
        facing = jnp.where(rotor, nu[p, nu.shape[1] - 1 :, :], nu[p, :1, :] + 1.0)
        for b in range(blocks):
            value = facing * ghost[p : p + 1, b * lanes : (b + 1) * lanes]
            out[p, b] = jnp.where(hit, value, 0.0)


def final_kernel(base, size, inverse, edge, field, pre, *rest):
    new, residual, new_held, residual_held, sems = rest[-5:]
    count, planes, rows, lanes = field.shape
    pieces = rest[:4] if rest[0].shape[0] == count else [rest[0].at[j] for j in range(4)]
    tile = pl.ds(pl.multiple_of((1 - lax.axis_index("row")) * (rows - 8), 8), 8)
    inst = lax.axis_index("inst")
    places = [16 * lax.rem(inst + k, 4) for k in (0, 1, 3, 2)]
    runs = [(0, base, min(size, planes - base))]
    if base + size > planes:
        runs.append((planes - base, 0, base + size - planes))
    copies = []
    for j in range(0, count, 2):
        for p in range(size):
            plane = (base + p) % planes
            for b in (j, j + 1):
                for k, piece in enumerate(pieces):
                    if rest[0].shape[0] == count:
                        at = pl.ds(pl.multiple_of(places[k], 16), 16)
                    else:
                        at = pl.ds(16 * k, 16)
                    residual_held[b, p, at] = pre[b, plane, at] - piece[b, p]
                residual_held[b, p, tile] = residual_held[b, p, tile] + edge[plane, b]
            high, low = split_bf16(
                jnp.concatenate([residual_held[j, p], residual_held[j + 1, p]], 1)
            )
            change = jnp.dot(
                inverse[...],
                jnp.concatenate([high, high, low], 0),
                preferred_element_type=jnp.float32,
            )
            new_held[j, p] = field[j, plane] + change[:, :lanes]
            new_held[j + 1, p] = field[j + 1, plane] + change[:, lanes:]
        for b in (j, j + 1):
            for held, out in ((residual_held, residual), (new_held, new)):
                for source, target, length in runs:
                    copies.append(
                        pltpu.make_async_copy(
                            held.at[b, source : source + length],
                            out.at[b, target : target + length],
                            sems.at[len(copies)],
                        )
                    )
                    copies[-1].start()
    for one in copies:
        one.wait()


def lag_weights(lag):
    delta = jnp.arange(INST).astype(jnp.float32) - lag
    total = 1.0 + jnp.cos(math.pi * delta)
    for k in range(1, INST // 2):
        total = total + 2.0 * jnp.cos(2.0 * math.pi * k / INST * delta)
    return total / INST


def local(state, viscosity, blade_counts, mode_orders):
    _, local_inst, variables, planes, rows, lanes = state.shape
    quarter = rows // 4
    blocks = local_inst * variables
    mesh_count = lax.axis_size("mesh")
    total = planes * mesh_count
    which = lax.axis_index("row")
    inst = lax.axis_index("inst")
    mesh_idx = lax.axis_index("mesh")
    counts = blade_counts.astype(jnp.float32)
    ratio = counts[1 - which] / counts[which]
    angle = 2.0 * math.pi / counts[which]
    field = state.reshape(blocks, planes, rows, lanes)
    nu = viscosity[0]
    first = mesh_idx == 0
    last = mesh_idx == mesh_count - 1

    def along(x, step):
        return lax.ppermute(x, "inst", [(j, (j + step) % 4) for j in range(4)])

    def in_hbm(*arrays):
        return [pltpu.with_memory_space_constraint(x, pltpu.HBM) for x in arrays]

    def exchange(up, down, far):
        from_down, from_up, from_far = along(up, 1), along(down, 3), along(far, 2)
        return from_up, from_down, from_far

    packed = pack(field, ((1, planes - 1), (0, 1)))
    gathered = exchange(*packed)

    top, bottom, own = pl.pallas_call(
        edges_kernel,
        out_shape=(shaped(blocks, rows, lanes),) * 2 + (shaped(blocks, planes, quarter, lanes),),
        in_specs=[HBM, VMEM],
        out_specs=(VMEM,) * 3,
        scratch_shapes=[pltpu.SemaphoreType.DMA((3, blocks))],
        compiler_params=params(),
        cost_estimate=cost(),
    )(pltpu.with_memory_space_constraint(field, pltpu.HBM), packed[0])
    low = lax.ppermute(top, "mesh", [(j, j + 1) for j in range(mesh_count - 1)])
    high = lax.ppermute(bottom, "mesh", [(j + 1, j) for j in range(mesh_count - 1)])

    split = (local_inst, variables)
    all_quarters = in_hbm(*(x.reshape(*split, planes, quarter, lanes) for x in (own, *gathered)))

    whole = shaped(*field.shape)
    at_once = 2
    slab = pl.BlockSpec((at_once, planes, rows, lanes), lambda b: (b, 0, 0, 0))
    plane = pl.BlockSpec((at_once, rows, lanes), lambda b: (b, 0, 0))
    pre = pl.pallas_call(
        stencil_kernel,
        grid=(blocks // at_once,),
        out_shape=pltpu.HBM(field.shape, jnp.float32),
        in_specs=[pl.BlockSpec((planes, rows, lanes), lambda b: (0, 0, 0)), plane, plane, slab],
        out_specs=slab,
        compiler_params=params(),
        cost_estimate=cost(),
    )(nu, *in_hbm(low, high), field)

    harmonics = pl.pallas_call(
        functools.partial(harmonics_kernel, total),
        out_shape=shaped(MODES, blocks * lanes),
        grid=(1,),
        in_specs=[
            SMEM,
            VMEM,
            pl.BlockSpec((blocks, planes, 8, lanes), lambda b: (0, 0, 0, 0)),
            pl.BlockSpec((blocks, planes, 8, lanes), lambda b: (0, 0, rows // 8 - 1, 0)),
        ],
        out_specs=pl.BlockSpec((MODES, blocks * lanes), lambda b: (0, 0)),
        compiler_params=params(),
        cost_estimate=cost(),
    )(mode_orders, packed[0], field, field)

    def crossing(flip):
        return [
            (r * mesh_count + m, (1 - r) * mesh_count + (m ^ flip))
            for r in range(2)
            for m in range(mesh_count)
        ]

    def doubled(x, flip):
        return x + lax.ppermute(x, "mesh", [(m, m ^ flip) for m in range(mesh_count)])

    two_ways = [lax.ppermute(harmonics, ("row", "mesh"), crossing(flip)) for flip in (0, 1)]
    harmonics = two_ways[0] + two_ways[1]
    early = lax.ppermute(harmonics, "mesh", [(m, m ^ 2) for m in range(mesh_count)])

    def sources(start, size, rims, after=()):
        at_once = 3
        pieces_in = [
            pl.BlockSpec(
                (2, at_once, 1, quarter, lanes),
                functools.partial(lambda plane, b: (0, b, plane, 0, 0), start + p),
            )
            for _ in range(4)
            for p in range(size)
        ]
        rim_specs = [
            pl.BlockSpec((INST, at_once, quarter, lanes), lambda b: (0, b, 0, 0)),
            pl.BlockSpec((planes, rows, lanes), lambda b: (0, 0, 0)),
        ]
        count = 4 if rims else 1

        def kernel(*refs):
            inputs, outputs = refs[: -count - len(after)], refs[-count:]
            source_kernel(bool(rims), *inputs, *outputs)

        if not rims:
            out_shape = (pltpu.HBM((4, *split, size, quarter, lanes), jnp.float32),)
            out_specs = (
                pl.BlockSpec((4, 2, at_once, size, quarter, lanes), lambda b: (0, 0, b, 0, 0, 0)),
            )
        else:
            out_shape = (pltpu.HBM((*split, size, quarter, lanes), jnp.float32),) * 4
            out_specs = (
                pl.BlockSpec((2, at_once, size, quarter, lanes), lambda b: (0, b, 0, 0, 0)),
            ) * 4
        outs = pl.pallas_call(
            kernel,
            out_shape=out_shape,
            grid=(variables // at_once,),
            in_specs=[SMEM] + pieces_in + rim_specs[: len(rims)] + [ANY] * len(after),
            out_specs=out_specs,
            compiler_params=params(),
            cost_estimate=cost(),
        )(ratio[None], *(x for x in all_quarters for _ in range(size)), *rims, *after)
        if not rims:
            out = outs[0].reshape(4, blocks, size, quarter, lanes)
            return (lax.all_to_all(out, "inst", split_axis=0, concat_axis=0, tiled=True), out)
        own, up, down, far = (x.reshape(blocks, size, quarter, lanes) for x in outs)
        return (own, *exchange(up, down, far))

    one_source = sources(0, 5, (), after=(*in_hbm(pre), early))

    weights = lag_weights(jnp.where(first, -ratio, ratio))
    turn = jnp.where(first, angle, -angle)
    ghost_shape = shaped(INST, variables, quarter, lanes)

    outermost = pl.BlockSpec((2, variables, 2, quarter, lanes), lambda b: (0, 0, 3, 0, 0))
    ghost_out = pl.pallas_call(
        mix_kernel,
        out_shape=ghost_shape,
        grid=(1,),
        in_specs=[SMEM] + [outermost] * 4 + [ANY],
        out_specs=pl.BlockSpec(ghost_shape.shape, lambda b: (0, 0, 0, 0)),
        compiler_params=params(),
        cost_estimate=cost(),
    )(
        jnp.concatenate([weights, jnp.stack([jnp.cos(turn), jnp.sin(turn)])]),
        *all_quarters,
        *in_hbm(one_source[1]),
    )
    ghost = lax.ppermute(ghost_out, "mesh", [(mesh_count - 1, 0), (0, mesh_count - 1)])

    two_source = sources(5, 3, (*in_hbm(ghost), nu))

    harmonics = pl.pallas_call(
        add_kernel,
        out_shape=harmonics,
        in_specs=[VMEM, VMEM, ANY],
        out_specs=VMEM,
        compiler_params=params(),
        cost_estimate=cost(),
    )(harmonics, early, *in_hbm(two_source[0]))
    harmonics = doubled(harmonics, 4)
    edge = pl.pallas_call(
        functools.partial(edge_kernel, total),
        out_shape=shaped(planes, blocks, 8, lanes),
        in_specs=[SMEM, VMEM, VMEM, VMEM],
        out_specs=VMEM,
        compiler_params=params(),
        cost_estimate=cost(),
    )(
        mode_orders,
        harmonics,
        lax.ppermute(harmonics, "mesh", [(m, m ^ 8) for m in range(mesh_count)]),
        nu,
    )

    inverse = jnp.asarray(inverse_parts(rows))
    kept = ()
    for base, size, group in ((1, 5, one_source[:1]), (1 + 5, planes - 5, two_source)):
        given = 4 + len(group)
        kept = pl.pallas_call(
            functools.partial(final_kernel, base, size),
            out_shape=(pltpu.HBM(field.shape, jnp.float32),) * 2,
            in_specs=[VMEM] * (4 + len(group)) + [HBM] * len(kept),
            out_specs=(HBM,) * 2,
            scratch_shapes=[pltpu.VMEM((blocks, size, rows, lanes), jnp.float32)] * 2
            + [pltpu.SemaphoreType.DMA((4 * blocks,))],
            input_output_aliases={given: 0, given + 1: 1} if kept else {},
            compiler_params=params(),
            cost_estimate=cost(),
        )(inverse, edge, field, pre, *group, *kept)
    new, residual = kept
    return (new.reshape(state.shape), residual.reshape(state.shape))


def solution(mesh):
    spread = P("row", "inst", None, "mesh", None, None)
    return jax.shard_map(
        local,
        mesh=mesh,
        in_specs=(spread, P("row", "mesh", None, None), P(), P()),
        out_specs=(spread, spread),
        check_vma=False,
    )
```

```python
import functools
import math

import numpy as np

import jax
import jax.numpy as jnp
from jax import lax
from jax.experimental import pallas as pl
from jax.experimental.pallas import tpu as pltpu
from jax.sharding import PartitionSpec as P

INST = 8
OUTER = 6
MODES = 24
LIMIT = 10 * 1024 * 1024
VMEM = pl.BlockSpec(memory_space=pltpu.VMEM)
SMEM = pl.BlockSpec(memory_space=pltpu.SMEM)
ANY = pl.BlockSpec(memory_space=pl.ANY)
HBM = pl.BlockSpec(memory_space=pltpu.HBM)
D1 = -0.5 / math.tan(math.pi / 8)
D2 = 0.5 / math.tan(math.pi / 4)
D3 = -0.5 / math.tan(3 * math.pi / 8)


def shaped(*dims):
    return jax.ShapeDtypeStruct(dims, jnp.float32)


def cost():
    return pl.CostEstimate(flops=1, bytes_accessed=1, transcendentals=0)


def inverse_parts(length):
    steps = np.arange(1, length + 1).astype(np.float64)
    basis = math.sqrt(2.0 / (length + 1)) * np.sin(
        math.pi * steps[:, None] * steps[None, :] / (length + 1)
    )
    eigen = 2.0 - np.cos(math.pi * steps / (length + 1))
    inverse = (0.2 * (basis / eigen[None, :]) @ basis.T).astype(np.float32)
    high = inverse.astype(jnp.bfloat16)
    low = (inverse - high.astype(np.float32)).astype(jnp.bfloat16)
    return np.concatenate([high, low, high], axis=1)


def split_bf16(x):
    high = x.astype(jnp.bfloat16)
    return high, (x - high.astype(jnp.float32)).astype(jnp.bfloat16)


def params():
    return pltpu.CompilerParams(vmem_limit_bytes=LIMIT)


def pack_kernel(planes, field, *rest):
    sems = rest[-1]
    copies = []

    def copy(source, target):
        one = pltpu.make_async_copy(source, target, sems.at[len(copies)])
        one.start()
        copies.append(one)

    outs = rest[:3]
    for k, out in zip((1, 3, 2), outs):
        place = lax.rem(lax.axis_index("inst") + k, 4) * 16
        rows = pl.ds(pl.multiple_of(place, 16), 16)
        done = 0
        for start, size in planes:
            for b in range(0, field.shape[0], 4):
                copy(
                    field.at[b : b + 4, start : start + size, rows, :],
                    out.at[b : b + 4, done : done + size],
                )
            done += size
    for one in copies:
        one.wait()


def edges_kernel(field, after, top, bottom, own, sems):
    rows = pl.ds(pl.multiple_of(lax.axis_index("inst") * 16, 16), 16)
    copies = [
        pltpu.make_async_copy(field.at[b, plane], out.at[b], sems.at[k, b])
        for k, (plane, out) in enumerate(((field.shape[1] - 1, top), (0, bottom)))
        for b in range(field.shape[0])
    ]
    last = field.shape[1] - 1
    copies.append(
        pltpu.make_async_copy(field.at[:, 1:, rows, :], own.at[:, :last], sems.at[2, 0])
    )
    copies.append(
        pltpu.make_async_copy(field.at[:, :1, rows, :], own.at[:, last:], sems.at[2, 1])
    )
    for one in copies:
        one.start()
    for one in copies:
        one.wait()


def pack(field, planes):
    blocks, _, rows, lanes = field.shape
    size = sum(size for _, size in planes)
    return pl.pallas_call(
        functools.partial(pack_kernel, planes),
        out_shape=(shaped(blocks, size, rows // 4, lanes),) * 3,
        in_specs=[HBM],
        out_specs=(VMEM,) * 3,
        scratch_shapes=[pltpu.SemaphoreType.DMA((32,))],
        compiler_params=params(),
        cost_estimate=cost(),
    )(pltpu.with_memory_space_constraint(field, pltpu.HBM))


def turns(position, mode, orders, total):
    order = jnp.zeros(mode.shape, jnp.int32)
    count = orders.shape[0]
    for j in range(count):
        order = jnp.where((mode == 1 + j) | (mode == 1 + count + j), orders[j], order)
    phase = lax.rem(position * order, total).astype(jnp.float32) * (2.0 * math.pi / total)
    value = jnp.where(mode <= count, jnp.cos(phase), jnp.sin(phase))
    return jnp.where(mode <= 2 * count, value, 0.0)


def harmonics_kernel(total, orders, after, front, back, out):
    blocks, planes, _, lanes = front.shape
    mode = lax.broadcasted_iota(jnp.int32, (MODES, planes), 0)
    position = lax.broadcasted_iota(jnp.int32, (MODES, planes), 1) + lax.axis_index("mesh") * planes
    basis = turns(position, mode, orders, total) * jnp.where(mode == 0, 1.0 / total, 2.0 / total)
    rotor = lax.axis_index("row") == 0
    for b in range(blocks):
        edge = jnp.where(rotor, back[b, :, 7, :], front[b, :, 0, :])
        out[:, b * lanes : (b + 1) * lanes] = jnp.dot(
            basis, edge, precision=lax.Precision.HIGHEST, preferred_element_type=jnp.float32
        )


def mix_kernel(scalars, own, up, down, far, after, out):
    weight = [scalars[k] for k in range(INST)]
    cosine, sine = scalars[INST], scalars[INST + 1]
    at = jnp.where(lax.axis_index("mesh") == 0, 1, 0)

    def mixed(var):
        u = [r[s, var, at] for r in (own, up, far, down) for s in range(2)]
        sums = []
        for a in range(INST):
            total = weight[a % INST] * u[0]
            for b in range(1, INST):
                total = total + weight[(a - b) % INST] * u[b]
            sums.append(total)
        return sums

    for var in (0, 1, 4, 5):
        for a, value in enumerate(mixed(var)):
            out[a, var] = value
    v, w = mixed(2), mixed(3)
    for a in range(INST):
        out[a, 2] = cosine * v[a] - sine * w[a]
        out[a, 3] = sine * v[a] + cosine * w[a]


def source_kernel(rims, scalars, *refs):
    if rims:
        outs, refs = refs[-4:], refs[:-4]
    else:
        outs, refs = refs[-1:], refs[:-1]
    if rims:
        ghost, nu = refs[-2:]
        refs = refs[:-2]
    size = len(refs) // 4
    own, up, down, far = (refs[k * size : (k + 1) * size] for k in range(4))
    ratio = scalars[0]
    c1, c2, c3 = (ratio * D1, ratio * D2, ratio * D3)
    if rims:
        out_own, out_up, out_down, out_far = outs
        order = (out_own, out_up, out_far, out_down)
    else:
        inst = lax.axis_index("inst")
        order = [outs[0].at[lax.rem(inst + k, 4)] for k in range(4)]
    for var in range(up[0].shape[1]):
        for p in range(size):
            u = [own[p][s, var, 0] for s in range(2)]
            u += [r[p][s, var, 0] for r in (up, far, down) for s in range(2)]
            near = [u[(n - 1) % INST] - u[(n + 1) % INST] for n in range(INST)]
            second = [c2 * (u[(n - 2) % INST] - u[(n + 2) % INST]) for n in range(4)]
            for n in range(INST):
                s = c1 * near[n] - c3 * near[(n + 4) % INST]
                s = s + second[n] if n < 4 else s - second[n - 4]
                order[n // 2][n % 2, var, p] = s
    if not rims:
        return

    def add_ghost(p, factor):
        for var in range(up[0].shape[1]):
            for n in range(INST):
                at = (n % 2, var, p)
                order[n // 2][at] = order[n // 2][at] - factor * ghost[n, var]

    place = pl.ds(pl.multiple_of(lax.axis_index("inst") * 16, 16), 16)

    @pl.when(lax.axis_index("mesh") == 0)
    def _():
        add_ghost(size - 1, nu[0, place, :] + 0.5)

    @pl.when(lax.axis_index("mesh") == lax.axis_size("mesh") - 1)
    def _():
        add_ghost(size - 2, nu[nu.shape[0] - 1, place, :])


def stencil_kernel(nu, low, high, field, one, two):
    blocks, planes, rows, lanes = field.shape
    lane = lax.broadcasted_iota(jnp.int32, (rows, lanes), 1)
    row = lax.broadcasted_iota(jnp.int32, (rows, lanes), 0)
    for b in range(blocks):
        for p in range(planes):
            u = field[b, p]
            before = low[b] if p == 0 else field[b, p - 1]
            after = high[b] if p == planes - 1 else field[b, p + 1]
            left = jnp.where(lane == 0, 0.0, pltpu.roll(u, 1, 1))
            right = jnp.where(lane == lanes - 1, 0.0, pltpu.roll(u, lanes - 1, 1))
            above = jnp.where(row == 0, 0.0, pltpu.roll(u, 1, 0))
            below = jnp.where(row == rows - 1, 0.0, pltpu.roll(u, rows - 1, 0))
            lap = (before + after) + (above + below) + (left + right) - 6.0 * u
            at = (p - 1) % planes
            out, at = (one, at) if at < OUTER else (two, at - OUTER)
            out[b, at] = nu[p] * lap - (u - above) - 0.5 * (u - before)


def add_kernel(one, two, after, out):
    out[...] = one[...] + two[...]


def edge_kernel(total, orders, one, two, nu, out):
    planes, blocks, rows, lanes = out.shape
    mode = lax.broadcasted_iota(jnp.int32, (planes, MODES), 1)
    position = lax.broadcasted_iota(jnp.int32, (planes, MODES), 0) + lax.axis_index("mesh") * planes
    ghost = jnp.dot(
        turns(position, mode, orders, total),
        one[...] + two[...],
        precision=lax.Precision.HIGHEST,
        preferred_element_type=jnp.float32,
    )
    rotor = lax.axis_index("row") == 0
    hit = lax.broadcasted_iota(jnp.int32, (rows, lanes), 0) == jnp.where(rotor, rows - 1, 0)
    for p in range(planes):
        facing = jnp.where(rotor, nu[p, nu.shape[1] - 1 :, :], nu[p, :1, :] + 1.0)
        for b in range(blocks):
            value = facing * ghost[p : p + 1, b * lanes : (b + 1) * lanes]
            out[p, b] = jnp.where(hit, value, 0.0)


def final_kernel(start, streamed, inverse, edge, field, pre, *rest):
    if streamed:
        rest, held_in, sems_in = rest[:-2], *rest[-2:]
        arrivals = [
            pltpu.make_async_copy(pre.at[b], held_in.at[b], sems_in.at[b])
            for b in range(field.shape[0])
        ]
        for one in arrivals:
            one.start()
        pre = held_in
    new, residual, new_held, residual_held, sems = rest[-5:]
    count, planes, rows, lanes = field.shape
    size = pre.shape[1]
    base = (start + 1) % planes
    pieces = rest[:4] if rest[0].shape[0] == count else [rest[0].at[j] for j in range(4)]
    tile = pl.ds(pl.multiple_of((1 - lax.axis_index("row")) * (rows - 8), 8), 8)
    inst = lax.axis_index("inst")
    places = [16 * lax.rem(inst + k, 4) for k in (0, 1, 3, 2)]
    runs = [(0, base, min(size, planes - base))]
    if base + size > planes:
        runs.append((planes - base, 0, base + size - planes))
    copies = []
    for j in range(0, count, 2):
        if streamed:
            arrivals[j].wait()
            arrivals[j + 1].wait()
        for p in range(size):
            plane = (base + p) % planes
            for b in (j, j + 1):
                for k, piece in enumerate(pieces):
                    if rest[0].shape[0] == count:
                        at = pl.ds(pl.multiple_of(places[k], 16), 16)
                    else:
                        at = pl.ds(16 * k, 16)
                    residual_held[b, p, at] = pre[b, p, at] - piece[b, p]
                residual_held[b, p, tile] = residual_held[b, p, tile] + edge[plane, b]
            high, low = split_bf16(
                jnp.concatenate([residual_held[j, p], residual_held[j + 1, p]], 1)
            )
            change = jnp.dot(
                inverse[...],
                jnp.concatenate([high, high, low], 0),
                preferred_element_type=jnp.float32,
            )
            new_held[j, p] = field[j, plane] + change[:, :lanes]
            new_held[j + 1, p] = field[j + 1, plane] + change[:, lanes:]
        for b in (j, j + 1):
            for held, out in ((residual_held, residual), (new_held, new)):
                for source, target, length in runs:
                    copies.append(
                        pltpu.make_async_copy(
                            held.at[b, source : source + length],
                            out.at[b, target : target + length],
                            sems.at[len(copies)],
                        )
                    )
                    copies[-1].start()
    for one in copies:
        one.wait()


def lag_weights(lag):
    delta = jnp.arange(INST).astype(jnp.float32) - lag
    total = 1.0 + jnp.cos(math.pi * delta)
    for k in range(1, INST // 2):
        total = total + 2.0 * jnp.cos(2.0 * math.pi * k / INST * delta)
    return total / INST


def local(state, viscosity, blade_counts, mode_orders):
    _, local_inst, variables, planes, rows, lanes = state.shape
    quarter = rows // 4
    blocks = local_inst * variables
    mesh_count = lax.axis_size("mesh")
    total = planes * mesh_count
    which = lax.axis_index("row")
    inst = lax.axis_index("inst")
    mesh_idx = lax.axis_index("mesh")
    counts = blade_counts.astype(jnp.float32)
    ratio = counts[1 - which] / counts[which]
    angle = 2.0 * math.pi / counts[which]
    field = state.reshape(blocks, planes, rows, lanes)
    nu = viscosity[0]
    first = mesh_idx == 0
    last = mesh_idx == mesh_count - 1

    def along(x, step):
        return lax.ppermute(x, "inst", [(j, (j + step) % 4) for j in range(4)])

    def in_hbm(*arrays):
        return [pltpu.with_memory_space_constraint(x, pltpu.HBM) for x in arrays]

    def exchange(up, down, far):
        from_down, from_up, from_far = along(up, 1), along(down, 3), along(far, 2)
        return from_up, from_down, from_far

    packed = pack(field, ((1, planes - 1), (0, 1)))
    gathered = exchange(*packed)

    top, bottom, own = pl.pallas_call(
        edges_kernel,
        out_shape=(shaped(blocks, rows, lanes),) * 2 + (shaped(blocks, planes, quarter, lanes),),
        in_specs=[HBM, VMEM],
        out_specs=(VMEM,) * 3,
        scratch_shapes=[pltpu.SemaphoreType.DMA((3, blocks))],
        compiler_params=params(),
        cost_estimate=cost(),
    )(pltpu.with_memory_space_constraint(field, pltpu.HBM), packed[0])
    low = lax.ppermute(top, "mesh", [(j, j + 1) for j in range(mesh_count - 1)])
    high = lax.ppermute(bottom, "mesh", [(j + 1, j) for j in range(mesh_count - 1)])

    split = (local_inst, variables)
    own, *theirs = (x.reshape(*split, planes, quarter, lanes) for x in (own, *gathered))
    all_quarters = (own, *in_hbm(*theirs))

    whole = shaped(*field.shape)
    at_once = 2
    slab = pl.BlockSpec((at_once, planes, rows, lanes), lambda b: (b, 0, 0, 0))
    plane = pl.BlockSpec((at_once, rows, lanes), lambda b: (b, 0, 0))
    pre_one, pre_two = pl.pallas_call(
        stencil_kernel,
        grid=(blocks // at_once,),
        out_shape=(
            pltpu.HBM((blocks, OUTER, rows, lanes), jnp.float32),
            shaped(blocks, planes - OUTER, rows, lanes),
        ),
        in_specs=[pl.BlockSpec((planes, rows, lanes), lambda b: (0, 0, 0)), plane, plane, slab],
        out_specs=(
            pl.BlockSpec((at_once, OUTER, rows, lanes), lambda b: (b, 0, 0, 0)),
            pl.BlockSpec((at_once, planes - OUTER, rows, lanes), lambda b: (b, 0, 0, 0)),
        ),
        compiler_params=params(),
        cost_estimate=cost(),
    )(nu, low, high, field)

    harmonics = pl.pallas_call(
        functools.partial(harmonics_kernel, total),
        out_shape=shaped(MODES, blocks * lanes),
        grid=(1,),
        in_specs=[
            SMEM,
            VMEM,
            pl.BlockSpec((blocks, planes, 8, lanes), lambda b: (0, 0, 0, 0)),
            pl.BlockSpec((blocks, planes, 8, lanes), lambda b: (0, 0, rows // 8 - 1, 0)),
        ],
        out_specs=pl.BlockSpec((MODES, blocks * lanes), lambda b: (0, 0)),
        compiler_params=params(),
        cost_estimate=cost(),
    )(mode_orders, packed[0], field, field)

    def crossing(flip):
        return [
            (r * mesh_count + m, (1 - r) * mesh_count + (m ^ flip))
            for r in range(2)
            for m in range(mesh_count)
        ]

    def doubled(x, flip):
        return x + lax.ppermute(x, "mesh", [(m, m ^ flip) for m in range(mesh_count)])

    two_ways = [lax.ppermute(harmonics, ("row", "mesh"), crossing(flip)) for flip in (0, 1)]
    harmonics = two_ways[0] + two_ways[1]
    early = lax.ppermute(harmonics, "mesh", [(m, m ^ 2) for m in range(mesh_count)])

    def sources(start, size, rims, after=()):
        at_once = 3
        pieces_in = [
            pl.BlockSpec(
                (2, at_once, 1, quarter, lanes),
                functools.partial(lambda plane, b: (0, b, plane, 0, 0), start + p),
            )
            for _ in range(4)
            for p in range(size)
        ]
        rim_specs = [
            pl.BlockSpec((INST, at_once, quarter, lanes), lambda b: (0, b, 0, 0)),
            pl.BlockSpec((planes, rows, lanes), lambda b: (0, 0, 0)),
        ]
        count = 4 if rims else 1

        def kernel(*refs):
            inputs, outputs = refs[: -count - len(after)], refs[-count:]
            source_kernel(bool(rims), *inputs, *outputs)

        if not rims:
            out_shape = (pltpu.HBM((4, *split, size, quarter, lanes), jnp.float32),)
            out_specs = (
                pl.BlockSpec((4, 2, at_once, size, quarter, lanes), lambda b: (0, 0, b, 0, 0, 0)),
            )
        else:
            out_shape = (pltpu.HBM((*split, size, quarter, lanes), jnp.float32),) * 4
            out_specs = (
                pl.BlockSpec((2, at_once, size, quarter, lanes), lambda b: (0, b, 0, 0, 0)),
            ) * 4
        outs = pl.pallas_call(
            kernel,
            out_shape=out_shape,
            grid=(variables // at_once,),
            in_specs=[SMEM] + pieces_in + rim_specs[: len(rims)] + [ANY] * len(after),
            out_specs=out_specs,
            compiler_params=params(),
            cost_estimate=cost(),
        )(ratio[None], *(x for x in all_quarters for _ in range(size)), *rims, *after)
        if not rims:
            out = outs[0].reshape(4, blocks, size, quarter, lanes)
            return (lax.all_to_all(out, "inst", split_axis=0, concat_axis=0, tiled=True), out)
        own, up, down, far = (x.reshape(blocks, size, quarter, lanes) for x in outs)
        return (own, *exchange(up, down, far))

    one_source = sources(0, OUTER, (), after=(*in_hbm(pre_one), early))

    weights = lag_weights(jnp.where(first, -ratio, ratio))
    turn = jnp.where(first, angle, -angle)
    ghost_shape = shaped(INST, variables, quarter, lanes)

    outermost = pl.BlockSpec((2, variables, 2, quarter, lanes), lambda b: (0, 0, 3, 0, 0))
    ghost_out = pl.pallas_call(
        mix_kernel,
        out_shape=ghost_shape,
        grid=(1,),
        in_specs=[SMEM] + [outermost] * 4 + [ANY],
        out_specs=pl.BlockSpec(ghost_shape.shape, lambda b: (0, 0, 0, 0)),
        compiler_params=params(),
        cost_estimate=cost(),
    )(
        jnp.concatenate([weights, jnp.stack([jnp.cos(turn), jnp.sin(turn)])]),
        *all_quarters,
        *in_hbm(one_source[1]),
    )
    ghost = lax.ppermute(ghost_out, "mesh", [(mesh_count - 1, 0), (0, mesh_count - 1)])

    two_source = sources(OUTER, planes - OUTER, (ghost, nu))

    harmonics = pl.pallas_call(
        add_kernel,
        out_shape=harmonics,
        in_specs=[VMEM, VMEM, ANY],
        out_specs=VMEM,
        compiler_params=params(),
        cost_estimate=cost(),
    )(harmonics, early, ghost_out)
    harmonics = doubled(harmonics, 4)
    edge = pl.pallas_call(
        functools.partial(edge_kernel, total),
        out_shape=shaped(planes, blocks, 8, lanes),
        in_specs=[SMEM, VMEM, VMEM, VMEM],
        out_specs=VMEM,
        compiler_params=params(),
        cost_estimate=cost(),
    )(
        mode_orders,
        harmonics,
        lax.ppermute(harmonics, "mesh", [(m, m ^ 8) for m in range(mesh_count)]),
        nu,
    )

    inverse = jnp.asarray(inverse_parts(rows))
    kept = ()
    for start, size, group, pre in ((0, OUTER, one_source[:1], pre_one), (OUTER, planes - OUTER, two_source, pre_two)):
        given = 4 + len(group)
        streamed = size == OUTER
        kept = pl.pallas_call(
            functools.partial(final_kernel, start, streamed),
            out_shape=(pltpu.HBM(field.shape, jnp.float32),) * 2,
            in_specs=[VMEM] * 3
            + [HBM if streamed else VMEM]
            + [VMEM] * len(group)
            + [HBM] * len(kept),
            out_specs=(HBM,) * 2,
            scratch_shapes=[pltpu.VMEM((blocks, size, rows, lanes), jnp.float32)] * 2
            + [pltpu.SemaphoreType.DMA((4 * blocks,))]
            + [
                pltpu.VMEM((blocks, size, rows, lanes), jnp.float32),
                pltpu.SemaphoreType.DMA((blocks,)),
            ][: 2 * streamed],
            input_output_aliases={given: 0, given + 1: 1} if kept else {},
            compiler_params=params(),
            cost_estimate=cost(),
        )(inverse, edge, field, *(in_hbm(pre) if streamed else [pre]), *group, *kept)
    new, residual = kept
    return (new.reshape(state.shape), residual.reshape(state.shape))


def solution(mesh):
    spread = P("row", "inst", None, "mesh", None, None)
    return jax.shard_map(
        local,
        mesh=mesh,
        in_specs=(spread, P("row", "mesh", None, None), P(), P()),
        out_specs=(spread, spread),
        check_vma=False,
    )
```

```python
import functools
import math

import numpy as np

import jax
import jax.numpy as jnp
from jax import lax
from jax.experimental import pallas as pl
from jax.experimental.pallas import tpu as pltpu
from jax.sharding import PartitionSpec as P

INST = 8
OUTER = 6
MODES = 24
LIMIT = 14 * 1024 * 1024
VMEM = pl.BlockSpec(memory_space=pltpu.VMEM)
SMEM = pl.BlockSpec(memory_space=pltpu.SMEM)
ANY = pl.BlockSpec(memory_space=pl.ANY)
HBM = pl.BlockSpec(memory_space=pltpu.HBM)
D1 = -0.5 / math.tan(math.pi / 8)
D2 = 0.5 / math.tan(math.pi / 4)
D3 = -0.5 / math.tan(3 * math.pi / 8)


def shaped(*dims):
    return jax.ShapeDtypeStruct(dims, jnp.float32)


def cost():
    return pl.CostEstimate(flops=1, bytes_accessed=1, transcendentals=0)


def inverse_parts(length):
    steps = np.arange(1, length + 1).astype(np.float64)
    basis = math.sqrt(2.0 / (length + 1)) * np.sin(
        math.pi * steps[:, None] * steps[None, :] / (length + 1)
    )
    eigen = 2.0 - np.cos(math.pi * steps / (length + 1))
    inverse = (0.2 * (basis / eigen[None, :]) @ basis.T).astype(np.float32)
    high = inverse.astype(jnp.bfloat16)
    low = (inverse - high.astype(np.float32)).astype(jnp.bfloat16)
    return np.concatenate([high, low, high], axis=1)


def split_bf16(x):
    high = x.astype(jnp.bfloat16)
    return high, (x - high.astype(jnp.float32)).astype(jnp.bfloat16)


def params():
    return pltpu.CompilerParams(vmem_limit_bytes=LIMIT)


def pack_kernel(planes, field, *rest):
    sems = rest[-1]
    copies = []

    def copy(source, target):
        one = pltpu.make_async_copy(source, target, sems.at[len(copies)])
        one.start()
        copies.append(one)

    outs = rest[:3]
    for k, out in zip((1, 3, 2), outs):
        place = lax.rem(lax.axis_index("inst") + k, 4) * 16
        rows = pl.ds(pl.multiple_of(place, 16), 16)
        done = 0
        for start, size in planes:
            for b in range(0, field.shape[0], 4):
                copy(
                    field.at[b : b + 4, start : start + size, rows, :],
                    out.at[b : b + 4, done : done + size],
                )
            done += size
    for one in copies:
        one.wait()


def edges_kernel(field, after, top, bottom, own, sems):
    rows = pl.ds(pl.multiple_of(lax.axis_index("inst") * 16, 16), 16)
    copies = [
        pltpu.make_async_copy(field.at[b, plane], out.at[b], sems.at[k, b])
        for k, (plane, out) in enumerate(((field.shape[1] - 1, top), (0, bottom)))
        for b in range(field.shape[0])
    ]
    last = field.shape[1] - 1
    copies.append(
        pltpu.make_async_copy(field.at[:, 1:, rows, :], own.at[:, :last], sems.at[2, 0])
    )
    copies.append(
        pltpu.make_async_copy(field.at[:, :1, rows, :], own.at[:, last:], sems.at[2, 1])
    )
    for one in copies:
        one.start()
    for one in copies:
        one.wait()


def pack(field, planes):
    blocks, _, rows, lanes = field.shape
    size = sum(size for _, size in planes)
    return pl.pallas_call(
        functools.partial(pack_kernel, planes),
        out_shape=(shaped(blocks, size, rows // 4, lanes),) * 3,
        in_specs=[HBM],
        out_specs=(VMEM,) * 3,
        scratch_shapes=[pltpu.SemaphoreType.DMA((32,))],
        compiler_params=params(),
        cost_estimate=cost(),
    )(pltpu.with_memory_space_constraint(field, pltpu.HBM))


def turns(position, mode, orders, total):
    order = jnp.zeros(mode.shape, jnp.int32)
    count = orders.shape[0]
    for j in range(count):
        order = jnp.where((mode == 1 + j) | (mode == 1 + count + j), orders[j], order)
    phase = lax.rem(position * order, total).astype(jnp.float32) * (2.0 * math.pi / total)
    value = jnp.where(mode <= count, jnp.cos(phase), jnp.sin(phase))
    return jnp.where(mode <= 2 * count, value, 0.0)


def harmonics_kernel(total, orders, after, front, back, out):
    blocks, planes, _, lanes = front.shape
    mode = lax.broadcasted_iota(jnp.int32, (MODES, planes), 0)
    position = lax.broadcasted_iota(jnp.int32, (MODES, planes), 1) + lax.axis_index("mesh") * planes
    basis = turns(position, mode, orders, total) * jnp.where(mode == 0, 1.0 / total, 2.0 / total)
    rotor = lax.axis_index("row") == 0
    for b in range(blocks):
        edge = jnp.where(rotor, back[b, :, 7, :], front[b, :, 0, :])
        out[:, b * lanes : (b + 1) * lanes] = jnp.dot(
            basis, edge, precision=lax.Precision.HIGHEST, preferred_element_type=jnp.float32
        )


def mix_kernel(scalars, own, up, down, far, after, out):
    weight = [scalars[k] for k in range(INST)]
    cosine, sine = scalars[INST], scalars[INST + 1]
    at = jnp.where(lax.axis_index("mesh") == 0, 1, 0)

    def mixed(var):
        u = [r[s, var, at] for r in (own, up, far, down) for s in range(2)]
        sums = []
        for a in range(INST):
            total = weight[a % INST] * u[0]
            for b in range(1, INST):
                total = total + weight[(a - b) % INST] * u[b]
            sums.append(total)
        return sums

    for var in (0, 1, 4, 5):
        for a, value in enumerate(mixed(var)):
            out[a, var] = value
    v, w = mixed(2), mixed(3)
    for a in range(INST):
        out[a, 2] = cosine * v[a] - sine * w[a]
        out[a, 3] = sine * v[a] + cosine * w[a]


def source_kernel(rims, scalars, *refs):
    if rims:
        outs, refs = refs[-4:], refs[:-4]
    else:
        outs, refs = refs[-1:], refs[:-1]
    if rims:
        ghost, nu = refs[-2:]
        refs = refs[:-2]
    size = len(refs) // 4
    own, up, down, far = (refs[k * size : (k + 1) * size] for k in range(4))
    ratio = scalars[0]
    c1, c2, c3 = (ratio * D1, ratio * D2, ratio * D3)
    if rims:
        out_own, out_up, out_down, out_far = outs
        order = (out_own, out_up, out_far, out_down)
    else:
        inst = lax.axis_index("inst")
        order = [outs[0].at[lax.rem(inst + k, 4)] for k in range(4)]
    for var in range(up[0].shape[1]):
        for p in range(size):
            u = [own[p][s, var, 0] for s in range(2)]
            u += [r[p][s, var, 0] for r in (up, far, down) for s in range(2)]
            near = [u[(n - 1) % INST] - u[(n + 1) % INST] for n in range(INST)]
            second = [c2 * (u[(n - 2) % INST] - u[(n + 2) % INST]) for n in range(4)]
            for n in range(INST):
                s = c1 * near[n] - c3 * near[(n + 4) % INST]
                s = s + second[n] if n < 4 else s - second[n - 4]
                order[n // 2][n % 2, var, p] = s
    if not rims:
        return

    def add_ghost(p, factor):
        for var in range(up[0].shape[1]):
            for n in range(INST):
                at = (n % 2, var, p)
                order[n // 2][at] = order[n // 2][at] - factor * ghost[n, var]

    place = pl.ds(pl.multiple_of(lax.axis_index("inst") * 16, 16), 16)

    @pl.when(lax.axis_index("mesh") == 0)
    def _():
        add_ghost(size - 1, nu[0, place, :] + 0.5)

    @pl.when(lax.axis_index("mesh") == lax.axis_size("mesh") - 1)
    def _():
        add_ghost(size - 2, nu[nu.shape[0] - 1, place, :])


def stencil_kernel(nu, low, high, field, one, two):
    blocks, planes, rows, lanes = field.shape
    lane = lax.broadcasted_iota(jnp.int32, (rows, lanes), 1)
    row = lax.broadcasted_iota(jnp.int32, (rows, lanes), 0)
    for b in range(blocks):
        for p in range(planes):
            u = field[b, p]
            before = low[b] if p == 0 else field[b, p - 1]
            after = high[b] if p == planes - 1 else field[b, p + 1]
            left = jnp.where(lane == 0, 0.0, pltpu.roll(u, 1, 1))
            right = jnp.where(lane == lanes - 1, 0.0, pltpu.roll(u, lanes - 1, 1))
            above = jnp.where(row == 0, 0.0, pltpu.roll(u, 1, 0))
            below = jnp.where(row == rows - 1, 0.0, pltpu.roll(u, rows - 1, 0))
            lap = (before + after) + (above + below) + (left + right) - 6.0 * u
            at = (p - 1) % planes
            out, at = (one, at) if at < OUTER else (two, at - OUTER)
            out[b, at] = nu[p] * lap - (u - above) - 0.5 * (u - before)


def add_kernel(one, two, after, out):
    out[...] = one[...] + two[...]


def edge_kernel(total, orders, one, two, nu, out):
    planes, blocks, rows, lanes = out.shape
    mode = lax.broadcasted_iota(jnp.int32, (planes, MODES), 1)
    position = lax.broadcasted_iota(jnp.int32, (planes, MODES), 0) + lax.axis_index("mesh") * planes
    ghost = jnp.dot(
        turns(position, mode, orders, total),
        one[...] + two[...],
        precision=lax.Precision.HIGHEST,
        preferred_element_type=jnp.float32,
    )
    rotor = lax.axis_index("row") == 0
    hit = lax.broadcasted_iota(jnp.int32, (rows, lanes), 0) == jnp.where(rotor, rows - 1, 0)
    for p in range(planes):
        facing = jnp.where(rotor, nu[p, nu.shape[1] - 1 :, :], nu[p, :1, :] + 1.0)
        for b in range(blocks):
            value = facing * ghost[p : p + 1, b * lanes : (b + 1) * lanes]
            out[p, b] = jnp.where(hit, value, 0.0)


def final_kernel(start, streamed, inverse, edge, field, pre, *rest):
    new, residual, new_held, residual_held, held_in, pieces, sems_in, sems = rest[-8:]
    count, planes, rows, lanes = field.shape
    size = held_in.shape[1]
    base = (start + 1) % planes
    inst = lax.axis_index("inst")
    arrivals = []
    for b in range(count):
        if streamed:
            pairs = [(pre.at[b], held_in.at[b]), (rest[0].at[:, b], pieces.at[b])]
        else:
            pairs = [(pre.at[b], held_in.at[b])]
            pairs += [
                (rest[k].at[b], pieces.at[b, lax.rem(inst + step, 4)])
                for k, step in enumerate((0, 1, 3, 2))
            ]
        arrivals.append(
            [pltpu.make_async_copy(x, y, sems_in.at[b, k]) for k, (x, y) in enumerate(pairs)]
        )
        for one in arrivals[-1]:
            one.start()
    tile = pl.ds(pl.multiple_of((1 - lax.axis_index("row")) * (rows - 8), 8), 8)
    runs = [(0, base, min(size, planes - base))]
    if base + size > planes:
        runs.append((planes - base, 0, base + size - planes))
    copies = []
    for j in range(0, count, 2):
        for one in arrivals[j] + arrivals[j + 1]:
            one.wait()
        for p in range(size):
            plane = (base + p) % planes
            for b in (j, j + 1):
                for k in range(4):
                    at = pl.ds(16 * k, 16)
                    residual_held[b, p, at] = held_in[b, p, at] - pieces[b, k, p]
                residual_held[b, p, tile] = residual_held[b, p, tile] + edge[plane, b]
            high, low = split_bf16(
                jnp.concatenate([residual_held[j, p], residual_held[j + 1, p]], 1)
            )
            change = jnp.dot(
                inverse[...],
                jnp.concatenate([high, high, low], 0),
                preferred_element_type=jnp.float32,
            )
            new_held[j, p] = field[j, plane] + change[:, :lanes]
            new_held[j + 1, p] = field[j + 1, plane] + change[:, lanes:]
        for b in (j, j + 1):
            for held, out in ((residual_held, residual), (new_held, new)):
                for source, target, length in runs:
                    copies.append(
                        pltpu.make_async_copy(
                            held.at[b, source : source + length],
                            out.at[b, target : target + length],
                            sems.at[len(copies)],
                        )
                    )
                    copies[-1].start()
    for one in copies:
        one.wait()


def lag_weights(lag):
    delta = jnp.arange(INST).astype(jnp.float32) - lag
    total = 1.0 + jnp.cos(math.pi * delta)
    for k in range(1, INST // 2):
        total = total + 2.0 * jnp.cos(2.0 * math.pi * k / INST * delta)
    return total / INST


def local(state, viscosity, blade_counts, mode_orders):
    _, local_inst, variables, planes, rows, lanes = state.shape
    quarter = rows // 4
    blocks = local_inst * variables
    mesh_count = lax.axis_size("mesh")
    total = planes * mesh_count
    which = lax.axis_index("row")
    inst = lax.axis_index("inst")
    mesh_idx = lax.axis_index("mesh")
    counts = blade_counts.astype(jnp.float32)
    ratio = counts[1 - which] / counts[which]
    angle = 2.0 * math.pi / counts[which]
    field = state.reshape(blocks, planes, rows, lanes)
    nu = viscosity[0]
    first = mesh_idx == 0
    last = mesh_idx == mesh_count - 1

    def along(x, step):
        return lax.ppermute(x, "inst", [(j, (j + step) % 4) for j in range(4)])

    def in_hbm(*arrays):
        return [pltpu.with_memory_space_constraint(x, pltpu.HBM) for x in arrays]

    def exchange(up, down, far):
        from_down, from_up, from_far = along(up, 1), along(down, 3), along(far, 2)
        return from_up, from_down, from_far

    packed = pack(field, ((1, planes - 1), (0, 1)))
    gathered = exchange(*packed)

    top, bottom, own = pl.pallas_call(
        edges_kernel,
        out_shape=(shaped(blocks, rows, lanes),) * 2 + (shaped(blocks, planes, quarter, lanes),),
        in_specs=[HBM, VMEM],
        out_specs=(VMEM,) * 3,
        scratch_shapes=[pltpu.SemaphoreType.DMA((3, blocks))],
        compiler_params=params(),
        cost_estimate=cost(),
    )(pltpu.with_memory_space_constraint(field, pltpu.HBM), packed[0])
    low = lax.ppermute(top, "mesh", [(j, j + 1) for j in range(mesh_count - 1)])
    high = lax.ppermute(bottom, "mesh", [(j + 1, j) for j in range(mesh_count - 1)])

    split = (local_inst, variables)
    all_quarters = in_hbm(*(x.reshape(*split, planes, quarter, lanes) for x in (own, *gathered)))

    whole = shaped(*field.shape)
    at_once = 2
    slab = pl.BlockSpec((at_once, planes, rows, lanes), lambda b: (b, 0, 0, 0))
    plane = pl.BlockSpec((at_once, rows, lanes), lambda b: (b, 0, 0))
    pre_one, pre_two = pl.pallas_call(
        stencil_kernel,
        grid=(blocks // at_once,),
        out_shape=(
            pltpu.HBM((blocks, OUTER, rows, lanes), jnp.float32),
            pltpu.HBM((blocks, planes - OUTER, rows, lanes), jnp.float32),
        ),
        in_specs=[pl.BlockSpec((planes, rows, lanes), lambda b: (0, 0, 0)), plane, plane, slab],
        out_specs=(
            pl.BlockSpec((at_once, OUTER, rows, lanes), lambda b: (b, 0, 0, 0)),
            pl.BlockSpec((at_once, planes - OUTER, rows, lanes), lambda b: (b, 0, 0, 0)),
        ),
        compiler_params=params(),
        cost_estimate=cost(),
    )(nu, *in_hbm(low, high), field)

    harmonics = pl.pallas_call(
        functools.partial(harmonics_kernel, total),
        out_shape=shaped(MODES, blocks * lanes),
        grid=(1,),
        in_specs=[
            SMEM,
            VMEM,
            pl.BlockSpec((blocks, planes, 8, lanes), lambda b: (0, 0, 0, 0)),
            pl.BlockSpec((blocks, planes, 8, lanes), lambda b: (0, 0, rows // 8 - 1, 0)),
        ],
        out_specs=pl.BlockSpec((MODES, blocks * lanes), lambda b: (0, 0)),
        compiler_params=params(),
        cost_estimate=cost(),
    )(mode_orders, packed[0], field, field)

    def crossing(flip):
        return [
            (r * mesh_count + m, (1 - r) * mesh_count + (m ^ flip))
            for r in range(2)
            for m in range(mesh_count)
        ]

    def doubled(x, flip):
        return x + lax.ppermute(x, "mesh", [(m, m ^ flip) for m in range(mesh_count)])

    two_ways = [lax.ppermute(harmonics, ("row", "mesh"), crossing(flip)) for flip in (0, 1)]
    harmonics = two_ways[0] + two_ways[1]
    early = lax.ppermute(harmonics, "mesh", [(m, m ^ 2) for m in range(mesh_count)])

    def sources(start, size, rims, after=()):
        at_once = 3
        pieces_in = [
            pl.BlockSpec(
                (2, at_once, 1, quarter, lanes),
                functools.partial(lambda plane, b: (0, b, plane, 0, 0), start + p),
            )
            for _ in range(4)
            for p in range(size)
        ]
        rim_specs = [
            pl.BlockSpec((INST, at_once, quarter, lanes), lambda b: (0, b, 0, 0)),
            pl.BlockSpec((planes, rows, lanes), lambda b: (0, 0, 0)),
        ]
        count = 4 if rims else 1

        def kernel(*refs):
            inputs, outputs = refs[: -count - len(after)], refs[-count:]
            source_kernel(bool(rims), *inputs, *outputs)

        if not rims:
            out_shape = (pltpu.HBM((4, *split, size, quarter, lanes), jnp.float32),)
            out_specs = (
                pl.BlockSpec((4, 2, at_once, size, quarter, lanes), lambda b: (0, 0, b, 0, 0, 0)),
            )
        else:
            out_shape = (pltpu.HBM((*split, size, quarter, lanes), jnp.float32),) * 4
            out_specs = (
                pl.BlockSpec((2, at_once, size, quarter, lanes), lambda b: (0, b, 0, 0, 0)),
            ) * 4
        outs = pl.pallas_call(
            kernel,
            out_shape=out_shape,
            grid=(variables // at_once,),
            in_specs=[SMEM] + pieces_in + rim_specs[: len(rims)] + [ANY] * len(after),
            out_specs=out_specs,
            compiler_params=params(),
            cost_estimate=cost(),
        )(ratio[None], *(x for x in all_quarters for _ in range(size)), *rims, *after)
        if not rims:
            out = outs[0].reshape(4, blocks, size, quarter, lanes)
            return (lax.all_to_all(out, "inst", split_axis=0, concat_axis=0, tiled=True), out)
        own, up, down, far = (x.reshape(blocks, size, quarter, lanes) for x in outs)
        return (own, *exchange(up, down, far))

    one_source = sources(0, OUTER, (), after=(*in_hbm(pre_one), early))

    weights = lag_weights(jnp.where(first, -ratio, ratio))
    turn = jnp.where(first, angle, -angle)
    ghost_shape = shaped(INST, variables, quarter, lanes)

    outermost = pl.BlockSpec((2, variables, 2, quarter, lanes), lambda b: (0, 0, 3, 0, 0))
    ghost_out = pl.pallas_call(
        mix_kernel,
        out_shape=ghost_shape,
        grid=(1,),
        in_specs=[SMEM] + [outermost] * 4 + [ANY],
        out_specs=pl.BlockSpec(ghost_shape.shape, lambda b: (0, 0, 0, 0)),
        compiler_params=params(),
        cost_estimate=cost(),
    )(
        jnp.concatenate([weights, jnp.stack([jnp.cos(turn), jnp.sin(turn)])]),
        *all_quarters,
        *in_hbm(one_source[1]),
    )
    ghost = lax.ppermute(ghost_out, "mesh", [(mesh_count - 1, 0), (0, mesh_count - 1)])

    harmonics = pl.pallas_call(
        add_kernel,
        out_shape=harmonics,
        in_specs=[VMEM, VMEM, ANY],
        out_specs=VMEM,
        compiler_params=params(),
        cost_estimate=cost(),
    )(harmonics, early, ghost_out)
    harmonics = doubled(harmonics, 4)
    opposite = lax.ppermute(harmonics, "mesh", [(m, m ^ 8) for m in range(mesh_count)])
    two_source = sources(OUTER, planes - OUTER, (ghost, nu), after=(opposite,))

    edge = pl.pallas_call(
        functools.partial(edge_kernel, total),
        out_shape=shaped(planes, blocks, 8, lanes),
        in_specs=[SMEM, VMEM, VMEM, VMEM],
        out_specs=VMEM,
        compiler_params=params(),
        cost_estimate=cost(),
    )(
        mode_orders,
        harmonics,
        opposite,
        nu,
    )

    inverse = jnp.asarray(inverse_parts(rows))
    kept = ()
    for start, size, group, pre in ((0, OUTER, one_source[:1], pre_one), (OUTER, planes - OUTER, two_source, pre_two)):
        given = 4 + len(group)
        streamed = size == OUTER
        kept = pl.pallas_call(
            functools.partial(final_kernel, start, streamed),
            out_shape=(pltpu.HBM(field.shape, jnp.float32),) * 2,
            in_specs=[VMEM] * 3 + [HBM] * (1 + len(group) + len(kept)),
            out_specs=(HBM,) * 2,
            scratch_shapes=[pltpu.VMEM((blocks, size, rows, lanes), jnp.float32)] * 3
            + [
                pltpu.VMEM((blocks, 4, size, quarter, lanes), jnp.float32),
                pltpu.SemaphoreType.DMA((blocks, 5)),
                pltpu.SemaphoreType.DMA((4 * blocks,)),
            ],
            input_output_aliases={given: 0, given + 1: 1} if kept else {},
            compiler_params=params(),
            cost_estimate=cost(),
        )(inverse, edge, field, *in_hbm(pre, *group), *kept)
    new, residual = kept
    return (new.reshape(state.shape), residual.reshape(state.shape))


def solution(mesh):
    spread = P("row", "inst", None, "mesh", None, None)
    return jax.shard_map(
        local,
        mesh=mesh,
        in_specs=(spread, P("row", "mesh", None, None), P(), P()),
        out_specs=(spread, spread),
        check_vma=False,
    )
```

```python
import functools
import math

import numpy as np

import jax
import jax.numpy as jnp
from jax import lax
from jax.experimental import pallas as pl
from jax.experimental.pallas import tpu as pltpu
from jax.sharding import PartitionSpec as P

INST = 8
OUTER = 6
MODES = 24
LIMIT = 14 * 1024 * 1024
VMEM = pl.BlockSpec(memory_space=pltpu.VMEM)
SMEM = pl.BlockSpec(memory_space=pltpu.SMEM)
ANY = pl.BlockSpec(memory_space=pl.ANY)
HBM = pl.BlockSpec(memory_space=pltpu.HBM)
D1 = -0.5 / math.tan(math.pi / 8)
D2 = 0.5 / math.tan(math.pi / 4)
D3 = -0.5 / math.tan(3 * math.pi / 8)


def shaped(*dims):
    return jax.ShapeDtypeStruct(dims, jnp.float32)


def cost():
    return pl.CostEstimate(flops=1, bytes_accessed=1, transcendentals=0)


def inverse_parts(length):
    steps = np.arange(1, length + 1).astype(np.float64)
    basis = math.sqrt(2.0 / (length + 1)) * np.sin(
        math.pi * steps[:, None] * steps[None, :] / (length + 1)
    )
    eigen = 2.0 - np.cos(math.pi * steps / (length + 1))
    inverse = (0.2 * (basis / eigen[None, :]) @ basis.T).astype(np.float32)
    high = inverse.astype(jnp.bfloat16)
    low = (inverse - high.astype(np.float32)).astype(jnp.bfloat16)
    return np.concatenate([high, low, high], axis=1)


def split_bf16(x):
    high = x.astype(jnp.bfloat16)
    return high, (x - high.astype(jnp.float32)).astype(jnp.bfloat16)


def params():
    return pltpu.CompilerParams(vmem_limit_bytes=LIMIT)


def pack_kernel(planes, field, *rest):
    sems = rest[-1]
    copies = []

    def copy(source, target):
        one = pltpu.make_async_copy(source, target, sems.at[len(copies)])
        one.start()
        copies.append(one)

    outs = rest[:3]
    for k, out in zip((1, 3, 2), outs):
        place = lax.rem(lax.axis_index("inst") + k, 4) * 16
        rows = pl.ds(pl.multiple_of(place, 16), 16)
        done = 0
        for start, size in planes:
            for b in range(0, field.shape[0], 4):
                copy(
                    field.at[b : b + 4, start : start + size, rows, :],
                    out.at[b : b + 4, done : done + size],
                )
            done += size
    for one in copies:
        one.wait()


def edges_kernel(field, after, top, bottom, own, sems):
    rows = pl.ds(pl.multiple_of(lax.axis_index("inst") * 16, 16), 16)
    copies = [
        pltpu.make_async_copy(field.at[b, plane], out.at[b], sems.at[k, b])
        for k, (plane, out) in enumerate(((field.shape[1] - 1, top), (0, bottom)))
        for b in range(field.shape[0])
    ]
    last = field.shape[1] - 1
    copies.append(
        pltpu.make_async_copy(field.at[:, 1:, rows, :], own.at[:, :last], sems.at[2, 0])
    )
    copies.append(
        pltpu.make_async_copy(field.at[:, :1, rows, :], own.at[:, last:], sems.at[2, 1])
    )
    for one in copies:
        one.start()
    for one in copies:
        one.wait()


def pack(field, planes):
    blocks, _, rows, lanes = field.shape
    size = sum(size for _, size in planes)
    return pl.pallas_call(
        functools.partial(pack_kernel, planes),
        out_shape=(shaped(blocks, size, rows // 4, lanes),) * 3,
        in_specs=[HBM],
        out_specs=(VMEM,) * 3,
        scratch_shapes=[pltpu.SemaphoreType.DMA((32,))],
        compiler_params=params(),
        cost_estimate=cost(),
    )(pltpu.with_memory_space_constraint(field, pltpu.HBM))


def turns(position, mode, orders, total):
    order = jnp.zeros(mode.shape, jnp.int32)
    count = orders.shape[0]
    for j in range(count):
        order = jnp.where((mode == 1 + j) | (mode == 1 + count + j), orders[j], order)
    phase = lax.rem(position * order, total).astype(jnp.float32) * (2.0 * math.pi / total)
    value = jnp.where(mode <= count, jnp.cos(phase), jnp.sin(phase))
    return jnp.where(mode <= 2 * count, value, 0.0)


def harmonics_kernel(total, orders, after, front, back, out):
    blocks, planes, _, lanes = front.shape
    mode = lax.broadcasted_iota(jnp.int32, (MODES, planes), 0)
    position = lax.broadcasted_iota(jnp.int32, (MODES, planes), 1) + lax.axis_index("mesh") * planes
    basis = turns(position, mode, orders, total) * jnp.where(mode == 0, 1.0 / total, 2.0 / total)
    rotor = lax.axis_index("row") == 0
    for b in range(blocks):
        edge = jnp.where(rotor, back[b, :, 7, :], front[b, :, 0, :])
        out[:, b * lanes : (b + 1) * lanes] = jnp.dot(
            basis, edge, precision=lax.Precision.HIGHEST, preferred_element_type=jnp.float32
        )


def mix_kernel(scalars, own, up, down, far, after, out):
    weight = [scalars[k] for k in range(INST)]
    cosine, sine = scalars[INST], scalars[INST + 1]
    at = jnp.where(lax.axis_index("mesh") == 0, 1, 0)

    def mixed(var):
        u = [r[s, var, at] for r in (own, up, far, down) for s in range(2)]
        sums = []
        for a in range(INST):
            total = weight[a % INST] * u[0]
            for b in range(1, INST):
                total = total + weight[(a - b) % INST] * u[b]
            sums.append(total)
        return sums

    for var in (0, 1, 4, 5):
        for a, value in enumerate(mixed(var)):
            out[a, var] = value
    v, w = mixed(2), mixed(3)
    for a in range(INST):
        out[a, 2] = cosine * v[a] - sine * w[a]
        out[a, 3] = sine * v[a] + cosine * w[a]


def source_kernel(rims, scalars, *refs):
    outs, refs = refs[-4:], refs[:-4]
    if rims:
        ghost, nu = refs[-2:]
        refs = refs[:-2]
    size = len(refs) // 4
    own, up, down, far = (refs[k * size : (k + 1) * size] for k in range(4))
    ratio = scalars[0]
    c1, c2, c3 = (ratio * D1, ratio * D2, ratio * D3)
    out_own, out_up, out_down, out_far = outs
    order = (out_own, out_up, out_far, out_down)
    for var in range(up[0].shape[1]):
        for p in range(size):
            u = [own[p][s, var, 0] for s in range(2)]
            u += [r[p][s, var, 0] for r in (up, far, down) for s in range(2)]
            near = [u[(n - 1) % INST] - u[(n + 1) % INST] for n in range(INST)]
            second = [c2 * (u[(n - 2) % INST] - u[(n + 2) % INST]) for n in range(4)]
            for n in range(INST):
                s = c1 * near[n] - c3 * near[(n + 4) % INST]
                s = s + second[n] if n < 4 else s - second[n - 4]
                order[n // 2][n % 2, var, p] = s
    if not rims:
        return

    def add_ghost(p, factor):
        for var in range(up[0].shape[1]):
            for n in range(INST):
                at = (n % 2, var, p)
                order[n // 2][at] = order[n // 2][at] - factor * ghost[n, var]

    place = pl.ds(pl.multiple_of(lax.axis_index("inst") * 16, 16), 16)

    @pl.when(lax.axis_index("mesh") == 0)
    def _():
        add_ghost(size - 1, nu[0, place, :] + 0.5)

    @pl.when(lax.axis_index("mesh") == lax.axis_size("mesh") - 1)
    def _():
        add_ghost(size - 2, nu[nu.shape[0] - 1, place, :])


def stencil_kernel(nu, low, high, field, one, two):
    blocks, planes, rows, lanes = field.shape
    lane = lax.broadcasted_iota(jnp.int32, (rows, lanes), 1)
    row = lax.broadcasted_iota(jnp.int32, (rows, lanes), 0)
    for b in range(blocks):
        for p in range(planes):
            u = field[b, p]
            before = low[b] if p == 0 else field[b, p - 1]
            after = high[b] if p == planes - 1 else field[b, p + 1]
            left = jnp.where(lane == 0, 0.0, pltpu.roll(u, 1, 1))
            right = jnp.where(lane == lanes - 1, 0.0, pltpu.roll(u, lanes - 1, 1))
            above = jnp.where(row == 0, 0.0, pltpu.roll(u, 1, 0))
            below = jnp.where(row == rows - 1, 0.0, pltpu.roll(u, rows - 1, 0))
            lap = (before + after) + (above + below) + (left + right) - 6.0 * u
            at = (p - 1) % planes
            out, at = (one, at) if at < OUTER else (two, at - OUTER)
            out[b, at] = nu[p] * lap - (u - above) - 0.5 * (u - before)


def add_kernel(one, two, after, out):
    out[...] = one[...] + two[...]


def edge_kernel(total, orders, one, two, nu, after, out):
    planes, blocks, rows, lanes = out.shape
    mode = lax.broadcasted_iota(jnp.int32, (planes, MODES), 1)
    position = lax.broadcasted_iota(jnp.int32, (planes, MODES), 0) + lax.axis_index("mesh") * planes
    ghost = jnp.dot(
        turns(position, mode, orders, total),
        one[...] + two[...],
        precision=lax.Precision.HIGHEST,
        preferred_element_type=jnp.float32,
    )
    rotor = lax.axis_index("row") == 0
    hit = lax.broadcasted_iota(jnp.int32, (rows, lanes), 0) == jnp.where(rotor, rows - 1, 0)
    for p in range(planes):
        facing = jnp.where(rotor, nu[p, nu.shape[1] - 1 :, :], nu[p, :1, :] + 1.0)
        for b in range(blocks):
            value = facing * ghost[p : p + 1, b * lanes : (b + 1) * lanes]
            out[p, b] = jnp.where(hit, value, 0.0)


def final_kernel(start, inverse, edge, field, pre, *rest):
    new, residual, new_held, residual_held, held_in, pieces, sems_in, sems = rest[-8:]
    count, planes, rows, lanes = field.shape
    size = held_in.shape[1]
    base = (start + 1) % planes
    inst = lax.axis_index("inst")
    arrivals = []
    for b in range(count):
        pairs = [(pre.at[b], held_in.at[b])]
        pairs += [
            (rest[k].at[b], pieces.at[b, lax.rem(inst + step, 4)])
            for k, step in enumerate((0, 1, 3, 2))
        ]
        arrivals.append(
            [pltpu.make_async_copy(x, y, sems_in.at[b, k]) for k, (x, y) in enumerate(pairs)]
        )
        for one in arrivals[-1]:
            one.start()
    tile = pl.ds(pl.multiple_of((1 - lax.axis_index("row")) * (rows - 8), 8), 8)
    runs = [(0, base, min(size, planes - base))]
    if base + size > planes:
        runs.append((planes - base, 0, base + size - planes))
    copies = []
    for j in range(0, count, 2):
        for one in arrivals[j] + arrivals[j + 1]:
            one.wait()
        for p in range(size):
            plane = (base + p) % planes
            for b in (j, j + 1):
                for k in range(4):
                    at = pl.ds(16 * k, 16)
                    residual_held[b, p, at] = held_in[b, p, at] - pieces[b, k, p]
                residual_held[b, p, tile] = residual_held[b, p, tile] + edge[plane, b]
            high, low = split_bf16(
                jnp.concatenate([residual_held[j, p], residual_held[j + 1, p]], 1)
            )
            change = jnp.dot(
                inverse[...],
                jnp.concatenate([high, high, low], 0),
                preferred_element_type=jnp.float32,
            )
            new_held[j, p] = field[j, plane] + change[:, :lanes]
            new_held[j + 1, p] = field[j + 1, plane] + change[:, lanes:]
        for b in (j, j + 1):
            for held, out in ((residual_held, residual), (new_held, new)):
                for source, target, length in runs:
                    copies.append(
                        pltpu.make_async_copy(
                            held.at[b, source : source + length],
                            out.at[b, target : target + length],
                            sems.at[len(copies)],
                        )
                    )
                    copies[-1].start()
    for one in copies:
        one.wait()


def lag_weights(lag):
    delta = jnp.arange(INST).astype(jnp.float32) - lag
    total = 1.0 + jnp.cos(math.pi * delta)
    for k in range(1, INST // 2):
        total = total + 2.0 * jnp.cos(2.0 * math.pi * k / INST * delta)
    return total / INST


def local(state, viscosity, blade_counts, mode_orders):
    _, local_inst, variables, planes, rows, lanes = state.shape
    quarter = rows // 4
    blocks = local_inst * variables
    mesh_count = lax.axis_size("mesh")
    total = planes * mesh_count
    which = lax.axis_index("row")
    inst = lax.axis_index("inst")
    mesh_idx = lax.axis_index("mesh")
    counts = blade_counts.astype(jnp.float32)
    ratio = counts[1 - which] / counts[which]
    angle = 2.0 * math.pi / counts[which]
    field = state.reshape(blocks, planes, rows, lanes)
    nu = viscosity[0]
    first = mesh_idx == 0
    last = mesh_idx == mesh_count - 1

    def along(x, step):
        return lax.ppermute(x, "inst", [(j, (j + step) % 4) for j in range(4)])

    def in_hbm(*arrays):
        return [pltpu.with_memory_space_constraint(x, pltpu.HBM) for x in arrays]

    def exchange(up, down, far):
        from_down, from_up, from_far = along(up, 1), along(down, 3), along(far, 2)
        return from_up, from_down, from_far

    packed = pack(field, ((1, planes - 1), (0, 1)))
    gathered = exchange(*packed)

    top, bottom, own = pl.pallas_call(
        edges_kernel,
        out_shape=(shaped(blocks, rows, lanes),) * 2 + (shaped(blocks, planes, quarter, lanes),),
        in_specs=[HBM, VMEM],
        out_specs=(VMEM,) * 3,
        scratch_shapes=[pltpu.SemaphoreType.DMA((3, blocks))],
        compiler_params=params(),
        cost_estimate=cost(),
    )(pltpu.with_memory_space_constraint(field, pltpu.HBM), packed[0])
    low = lax.ppermute(top, "mesh", [(j, j + 1) for j in range(mesh_count - 1)])
    high = lax.ppermute(bottom, "mesh", [(j + 1, j) for j in range(mesh_count - 1)])

    split = (local_inst, variables)
    all_quarters = in_hbm(*(x.reshape(*split, planes, quarter, lanes) for x in (own, *gathered)))

    whole = shaped(*field.shape)
    at_once = 2
    slab = pl.BlockSpec((at_once, planes, rows, lanes), lambda b: (b, 0, 0, 0))
    plane = pl.BlockSpec((at_once, rows, lanes), lambda b: (b, 0, 0))
    pre_one, pre_two = pl.pallas_call(
        stencil_kernel,
        grid=(blocks // at_once,),
        out_shape=(
            pltpu.HBM((blocks, OUTER, rows, lanes), jnp.float32),
            pltpu.HBM((blocks, planes - OUTER, rows, lanes), jnp.float32),
        ),
        in_specs=[pl.BlockSpec((planes, rows, lanes), lambda b: (0, 0, 0)), plane, plane, slab],
        out_specs=(
            pl.BlockSpec((at_once, OUTER, rows, lanes), lambda b: (b, 0, 0, 0)),
            pl.BlockSpec((at_once, planes - OUTER, rows, lanes), lambda b: (b, 0, 0, 0)),
        ),
        compiler_params=params(),
        cost_estimate=cost(),
    )(nu, *in_hbm(low, high), field)

    harmonics = pl.pallas_call(
        functools.partial(harmonics_kernel, total),
        out_shape=shaped(MODES, blocks * lanes),
        grid=(1,),
        in_specs=[
            SMEM,
            VMEM,
            pl.BlockSpec((blocks, planes, 8, lanes), lambda b: (0, 0, 0, 0)),
            pl.BlockSpec((blocks, planes, 8, lanes), lambda b: (0, 0, rows // 8 - 1, 0)),
        ],
        out_specs=pl.BlockSpec((MODES, blocks * lanes), lambda b: (0, 0)),
        compiler_params=params(),
        cost_estimate=cost(),
    )(mode_orders, packed[0], field, field)

    def crossing(flip):
        return [
            (r * mesh_count + m, (1 - r) * mesh_count + (m ^ flip))
            for r in range(2)
            for m in range(mesh_count)
        ]

    def doubled(x, flip):
        return x + lax.ppermute(x, "mesh", [(m, m ^ flip) for m in range(mesh_count)])

    two_ways = [lax.ppermute(harmonics, ("row", "mesh"), crossing(flip)) for flip in (0, 1)]
    harmonics = two_ways[0] + two_ways[1]
    early = lax.ppermute(harmonics, "mesh", [(m, m ^ 2) for m in range(mesh_count)])

    def sources(start, size, rims, after=()):
        at_once = 3
        pieces_in = [
            pl.BlockSpec(
                (2, at_once, 1, quarter, lanes),
                functools.partial(lambda plane, b: (0, b, plane, 0, 0), start + p),
            )
            for _ in range(4)
            for p in range(size)
        ]
        rim_specs = [
            pl.BlockSpec((INST, at_once, quarter, lanes), lambda b: (0, b, 0, 0)),
            pl.BlockSpec((planes, rows, lanes), lambda b: (0, 0, 0)),
        ]
        def kernel(*refs):
            inputs, outputs = refs[: -4 - len(after)], refs[-4:]
            source_kernel(bool(rims), *inputs, *outputs)

        outs = pl.pallas_call(
            kernel,
            out_shape=(pltpu.HBM((*split, size, quarter, lanes), jnp.float32),) * 4,
            grid=(variables // at_once,),
            in_specs=[SMEM] + pieces_in + rim_specs[: len(rims)] + [ANY] * len(after),
            out_specs=(
                pl.BlockSpec((2, at_once, size, quarter, lanes), lambda b: (0, b, 0, 0, 0)),
            )
            * 4,
            compiler_params=params(),
            cost_estimate=cost(),
        )(ratio[None], *(x for x in all_quarters for _ in range(size)), *rims, *after)
        own, up, down, far = (x.reshape(blocks, size, quarter, lanes) for x in outs)
        return (own, *exchange(up, down, far))

    one_source = sources(0, OUTER, (), after=(*in_hbm(pre_one), early))

    weights = lag_weights(jnp.where(first, -ratio, ratio))
    turn = jnp.where(first, angle, -angle)
    ghost_shape = shaped(INST, variables, quarter, lanes)

    outermost = pl.BlockSpec((2, variables, 2, quarter, lanes), lambda b: (0, 0, 3, 0, 0))
    ghost_out = pl.pallas_call(
        mix_kernel,
        out_shape=ghost_shape,
        grid=(1,),
        in_specs=[SMEM] + [outermost] * 4 + [ANY],
        out_specs=pl.BlockSpec(ghost_shape.shape, lambda b: (0, 0, 0, 0)),
        compiler_params=params(),
        cost_estimate=cost(),
    )(
        jnp.concatenate([weights, jnp.stack([jnp.cos(turn), jnp.sin(turn)])]),
        *all_quarters,
        *in_hbm(one_source[0]),
    )
    ghost = lax.ppermute(ghost_out, "mesh", [(mesh_count - 1, 0), (0, mesh_count - 1)])

    harmonics = pl.pallas_call(
        add_kernel,
        out_shape=harmonics,
        in_specs=[VMEM, VMEM, ANY],
        out_specs=VMEM,
        compiler_params=params(),
        cost_estimate=cost(),
    )(harmonics, early, ghost_out)
    harmonics = doubled(harmonics, 4)
    opposite = lax.ppermute(harmonics, "mesh", [(m, m ^ 8) for m in range(mesh_count)])
    two_source = sources(OUTER, planes - OUTER, (ghost, nu), after=(opposite, *one_source[1:3]))

    edge = pl.pallas_call(
        functools.partial(edge_kernel, total),
        out_shape=shaped(planes, blocks, 8, lanes),
        in_specs=[SMEM, VMEM, VMEM, VMEM, ANY],
        out_specs=VMEM,
        compiler_params=params(),
        cost_estimate=cost(),
    )(
        mode_orders,
        harmonics,
        opposite,
        nu,
        one_source[3],
    )

    inverse = jnp.asarray(inverse_parts(rows))
    kept = ()
    for start, size, group, pre in ((0, OUTER, one_source, pre_one), (OUTER, planes - OUTER, two_source, pre_two)):
        given = 4 + len(group)
        kept = pl.pallas_call(
            functools.partial(final_kernel, start),
            out_shape=(pltpu.HBM(field.shape, jnp.float32),) * 2,
            in_specs=[VMEM] * 3 + [HBM] * 2 + [ANY] * 3 + [HBM] * len(kept),
            out_specs=(HBM,) * 2,
            scratch_shapes=[pltpu.VMEM((blocks, size, rows, lanes), jnp.float32)] * 3
            + [
                pltpu.VMEM((blocks, 4, size, quarter, lanes), jnp.float32),
                pltpu.SemaphoreType.DMA((blocks, 5)),
                pltpu.SemaphoreType.DMA((4 * blocks,)),
            ],
            input_output_aliases={given: 0, given + 1: 1} if kept else {},
            compiler_params=params(),
            cost_estimate=cost(),
        )(inverse, edge, field, *in_hbm(pre, group[0]), *group[1:], *kept)
    new, residual = kept
    return (new.reshape(state.shape), residual.reshape(state.shape))


def solution(mesh):
    spread = P("row", "inst", None, "mesh", None, None)
    return jax.shard_map(
        local,
        mesh=mesh,
        in_specs=(spread, P("row", "mesh", None, None), P(), P()),
        out_specs=(spread, spread),
        check_vma=False,
    )
```

```python
import functools
import math

import numpy as np

import jax
import jax.numpy as jnp
from jax import lax
from jax.experimental import pallas as pl
from jax.experimental.pallas import tpu as pltpu
from jax.sharding import PartitionSpec as P

INST = 8
OUTER = 6
MODES = 24
LIMIT = 14 * 1024 * 1024
VMEM = pl.BlockSpec(memory_space=pltpu.VMEM)
SMEM = pl.BlockSpec(memory_space=pltpu.SMEM)
ANY = pl.BlockSpec(memory_space=pl.ANY)
HBM = pl.BlockSpec(memory_space=pltpu.HBM)
D1 = -0.5 / math.tan(math.pi / 8)
D2 = 0.5 / math.tan(math.pi / 4)
D3 = -0.5 / math.tan(3 * math.pi / 8)


def shaped(*dims):
    return jax.ShapeDtypeStruct(dims, jnp.float32)


def cost():
    return pl.CostEstimate(flops=1, bytes_accessed=1, transcendentals=0)


def inverse_parts(length):
    steps = np.arange(1, length + 1).astype(np.float64)
    basis = math.sqrt(2.0 / (length + 1)) * np.sin(
        math.pi * steps[:, None] * steps[None, :] / (length + 1)
    )
    eigen = 2.0 - np.cos(math.pi * steps / (length + 1))
    inverse = (0.2 * (basis / eigen[None, :]) @ basis.T).astype(np.float32)
    high = inverse.astype(jnp.bfloat16)
    low = (inverse - high.astype(np.float32)).astype(jnp.bfloat16)
    return np.concatenate([high, low, high], axis=1)


def split_bf16(x):
    high = x.astype(jnp.bfloat16)
    return high, (x - high.astype(jnp.float32)).astype(jnp.bfloat16)


def params():
    return pltpu.CompilerParams(vmem_limit_bytes=LIMIT)


def pack_kernel(planes, field, *rest):
    sems = rest[-1]
    copies = []

    def copy(source, target):
        one = pltpu.make_async_copy(source, target, sems.at[len(copies)])
        one.start()
        copies.append(one)

    outs = rest[:3]
    for k, out in zip((1, 3, 2), outs):
        place = lax.rem(lax.axis_index("inst") + k, 4) * 16
        rows = pl.ds(pl.multiple_of(place, 16), 16)
        done = 0
        for start, size in planes:
            for b in range(0, field.shape[0], 4):
                copy(
                    field.at[b : b + 4, start : start + size, rows, :],
                    out.at[b : b + 4, done : done + size],
                )
            done += size
    for one in copies:
        one.wait()


def edges_kernel(field, after, top, bottom, own, sems):
    rows = pl.ds(pl.multiple_of(lax.axis_index("inst") * 16, 16), 16)
    copies = [
        pltpu.make_async_copy(field.at[b, plane], out.at[b], sems.at[k, b])
        for k, (plane, out) in enumerate(((field.shape[1] - 1, top), (0, bottom)))
        for b in range(field.shape[0])
    ]
    last = field.shape[1] - 1
    copies.append(
        pltpu.make_async_copy(field.at[:, 1:, rows, :], own.at[:, :last], sems.at[2, 0])
    )
    copies.append(
        pltpu.make_async_copy(field.at[:, :1, rows, :], own.at[:, last:], sems.at[2, 1])
    )
    for one in copies:
        one.start()
    for one in copies:
        one.wait()


def pack(field, planes):
    blocks, _, rows, lanes = field.shape
    size = sum(size for _, size in planes)
    return pl.pallas_call(
        functools.partial(pack_kernel, planes),
        out_shape=(shaped(blocks, size, rows // 4, lanes),) * 3,
        in_specs=[HBM],
        out_specs=(VMEM,) * 3,
        scratch_shapes=[pltpu.SemaphoreType.DMA((32,))],
        compiler_params=params(),
        cost_estimate=cost(),
    )(pltpu.with_memory_space_constraint(field, pltpu.HBM))


def turns(position, mode, orders, total):
    order = jnp.zeros(mode.shape, jnp.int32)
    count = orders.shape[0]
    for j in range(count):
        order = jnp.where((mode == 1 + j) | (mode == 1 + count + j), orders[j], order)
    phase = lax.rem(position * order, total).astype(jnp.float32) * (2.0 * math.pi / total)
    value = jnp.where(mode <= count, jnp.cos(phase), jnp.sin(phase))
    return jnp.where(mode <= 2 * count, value, 0.0)


def harmonics_kernel(total, orders, after, front, back, out):
    blocks, planes, _, lanes = front.shape
    mode = lax.broadcasted_iota(jnp.int32, (MODES, planes), 0)
    position = lax.broadcasted_iota(jnp.int32, (MODES, planes), 1) + lax.axis_index("mesh") * planes
    basis = turns(position, mode, orders, total) * jnp.where(mode == 0, 1.0 / total, 2.0 / total)
    rotor = lax.axis_index("row") == 0
    for b in range(blocks):
        edge = jnp.where(rotor, back[b, :, 7, :], front[b, :, 0, :])
        out[:, b * lanes : (b + 1) * lanes] = jnp.dot(
            basis, edge, precision=lax.Precision.HIGHEST, preferred_element_type=jnp.float32
        )


def mix_kernel(scalars, own, up, down, far, after, *outs):
    weight = [scalars[k] for k in range(INST)]
    cosine, sine = scalars[INST], scalars[INST + 1]
    at = jnp.where(lax.axis_index("mesh") == 0, 1, 0)

    def mixed(var):
        u = [r[s, var, at] for r in (own, up, far, down) for s in range(2)]
        sums = []
        for a in range(INST):
            total = weight[a % INST] * u[0]
            for b in range(1, INST):
                total = total + weight[(a - b) % INST] * u[b]
            sums.append(total)
        return sums

    half = INST // 2

    def put(var, values):
        for a, value in enumerate(values):
            outs[a // half][a % half, var] = value

    for var in (0, 1, 4, 5):
        put(var, mixed(var))
    v, w = mixed(2), mixed(3)
    put(2, [cosine * x - sine * y for x, y in zip(v, w)])
    put(3, [sine * x + cosine * y for x, y in zip(v, w)])


def source_kernel(rims, scalars, *refs):
    outs, refs = refs[-4:], refs[:-4]
    if rims:
        *ghost, nu = refs[-3:]
        refs = refs[:-3]
    size = len(refs) // 4
    own, up, down, far = (refs[k * size : (k + 1) * size] for k in range(4))
    ratio = scalars[0]
    c1, c2, c3 = (ratio * D1, ratio * D2, ratio * D3)
    out_own, out_up, out_down, out_far = outs
    order = (out_own, out_up, out_far, out_down)
    for var in range(up[0].shape[1]):
        for p in range(size):
            u = [own[p][s, var, 0] for s in range(2)]
            u += [r[p][s, var, 0] for r in (up, far, down) for s in range(2)]
            near = [u[(n - 1) % INST] - u[(n + 1) % INST] for n in range(INST)]
            second = [c2 * (u[(n - 2) % INST] - u[(n + 2) % INST]) for n in range(4)]
            for n in range(INST):
                s = c1 * near[n] - c3 * near[(n + 4) % INST]
                s = s + second[n] if n < 4 else s - second[n - 4]
                order[n // 2][n % 2, var, p] = s
    if not rims:
        return

    def add_ghost(p, factor):
        for var in range(up[0].shape[1]):
            for n in range(INST):
                at = (n % 2, var, p)
                order[n // 2][at] = order[n // 2][at] - factor * ghost[n // 4][n % 4, var]

    place = pl.ds(pl.multiple_of(lax.axis_index("inst") * 16, 16), 16)

    @pl.when(lax.axis_index("mesh") == 0)
    def _():
        add_ghost(size - 1, nu[0, place, :] + 0.5)

    @pl.when(lax.axis_index("mesh") == lax.axis_size("mesh") - 1)
    def _():
        add_ghost(size - 2, nu[nu.shape[0] - 1, place, :])


def stencil_kernel(nu, low, high, field, one, two):
    blocks, planes, rows, lanes = field.shape
    lane = lax.broadcasted_iota(jnp.int32, (rows, lanes), 1)
    row = lax.broadcasted_iota(jnp.int32, (rows, lanes), 0)
    for b in range(blocks):
        for p in range(planes):
            u = field[b, p]
            before = low[b] if p == 0 else field[b, p - 1]
            after = high[b] if p == planes - 1 else field[b, p + 1]
            left = jnp.where(lane == 0, 0.0, pltpu.roll(u, 1, 1))
            right = jnp.where(lane == lanes - 1, 0.0, pltpu.roll(u, lanes - 1, 1))
            above = jnp.where(row == 0, 0.0, pltpu.roll(u, 1, 0))
            below = jnp.where(row == rows - 1, 0.0, pltpu.roll(u, rows - 1, 0))
            lap = (before + after) + (above + below) + (left + right) - 6.0 * u
            at = (p - 1) % planes
            out, at = (one, at) if at < OUTER else (two, at - OUTER)
            out[b, at] = nu[p] * lap - (u - above) - 0.5 * (u - before)


def add_kernel(one, two, after, out):
    out[...] = one[...] + two[...]


def edge_kernel(total, orders, one, two, nu, *rest):
    out = rest[-1]
    planes, blocks, rows, lanes = out.shape
    mode = lax.broadcasted_iota(jnp.int32, (planes, MODES), 1)
    position = lax.broadcasted_iota(jnp.int32, (planes, MODES), 0) + lax.axis_index("mesh") * planes
    ghost = jnp.dot(
        turns(position, mode, orders, total),
        one[...] + two[...],
        precision=lax.Precision.HIGHEST,
        preferred_element_type=jnp.float32,
    )
    rotor = lax.axis_index("row") == 0
    hit = lax.broadcasted_iota(jnp.int32, (rows, lanes), 0) == jnp.where(rotor, rows - 1, 0)
    for p in range(planes):
        facing = jnp.where(rotor, nu[p, nu.shape[1] - 1 :, :], nu[p, :1, :] + 1.0)
        for b in range(blocks):
            value = facing * ghost[p : p + 1, b * lanes : (b + 1) * lanes]
            out[p, b] = jnp.where(hit, value, 0.0)


def final_kernel(start, chunk, inverse, edge, field, pre, *rest):
    new, residual, new_held, residual_held, held_in, pieces, sems_in, sems = rest[-8:]
    count, planes, rows, lanes = field.shape
    size = held_in.shape[1]
    base = (start + 1) % planes
    inst = lax.axis_index("inst")
    arrivals = []
    for b in range(0, count, chunk):
        part = slice(b, b + chunk)
        pairs = [(pre.at[part], held_in.at[part])]
        pairs += [
            (rest[k].at[part], pieces.at[lax.rem(inst + step, 4), part])
            for k, step in enumerate((0, 1, 3, 2))
        ]
        arrivals.append(
            [
                pltpu.make_async_copy(x, y, sems_in.at[b // chunk, k])
                for k, (x, y) in enumerate(pairs)
            ]
        )
        for one in arrivals[-1]:
            one.start()
    tile = pl.ds(pl.multiple_of((1 - lax.axis_index("row")) * (rows - 8), 8), 8)
    runs = [(0, base, min(size, planes - base))]
    if base + size > planes:
        runs.append((planes - base, 0, base + size - planes))
    copies = []
    for j in range(0, count, 2):
        if j % chunk == 0:
            for one in arrivals[j // chunk]:
                one.wait()
        for p in range(size):
            plane = (base + p) % planes
            for b in (j, j + 1):
                for k in range(4):
                    at = pl.ds(16 * k, 16)
                    residual_held[b, p, at] = held_in[b, p, at] - pieces[k, b, p]
                residual_held[b, p, tile] = residual_held[b, p, tile] + edge[plane, b]
            high, low = split_bf16(
                jnp.concatenate([residual_held[j, p], residual_held[j + 1, p]], 1)
            )
            change = jnp.dot(
                inverse[...],
                jnp.concatenate([high, high, low], 0),
                preferred_element_type=jnp.float32,
            )
            new_held[j, p] = field[j, plane] + change[:, :lanes]
            new_held[j + 1, p] = field[j + 1, plane] + change[:, lanes:]
        if (j + 2) % chunk == 0:
            part = slice(j + 2 - chunk, j + 2)
            for held, out in ((residual_held, residual), (new_held, new)):
                for source, target, length in runs:
                    copies.append(
                        pltpu.make_async_copy(
                            held.at[part, source : source + length],
                            out.at[part, target : target + length],
                            sems.at[len(copies)],
                        )
                    )
                    copies[-1].start()
    for one in copies:
        one.wait()


def lag_weights(lag):
    delta = jnp.arange(INST).astype(jnp.float32) - lag
    total = 1.0 + jnp.cos(math.pi * delta)
    for k in range(1, INST // 2):
        total = total + 2.0 * jnp.cos(2.0 * math.pi * k / INST * delta)
    return total / INST


def local(state, viscosity, blade_counts, mode_orders):
    _, local_inst, variables, planes, rows, lanes = state.shape
    quarter = rows // 4
    blocks = local_inst * variables
    mesh_count = lax.axis_size("mesh")
    total = planes * mesh_count
    which = lax.axis_index("row")
    inst = lax.axis_index("inst")
    mesh_idx = lax.axis_index("mesh")
    counts = blade_counts.astype(jnp.float32)
    ratio = counts[1 - which] / counts[which]
    angle = 2.0 * math.pi / counts[which]
    field = state.reshape(blocks, planes, rows, lanes)
    nu = viscosity[0]
    first = mesh_idx == 0
    last = mesh_idx == mesh_count - 1

    def along(x, step):
        return lax.ppermute(x, "inst", [(j, (j + step) % 4) for j in range(4)])

    def in_hbm(*arrays):
        return [pltpu.with_memory_space_constraint(x, pltpu.HBM) for x in arrays]

    def exchange(up, down, far):
        from_down, from_up, from_far = along(up, 1), along(down, 3), along(far, 2)
        return from_up, from_down, from_far

    packed = pack(field, ((1, planes - 1), (0, 1)))
    gathered = exchange(*packed)

    top, bottom, own = pl.pallas_call(
        edges_kernel,
        out_shape=(shaped(blocks, rows, lanes),) * 2 + (shaped(blocks, planes, quarter, lanes),),
        in_specs=[HBM, VMEM],
        out_specs=(VMEM,) * 3,
        scratch_shapes=[pltpu.SemaphoreType.DMA((3, blocks))],
        compiler_params=params(),
        cost_estimate=cost(),
    )(pltpu.with_memory_space_constraint(field, pltpu.HBM), packed[0])
    low = lax.ppermute(top, "mesh", [(j, j + 1) for j in range(mesh_count - 1)])
    high = lax.ppermute(bottom, "mesh", [(j + 1, j) for j in range(mesh_count - 1)])

    split = (local_inst, variables)
    all_quarters = in_hbm(*(x.reshape(*split, planes, quarter, lanes) for x in (own, *gathered)))

    whole = shaped(*field.shape)
    at_once = 2
    slab = pl.BlockSpec((at_once, planes, rows, lanes), lambda b: (b, 0, 0, 0))
    plane = pl.BlockSpec((at_once, rows, lanes), lambda b: (b, 0, 0))
    pre_one, pre_two = pl.pallas_call(
        stencil_kernel,
        grid=(blocks // at_once,),
        out_shape=(
            pltpu.HBM((blocks, OUTER, rows, lanes), jnp.float32),
            pltpu.HBM((blocks, planes - OUTER, rows, lanes), jnp.float32),
        ),
        in_specs=[pl.BlockSpec((planes, rows, lanes), lambda b: (0, 0, 0)), plane, plane, slab],
        out_specs=(
            pl.BlockSpec((at_once, OUTER, rows, lanes), lambda b: (b, 0, 0, 0)),
            pl.BlockSpec((at_once, planes - OUTER, rows, lanes), lambda b: (b, 0, 0, 0)),
        ),
        compiler_params=params(),
        cost_estimate=cost(),
    )(nu, *in_hbm(low, high), field)

    harmonics = pl.pallas_call(
        functools.partial(harmonics_kernel, total),
        out_shape=shaped(MODES, blocks * lanes),
        grid=(1,),
        in_specs=[
            SMEM,
            VMEM,
            pl.BlockSpec((blocks, planes, 8, lanes), lambda b: (0, 0, 0, 0)),
            pl.BlockSpec((blocks, planes, 8, lanes), lambda b: (0, 0, rows // 8 - 1, 0)),
        ],
        out_specs=pl.BlockSpec((MODES, blocks * lanes), lambda b: (0, 0)),
        compiler_params=params(),
        cost_estimate=cost(),
    )(mode_orders, packed[0], field, field)

    def crossing(flip):
        return [
            (r * mesh_count + m, (1 - r) * mesh_count + (m ^ flip))
            for r in range(2)
            for m in range(mesh_count)
        ]

    def doubled(x, flip):
        return x + lax.ppermute(x, "mesh", [(m, m ^ flip) for m in range(mesh_count)])

    two_ways = [lax.ppermute(harmonics, ("row", "mesh"), crossing(flip)) for flip in (0, 1)]
    harmonics = two_ways[0] + two_ways[1]
    early = lax.ppermute(harmonics, "mesh", [(m, m ^ 2) for m in range(mesh_count)])

    def sources(start, size, rims, after=()):
        at_once = 3
        pieces_in = [
            pl.BlockSpec(
                (2, at_once, 1, quarter, lanes),
                functools.partial(lambda plane, b: (0, b, plane, 0, 0), start + p),
            )
            for _ in range(4)
            for p in range(size)
        ]
        rim_specs = [
            pl.BlockSpec((INST // 2, at_once, quarter, lanes), lambda b: (0, b, 0, 0)),
            pl.BlockSpec((INST // 2, at_once, quarter, lanes), lambda b: (0, b, 0, 0)),
            pl.BlockSpec((planes, rows, lanes), lambda b: (0, 0, 0)),
        ]
        def kernel(*refs):
            inputs, outputs = refs[: -4 - len(after)], refs[-4:]
            source_kernel(bool(rims), *inputs, *outputs)

        outs = pl.pallas_call(
            kernel,
            out_shape=(pltpu.HBM((*split, size, quarter, lanes), jnp.float32),) * 4,
            grid=(variables // at_once,),
            in_specs=[SMEM] + pieces_in + rim_specs[: len(rims)] + [ANY] * len(after),
            out_specs=(
                pl.BlockSpec((2, at_once, size, quarter, lanes), lambda b: (0, b, 0, 0, 0)),
            )
            * 4,
            compiler_params=params(),
            cost_estimate=cost(),
        )(ratio[None], *(x for x in all_quarters for _ in range(size)), *rims, *after)
        own, up, down, far = (x.reshape(blocks, size, quarter, lanes) for x in outs)
        return (own, *exchange(up, down, far))

    one_source = sources(0, OUTER, (), after=(*in_hbm(pre_one), early))

    weights = lag_weights(jnp.where(first, -ratio, ratio))
    turn = jnp.where(first, angle, -angle)
    ghost_shape = shaped(INST // 2, variables, quarter, lanes)

    outermost = pl.BlockSpec((2, variables, 2, quarter, lanes), lambda b: (0, 0, 3, 0, 0))
    ghost_out = pl.pallas_call(
        mix_kernel,
        out_shape=(ghost_shape,) * 2,
        grid=(1,),
        in_specs=[SMEM] + [outermost] * 4 + [ANY],
        out_specs=(pl.BlockSpec(ghost_shape.shape, lambda b: (0, 0, 0, 0)),) * 2,
        compiler_params=params(),
        cost_estimate=cost(),
    )(
        jnp.concatenate([weights, jnp.stack([jnp.cos(turn), jnp.sin(turn)])]),
        *all_quarters,
        *in_hbm(one_source[0]),
    )
    ghost = [
        lax.ppermute(part, "mesh", [(mesh_count - 1, 0), (0, mesh_count - 1)]) for part in ghost_out
    ]

    harmonics = pl.pallas_call(
        add_kernel,
        out_shape=harmonics,
        in_specs=[VMEM, VMEM, ANY],
        out_specs=VMEM,
        compiler_params=params(),
        cost_estimate=cost(),
    )(harmonics, early, ghost_out[0])
    harmonics = doubled(harmonics, 4)
    opposite = lax.ppermute(harmonics, "mesh", [(m, m ^ 8) for m in range(mesh_count)])
    two_source = sources(OUTER, planes - OUTER, (*ghost, nu), after=(opposite,))

    edge = pl.pallas_call(
        functools.partial(edge_kernel, total),
        out_shape=shaped(planes, blocks, 8, lanes),
        in_specs=[SMEM, VMEM, VMEM, VMEM] + [ANY] * 3,
        out_specs=VMEM,
        compiler_params=params(),
        cost_estimate=cost(),
    )(
        mode_orders,
        harmonics,
        opposite,
        nu,
        *one_source[1:],
    )

    inverse = jnp.asarray(inverse_parts(rows))
    kept = ()
    for start, size, group, pre in ((0, OUTER, one_source, pre_one), (OUTER, planes - OUTER, two_source, pre_two)):
        given = 4 + len(group)
        kept = pl.pallas_call(
            functools.partial(final_kernel, start, 2 if size > 3 else 4),
            out_shape=(pltpu.HBM(field.shape, jnp.float32),) * 2,
            in_specs=[VMEM] * 3 + [HBM] * 2 + [ANY] * 3 + [HBM] * len(kept),
            out_specs=(HBM,) * 2,
            scratch_shapes=[pltpu.VMEM((blocks, size, rows, lanes), jnp.float32)] * 3
            + [
                pltpu.VMEM((4, blocks, size, quarter, lanes), jnp.float32),
                pltpu.SemaphoreType.DMA((blocks, 5)),
                pltpu.SemaphoreType.DMA((4 * blocks,)),
            ],
            input_output_aliases={given: 0, given + 1: 1} if kept else {},
            compiler_params=params(),
            cost_estimate=cost(),
        )(inverse, edge, field, *in_hbm(pre, group[0]), *group[1:], *kept)
    new, residual = kept
    return (new.reshape(state.shape), residual.reshape(state.shape))


def solution(mesh):
    spread = P("row", "inst", None, "mesh", None, None)
    return jax.shard_map(
        local,
        mesh=mesh,
        in_specs=(spread, P("row", "mesh", None, None), P(), P()),
        out_specs=(spread, spread),
        check_vma=False,
    )
```

```python
import functools
import math

import numpy as np

import jax
import jax.numpy as jnp
from jax import lax
from jax.experimental import pallas as pl
from jax.experimental.pallas import tpu as pltpu
from jax.sharding import PartitionSpec as P

INST = 8
OUTER = 6
MODES = 24
LIMIT = 14 * 1024 * 1024
VMEM = pl.BlockSpec(memory_space=pltpu.VMEM)
SMEM = pl.BlockSpec(memory_space=pltpu.SMEM)
ANY = pl.BlockSpec(memory_space=pl.ANY)
HBM = pl.BlockSpec(memory_space=pltpu.HBM)
D1 = -0.5 / math.tan(math.pi / 8)
D2 = 0.5 / math.tan(math.pi / 4)
D3 = -0.5 / math.tan(3 * math.pi / 8)


def shaped(*dims):
    return jax.ShapeDtypeStruct(dims, jnp.float32)


def cost():
    return pl.CostEstimate(flops=1, bytes_accessed=1, transcendentals=0)


def inverse_parts(length):
    steps = np.arange(1, length + 1).astype(np.float64)
    basis = math.sqrt(2.0 / (length + 1)) * np.sin(
        math.pi * steps[:, None] * steps[None, :] / (length + 1)
    )
    eigen = 2.0 - np.cos(math.pi * steps / (length + 1))
    inverse = (0.2 * (basis / eigen[None, :]) @ basis.T).astype(np.float32)
    high = inverse.astype(jnp.bfloat16)
    low = (inverse - high.astype(np.float32)).astype(jnp.bfloat16)
    return np.concatenate([high, low, high], axis=1)


def split_bf16(x):
    high = x.astype(jnp.bfloat16)
    return high, (x - high.astype(jnp.float32)).astype(jnp.bfloat16)


def params():
    return pltpu.CompilerParams(vmem_limit_bytes=LIMIT)


def pack_kernel(planes, field, *rest):
    sems = rest[-1]
    copies = []

    def copy(source, target):
        one = pltpu.make_async_copy(source, target, sems.at[len(copies)])
        one.start()
        copies.append(one)

    outs = rest[:3]
    for k, out in zip((1, 3, 2), outs):
        place = lax.rem(lax.axis_index("inst") + k, 4) * 16
        rows = pl.ds(pl.multiple_of(place, 16), 16)
        done = 0
        for start, size in planes:
            for b in range(0, field.shape[0], 4):
                copy(
                    field.at[b : b + 4, start : start + size, rows, :],
                    out.at[b : b + 4, done : done + size],
                )
            done += size
    for one in copies:
        one.wait()


def edges_kernel(field, after, top, bottom, own, sems):
    rows = pl.ds(pl.multiple_of(lax.axis_index("inst") * 16, 16), 16)
    copies = [
        pltpu.make_async_copy(field.at[b, plane], out.at[b], sems.at[k, b])
        for k, (plane, out) in enumerate(((field.shape[1] - 1, top), (0, bottom)))
        for b in range(field.shape[0])
    ]
    last = field.shape[1] - 1
    copies.append(
        pltpu.make_async_copy(field.at[:, 1:, rows, :], own.at[:, :last], sems.at[2, 0])
    )
    copies.append(
        pltpu.make_async_copy(field.at[:, :1, rows, :], own.at[:, last:], sems.at[2, 1])
    )
    for one in copies:
        one.start()
    for one in copies:
        one.wait()


def pack(field, planes):
    blocks, _, rows, lanes = field.shape
    size = sum(size for _, size in planes)
    return pl.pallas_call(
        functools.partial(pack_kernel, planes),
        out_shape=(shaped(blocks, size, rows // 4, lanes),) * 3,
        in_specs=[HBM],
        out_specs=(VMEM,) * 3,
        scratch_shapes=[pltpu.SemaphoreType.DMA((32,))],
        compiler_params=params(),
        cost_estimate=cost(),
    )(pltpu.with_memory_space_constraint(field, pltpu.HBM))


def turns(position, mode, orders, total):
    order = jnp.zeros(mode.shape, jnp.int32)
    count = orders.shape[0]
    for j in range(count):
        order = jnp.where((mode == 1 + j) | (mode == 1 + count + j), orders[j], order)
    phase = lax.rem(position * order, total).astype(jnp.float32) * (2.0 * math.pi / total)
    value = jnp.where(mode <= count, jnp.cos(phase), jnp.sin(phase))
    return jnp.where(mode <= 2 * count, value, 0.0)


def harmonics_kernel(total, orders, after, front, back, out):
    blocks, planes, _, lanes = front.shape
    mode = lax.broadcasted_iota(jnp.int32, (MODES, planes), 0)
    position = lax.broadcasted_iota(jnp.int32, (MODES, planes), 1) + lax.axis_index("mesh") * planes
    basis = turns(position, mode, orders, total) * jnp.where(mode == 0, 1.0 / total, 2.0 / total)
    rotor = lax.axis_index("row") == 0
    for b in range(blocks):
        edge = jnp.where(rotor, back[b, :, 7, :], front[b, :, 0, :])
        out[:, b * lanes : (b + 1) * lanes] = jnp.dot(
            basis, edge, precision=lax.Precision.HIGHEST, preferred_element_type=jnp.float32
        )


def mix_kernel(scalars, own, up, down, far, after, *outs):
    weight = [scalars[k] for k in range(INST)]
    cosine, sine = scalars[INST], scalars[INST + 1]
    at = jnp.where(lax.axis_index("mesh") == 0, 1, 0)

    def mixed(var):
        u = [r[s, var, at] for r in (own, up, far, down) for s in range(2)]
        sums = []
        for a in range(INST):
            total = weight[a % INST] * u[0]
            for b in range(1, INST):
                total = total + weight[(a - b) % INST] * u[b]
            sums.append(total)
        return sums

    half = INST // 2

    def put(var, values):
        for a, value in enumerate(values):
            outs[a // half][a % half, var] = value

    for var in (0, 1, 4, 5):
        put(var, mixed(var))
    v, w = mixed(2), mixed(3)
    put(2, [cosine * x - sine * y for x, y in zip(v, w)])
    put(3, [sine * x + cosine * y for x, y in zip(v, w)])


def source_kernel(rims, scalars, *refs):
    outs, refs = refs[-4:], refs[:-4]
    if rims:
        *ghost, nu = refs[-3:]
        refs = refs[:-3]
    size = len(refs) // 4
    own, up, down, far = (refs[k * size : (k + 1) * size] for k in range(4))
    ratio = scalars[0]
    c1, c2, c3 = (ratio * D1, ratio * D2, ratio * D3)
    out_own, out_up, out_down, out_far = outs
    order = (out_own, out_up, out_far, out_down)
    for var in range(up[0].shape[1]):
        for p in range(size):
            u = [own[p][s, var, 0] for s in range(2)]
            u += [r[p][s, var, 0] for r in (up, far, down) for s in range(2)]
            near = [u[(n - 1) % INST] - u[(n + 1) % INST] for n in range(INST)]
            second = [c2 * (u[(n - 2) % INST] - u[(n + 2) % INST]) for n in range(4)]
            for n in range(INST):
                s = c1 * near[n] - c3 * near[(n + 4) % INST]
                s = s + second[n] if n < 4 else s - second[n - 4]
                order[n // 2][n % 2, var, p] = s
    if not rims:
        return

    def add_ghost(p, factor):
        for var in range(up[0].shape[1]):
            for n in range(INST):
                at = (n % 2, var, p)
                order[n // 2][at] = order[n // 2][at] - factor * ghost[n // 4][n % 4, var]

    place = pl.ds(pl.multiple_of(lax.axis_index("inst") * 16, 16), 16)

    @pl.when(lax.axis_index("mesh") == 0)
    def _():
        add_ghost(size - 1, nu[0, place, :] + 0.5)

    @pl.when(lax.axis_index("mesh") == lax.axis_size("mesh") - 1)
    def _():
        add_ghost(size - 2, nu[nu.shape[0] - 1, place, :])


def stencil_kernel(nu, low, high, field, one, two):
    blocks, planes, rows, lanes = field.shape
    lane = lax.broadcasted_iota(jnp.int32, (rows, lanes), 1)
    row = lax.broadcasted_iota(jnp.int32, (rows, lanes), 0)
    for b in range(blocks):
        for p in range(planes):
            u = field[b, p]
            before = low[b] if p == 0 else field[b, p - 1]
            after = high[b] if p == planes - 1 else field[b, p + 1]
            left = jnp.where(lane == 0, 0.0, pltpu.roll(u, 1, 1))
            right = jnp.where(lane == lanes - 1, 0.0, pltpu.roll(u, lanes - 1, 1))
            above = jnp.where(row == 0, 0.0, pltpu.roll(u, 1, 0))
            below = jnp.where(row == rows - 1, 0.0, pltpu.roll(u, rows - 1, 0))
            lap = (before + after) + (above + below) + (left + right) - 6.0 * u
            at = (p - 1) % planes
            out, at = (one, at) if at < OUTER else (two, at - OUTER)
            out[b, at] = nu[p] * lap - (u - above) - 0.5 * (u - before)


def add_kernel(one, two, after, out):
    out[...] = one[...] + two[...]


def edge_kernel(total, orders, one, two, nu, *rest):
    out = rest[-1]
    planes, blocks, rows, lanes = out.shape
    mode = lax.broadcasted_iota(jnp.int32, (planes, MODES), 1)
    position = lax.broadcasted_iota(jnp.int32, (planes, MODES), 0) + lax.axis_index("mesh") * planes
    ghost = jnp.dot(
        turns(position, mode, orders, total),
        one[...] + two[...],
        precision=lax.Precision.HIGHEST,
        preferred_element_type=jnp.float32,
    )
    rotor = lax.axis_index("row") == 0
    hit = lax.broadcasted_iota(jnp.int32, (rows, lanes), 0) == jnp.where(rotor, rows - 1, 0)
    for p in range(planes):
        facing = jnp.where(rotor, nu[p, nu.shape[1] - 1 :, :], nu[p, :1, :] + 1.0)
        for b in range(blocks):
            value = facing * ghost[p : p + 1, b * lanes : (b + 1) * lanes]
            out[p, b] = jnp.where(hit, value, 0.0)


def final_kernel(start, chunk, near, inverse, edge, field, pre, *rest):
    new, residual, new_held, residual_held = rest[-6 - 2 * (not near) : -2 - 2 * (not near)]
    sems_in, sems = rest[-2:]
    count, planes, rows, lanes = field.shape
    size = pre.shape[1]
    base = (start + 1) % planes
    inst = lax.axis_index("inst")
    steps = (0, 1, 3, 2)
    arrivals = []
    if not near:
        held_in, pieces = rest[-4:-2]
    for b in range(0, count, chunk):
        if near:
            arrivals.append([])
            continue
        part = slice(b, b + chunk)
        pairs = [(pre.at[part], held_in.at[part])]
        pairs += [
            (rest[k].at[part], pieces.at[lax.rem(inst + step, 4), part])
            for k, step in enumerate(steps)
        ]
        arrivals.append(
            [
                pltpu.make_async_copy(x, y, sems_in.at[b // chunk, k])
                for k, (x, y) in enumerate(pairs)
            ]
        )
        for one in arrivals[-1]:
            one.start()
    tile = pl.ds(pl.multiple_of((1 - lax.axis_index("row")) * (rows - 8), 8), 8)
    runs = [(0, base, min(size, planes - base))]
    if base + size > planes:
        runs.append((planes - base, 0, base + size - planes))
    copies = []
    for j in range(0, count, 2):
        if j % chunk == 0:
            for one in arrivals[j // chunk]:
                one.wait()
        for p in range(size):
            plane = (base + p) % planes
            for b in (j, j + 1):
                for k, step in enumerate(steps):
                    if near:
                        at = pl.ds(pl.multiple_of(16 * lax.rem(inst + step, 4), 16), 16)
                        residual_held[b, p, at] = pre[b, p, at] - rest[k][b, p]
                    else:
                        at = pl.ds(16 * k, 16)
                        residual_held[b, p, at] = held_in[b, p, at] - pieces[k, b, p]
                residual_held[b, p, tile] = residual_held[b, p, tile] + edge[plane, b]
            high, low = split_bf16(
                jnp.concatenate([residual_held[j, p], residual_held[j + 1, p]], 1)
            )
            change = jnp.dot(
                inverse[...],
                jnp.concatenate([high, high, low], 0),
                preferred_element_type=jnp.float32,
            )
            new_held[j, p] = field[j, plane] + change[:, :lanes]
            new_held[j + 1, p] = field[j + 1, plane] + change[:, lanes:]
        if (j + 2) % chunk == 0:
            part = slice(j + 2 - chunk, j + 2)
            for held, out in ((residual_held, residual), (new_held, new)):
                for source, target, length in runs:
                    copies.append(
                        pltpu.make_async_copy(
                            held.at[part, source : source + length],
                            out.at[part, target : target + length],
                            sems.at[len(copies)],
                        )
                    )
                    copies[-1].start()
    for one in copies:
        one.wait()


def lag_weights(lag):
    delta = jnp.arange(INST).astype(jnp.float32) - lag
    total = 1.0 + jnp.cos(math.pi * delta)
    for k in range(1, INST // 2):
        total = total + 2.0 * jnp.cos(2.0 * math.pi * k / INST * delta)
    return total / INST


def local(state, viscosity, blade_counts, mode_orders):
    _, local_inst, variables, planes, rows, lanes = state.shape
    quarter = rows // 4
    blocks = local_inst * variables
    mesh_count = lax.axis_size("mesh")
    total = planes * mesh_count
    which = lax.axis_index("row")
    inst = lax.axis_index("inst")
    mesh_idx = lax.axis_index("mesh")
    counts = blade_counts.astype(jnp.float32)
    ratio = counts[1 - which] / counts[which]
    angle = 2.0 * math.pi / counts[which]
    field = state.reshape(blocks, planes, rows, lanes)
    nu = viscosity[0]
    first = mesh_idx == 0
    last = mesh_idx == mesh_count - 1

    def along(x, step):
        return lax.ppermute(x, "inst", [(j, (j + step) % 4) for j in range(4)])

    def in_hbm(*arrays):
        return [pltpu.with_memory_space_constraint(x, pltpu.HBM) for x in arrays]

    def exchange(up, down, far):
        from_down, from_up, from_far = along(up, 1), along(down, 3), along(far, 2)
        return from_up, from_down, from_far

    packed = pack(field, ((1, planes - 1), (0, 1)))
    gathered = exchange(*packed)

    top, bottom, own = pl.pallas_call(
        edges_kernel,
        out_shape=(shaped(blocks, rows, lanes),) * 2 + (shaped(blocks, planes, quarter, lanes),),
        in_specs=[HBM, VMEM],
        out_specs=(VMEM,) * 3,
        scratch_shapes=[pltpu.SemaphoreType.DMA((3, blocks))],
        compiler_params=params(),
        cost_estimate=cost(),
    )(pltpu.with_memory_space_constraint(field, pltpu.HBM), packed[0])
    low = lax.ppermute(top, "mesh", [(j, j + 1) for j in range(mesh_count - 1)])
    high = lax.ppermute(bottom, "mesh", [(j + 1, j) for j in range(mesh_count - 1)])

    split = (local_inst, variables)
    all_quarters = in_hbm(*(x.reshape(*split, planes, quarter, lanes) for x in (own, *gathered)))

    whole = shaped(*field.shape)
    at_once = 2
    slab = pl.BlockSpec((at_once, planes, rows, lanes), lambda b: (b, 0, 0, 0))
    plane = pl.BlockSpec((at_once, rows, lanes), lambda b: (b, 0, 0))
    pre_one, pre_two = pl.pallas_call(
        stencil_kernel,
        grid=(blocks // at_once,),
        out_shape=(
            pltpu.HBM((blocks, OUTER, rows, lanes), jnp.float32),
            pltpu.HBM((blocks, planes - OUTER, rows, lanes), jnp.float32),
        ),
        in_specs=[pl.BlockSpec((planes, rows, lanes), lambda b: (0, 0, 0)), plane, plane, slab],
        out_specs=(
            pl.BlockSpec((at_once, OUTER, rows, lanes), lambda b: (b, 0, 0, 0)),
            pl.BlockSpec((at_once, planes - OUTER, rows, lanes), lambda b: (b, 0, 0, 0)),
        ),
        compiler_params=params(),
        cost_estimate=cost(),
    )(nu, *in_hbm(low, high), field)

    harmonics = pl.pallas_call(
        functools.partial(harmonics_kernel, total),
        out_shape=shaped(MODES, blocks * lanes),
        grid=(1,),
        in_specs=[
            SMEM,
            VMEM,
            pl.BlockSpec((blocks, planes, 8, lanes), lambda b: (0, 0, 0, 0)),
            pl.BlockSpec((blocks, planes, 8, lanes), lambda b: (0, 0, rows // 8 - 1, 0)),
        ],
        out_specs=pl.BlockSpec((MODES, blocks * lanes), lambda b: (0, 0)),
        compiler_params=params(),
        cost_estimate=cost(),
    )(mode_orders, packed[0], field, field)

    def crossing(flip):
        return [
            (r * mesh_count + m, (1 - r) * mesh_count + (m ^ flip))
            for r in range(2)
            for m in range(mesh_count)
        ]

    def doubled(x, flip):
        return x + lax.ppermute(x, "mesh", [(m, m ^ flip) for m in range(mesh_count)])

    two_ways = [lax.ppermute(harmonics, ("row", "mesh"), crossing(flip)) for flip in (0, 1)]
    harmonics = two_ways[0] + two_ways[1]
    early = lax.ppermute(harmonics, "mesh", [(m, m ^ 2) for m in range(mesh_count)])

    def sources(start, size, rims, after=()):
        at_once = 3
        pieces_in = [
            pl.BlockSpec(
                (2, at_once, 1, quarter, lanes),
                functools.partial(lambda plane, b: (0, b, plane, 0, 0), start + p),
            )
            for _ in range(4)
            for p in range(size)
        ]
        rim_specs = [
            pl.BlockSpec((INST // 2, at_once, quarter, lanes), lambda b: (0, b, 0, 0)),
            pl.BlockSpec((INST // 2, at_once, quarter, lanes), lambda b: (0, b, 0, 0)),
            pl.BlockSpec((planes, rows, lanes), lambda b: (0, 0, 0)),
        ]
        def kernel(*refs):
            inputs, outputs = refs[: -4 - len(after)], refs[-4:]
            source_kernel(bool(rims), *inputs, *outputs)

        outs = pl.pallas_call(
            kernel,
            out_shape=(pltpu.HBM((*split, size, quarter, lanes), jnp.float32),) * 4,
            grid=(variables // at_once,),
            in_specs=[SMEM] + pieces_in + rim_specs[: len(rims)] + [ANY] * len(after),
            out_specs=(
                pl.BlockSpec((2, at_once, size, quarter, lanes), lambda b: (0, b, 0, 0, 0)),
            )
            * 4,
            compiler_params=params(),
            cost_estimate=cost(),
        )(ratio[None], *(x for x in all_quarters for _ in range(size)), *rims, *after)
        own, up, down, far = (x.reshape(blocks, size, quarter, lanes) for x in outs)
        return (own, *exchange(up, down, far))

    one_source = sources(0, OUTER, (), after=(*in_hbm(pre_one), early))

    weights = lag_weights(jnp.where(first, -ratio, ratio))
    turn = jnp.where(first, angle, -angle)
    ghost_shape = shaped(INST // 2, variables, quarter, lanes)

    outermost = pl.BlockSpec((2, variables, 2, quarter, lanes), lambda b: (0, 0, 3, 0, 0))
    ghost_out = pl.pallas_call(
        mix_kernel,
        out_shape=(ghost_shape,) * 2,
        grid=(1,),
        in_specs=[SMEM] + [outermost] * 4 + [ANY],
        out_specs=(pl.BlockSpec(ghost_shape.shape, lambda b: (0, 0, 0, 0)),) * 2,
        compiler_params=params(),
        cost_estimate=cost(),
    )(
        jnp.concatenate([weights, jnp.stack([jnp.cos(turn), jnp.sin(turn)])]),
        *all_quarters,
        *in_hbm(one_source[0]),
    )
    ghost = [
        lax.ppermute(part, "mesh", [(mesh_count - 1, 0), (0, mesh_count - 1)]) for part in ghost_out
    ]

    harmonics = pl.pallas_call(
        add_kernel,
        out_shape=harmonics,
        in_specs=[VMEM, VMEM, ANY],
        out_specs=VMEM,
        compiler_params=params(),
        cost_estimate=cost(),
    )(harmonics, early, ghost_out[0])
    harmonics = doubled(harmonics, 4)
    opposite = lax.ppermute(harmonics, "mesh", [(m, m ^ 8) for m in range(mesh_count)])
    two_source = sources(OUTER, planes - OUTER, (*ghost, nu), after=(opposite,))

    edge = pl.pallas_call(
        functools.partial(edge_kernel, total),
        out_shape=shaped(planes, blocks, 8, lanes),
        in_specs=[SMEM, VMEM, VMEM, VMEM] + [ANY] * 3,
        out_specs=VMEM,
        compiler_params=params(),
        cost_estimate=cost(),
    )(
        mode_orders,
        harmonics,
        opposite,
        nu,
        *one_source[1:],
    )

    inverse = jnp.asarray(inverse_parts(rows))
    kept = ()
    for start, size, group, pre in ((0, OUTER, one_source, pre_one), (OUTER, planes - OUTER, two_source, pre_two)):
        given = 4 + len(group)
        near = size < 4
        if near:
            group = [pltpu.with_memory_space_constraint(x, pltpu.VMEM) for x in group]
            given_in = (pre, *group)
        else:
            given_in = (*in_hbm(pre, group[0]), *group[1:])
        kept = pl.pallas_call(
            functools.partial(final_kernel, start, 4 if near else 2, near),
            out_shape=(pltpu.HBM(field.shape, jnp.float32),) * 2,
            in_specs=[VMEM] * 3
            + ([VMEM] * 5 if near else [HBM] * 2 + [ANY] * 3)
            + [HBM] * len(kept),
            out_specs=(HBM,) * 2,
            scratch_shapes=[pltpu.VMEM((blocks, size, rows, lanes), jnp.float32)] * (2 + (not near))
            + [pltpu.VMEM((4, blocks, size, quarter, lanes), jnp.float32)] * (not near)
            + [pltpu.SemaphoreType.DMA((blocks, 5)), pltpu.SemaphoreType.DMA((4 * blocks,))],
            input_output_aliases={given: 0, given + 1: 1} if kept else {},
            compiler_params=params(),
            cost_estimate=cost(),
        )(inverse, edge, field, *given_in, *kept)
    new, residual = kept
    return (new.reshape(state.shape), residual.reshape(state.shape))


def solution(mesh):
    spread = P("row", "inst", None, "mesh", None, None)
    return jax.shard_map(
        local,
        mesh=mesh,
        in_specs=(spread, P("row", "mesh", None, None), P(), P()),
        out_specs=(spread, spread),
        check_vma=False,
    )
```

```python
import functools
import math

import numpy as np

import jax
import jax.numpy as jnp
from jax import lax
from jax.experimental import pallas as pl
from jax.experimental.pallas import tpu as pltpu
from jax.sharding import PartitionSpec as P

INST = 8
OUTER = 6
MODES = 24
LIMIT = 14 * 1024 * 1024
VMEM = pl.BlockSpec(memory_space=pltpu.VMEM)
SMEM = pl.BlockSpec(memory_space=pltpu.SMEM)
ANY = pl.BlockSpec(memory_space=pl.ANY)
HBM = pl.BlockSpec(memory_space=pltpu.HBM)
D1 = -0.5 / math.tan(math.pi / 8)
D2 = 0.5 / math.tan(math.pi / 4)
D3 = -0.5 / math.tan(3 * math.pi / 8)


def shaped(*dims):
    return jax.ShapeDtypeStruct(dims, jnp.float32)


def cost():
    return pl.CostEstimate(flops=1, bytes_accessed=1, transcendentals=0)


def inverse_parts(length):
    steps = np.arange(1, length + 1).astype(np.float64)
    basis = math.sqrt(2.0 / (length + 1)) * np.sin(
        math.pi * steps[:, None] * steps[None, :] / (length + 1)
    )
    eigen = 2.0 - np.cos(math.pi * steps / (length + 1))
    inverse = (0.2 * (basis / eigen[None, :]) @ basis.T).astype(np.float32)
    high = inverse.astype(jnp.bfloat16)
    low = (inverse - high.astype(np.float32)).astype(jnp.bfloat16)
    return np.concatenate([high, low, high], axis=1)


def split_bf16(x):
    high = x.astype(jnp.bfloat16)
    return high, (x - high.astype(jnp.float32)).astype(jnp.bfloat16)


def params():
    return pltpu.CompilerParams(vmem_limit_bytes=LIMIT)


def pack_kernel(planes, field, *rest):
    sems = rest[-1]
    copies = []

    def copy(source, target):
        one = pltpu.make_async_copy(source, target, sems.at[len(copies)])
        one.start()
        copies.append(one)

    outs = rest[:3]
    for k, out in zip((1, 3, 2), outs):
        place = lax.rem(lax.axis_index("inst") + k, 4) * 16
        rows = pl.ds(pl.multiple_of(place, 16), 16)
        done = 0
        for start, size in planes:
            for b in range(0, field.shape[0], 4):
                copy(
                    field.at[b : b + 4, start : start + size, rows, :],
                    out.at[b : b + 4, done : done + size],
                )
            done += size
    for one in copies:
        one.wait()


def edges_kernel(field, after, top, bottom, own, sems):
    rows = pl.ds(pl.multiple_of(lax.axis_index("inst") * 16, 16), 16)
    copies = [
        pltpu.make_async_copy(field.at[b, plane], out.at[b], sems.at[k, b])
        for k, (plane, out) in enumerate(((field.shape[1] - 1, top), (0, bottom)))
        for b in range(field.shape[0])
    ]
    last = field.shape[1] - 1
    copies.append(
        pltpu.make_async_copy(field.at[:, 1:, rows, :], own.at[:, :last], sems.at[2, 0])
    )
    copies.append(
        pltpu.make_async_copy(field.at[:, :1, rows, :], own.at[:, last:], sems.at[2, 1])
    )
    for one in copies:
        one.start()
    for one in copies:
        one.wait()


def pack(field, planes):
    blocks, _, rows, lanes = field.shape
    size = sum(size for _, size in planes)
    return pl.pallas_call(
        functools.partial(pack_kernel, planes),
        out_shape=(shaped(blocks, size, rows // 4, lanes),) * 3,
        in_specs=[HBM],
        out_specs=(VMEM,) * 3,
        scratch_shapes=[pltpu.SemaphoreType.DMA((32,))],
        compiler_params=params(),
        cost_estimate=cost(),
    )(pltpu.with_memory_space_constraint(field, pltpu.HBM))


def turns(position, mode, orders, total):
    order = jnp.zeros(mode.shape, jnp.int32)
    count = orders.shape[0]
    for j in range(count):
        order = jnp.where((mode == 1 + j) | (mode == 1 + count + j), orders[j], order)
    phase = lax.rem(position * order, total).astype(jnp.float32) * (2.0 * math.pi / total)
    value = jnp.where(mode <= count, jnp.cos(phase), jnp.sin(phase))
    return jnp.where(mode <= 2 * count, value, 0.0)


def harmonics_kernel(total, orders, after, front, back, out):
    blocks, planes, _, lanes = front.shape
    mode = lax.broadcasted_iota(jnp.int32, (MODES, planes), 0)
    position = lax.broadcasted_iota(jnp.int32, (MODES, planes), 1) + lax.axis_index("mesh") * planes
    basis = turns(position, mode, orders, total) * jnp.where(mode == 0, 1.0 / total, 2.0 / total)
    rotor = lax.axis_index("row") == 0
    for b in range(blocks):
        edge = jnp.where(rotor, back[b, :, 7, :], front[b, :, 0, :])
        out[:, b * lanes : (b + 1) * lanes] = jnp.dot(
            basis, edge, precision=lax.Precision.HIGHEST, preferred_element_type=jnp.float32
        )


def mix_kernel(scalars, own, up, down, far, after, *outs):
    weight = [scalars[k] for k in range(INST)]
    cosine, sine = scalars[INST], scalars[INST + 1]
    at = jnp.where(lax.axis_index("mesh") == 0, 1, 0)
    first = up.shape[2] - 2

    def mixed(var):
        u = [own[s, var, at] for s in range(2)]
        u += [r[s, var, first + at] for r in (up, far, down) for s in range(2)]
        sums = []
        for a in range(INST):
            total = weight[a % INST] * u[0]
            for b in range(1, INST):
                total = total + weight[(a - b) % INST] * u[b]
            sums.append(total)
        return sums

    half = INST // 2

    def put(var, values):
        for a, value in enumerate(values):
            outs[a // half][a % half, var] = value

    for var in (0, 1, 4, 5):
        put(var, mixed(var))
    v, w = mixed(2), mixed(3)
    put(2, [cosine * x - sine * y for x, y in zip(v, w)])
    put(3, [sine * x + cosine * y for x, y in zip(v, w)])


def source_kernel(rims, start, scalars, *refs):
    outs, refs = refs[-4:], refs[:-4]
    if rims:
        *ghost, nu = refs[-3:]
        refs = refs[:-3]
    own, up, down, far = refs
    at_once, size = outs[0].shape[1:3]
    block = pl.program_id(0) * at_once
    ratio = scalars[0]
    c1, c2, c3 = (ratio * D1, ratio * D2, ratio * D3)
    out_own, out_up, out_down, out_far = outs
    order = (out_own, out_up, out_far, out_down)
    for var in range(at_once):
        for p in range(size):
            u = [own[s, var, start + p] for s in range(2)]
            u += [r[s, block + var, start + p] for r in (up, far, down) for s in range(2)]
            near = [u[(n - 1) % INST] - u[(n + 1) % INST] for n in range(INST)]
            second = [c2 * (u[(n - 2) % INST] - u[(n + 2) % INST]) for n in range(4)]
            for n in range(INST):
                s = c1 * near[n] - c3 * near[(n + 4) % INST]
                s = s + second[n] if n < 4 else s - second[n - 4]
                order[n // 2][n % 2, var, p] = s
    if not rims:
        return

    def add_ghost(p, factor):
        for var in range(at_once):
            for n in range(INST):
                at = (n % 2, var, p)
                order[n // 2][at] = order[n // 2][at] - factor * ghost[n // 4][n % 4, block + var]

    place = pl.ds(pl.multiple_of(lax.axis_index("inst") * 16, 16), 16)

    @pl.when(lax.axis_index("mesh") == 0)
    def _():
        add_ghost(size - 1, nu[0, place, :] + 0.5)

    @pl.when(lax.axis_index("mesh") == lax.axis_size("mesh") - 1)
    def _():
        add_ghost(size - 2, nu[nu.shape[0] - 1, place, :])


def stencil_kernel(nu, low, high, field, one, two):
    blocks, planes, rows, lanes = field.shape
    lane = lax.broadcasted_iota(jnp.int32, (rows, lanes), 1)
    row = lax.broadcasted_iota(jnp.int32, (rows, lanes), 0)
    for b in range(blocks):
        for p in range(planes):
            u = field[b, p]
            before = low[b] if p == 0 else field[b, p - 1]
            after = high[b] if p == planes - 1 else field[b, p + 1]
            left = jnp.where(lane == 0, 0.0, pltpu.roll(u, 1, 1))
            right = jnp.where(lane == lanes - 1, 0.0, pltpu.roll(u, lanes - 1, 1))
            above = jnp.where(row == 0, 0.0, pltpu.roll(u, 1, 0))
            below = jnp.where(row == rows - 1, 0.0, pltpu.roll(u, rows - 1, 0))
            lap = (before + after) + (above + below) + (left + right) - 6.0 * u
            at = (p - 1) % planes
            out, at = (one, at) if at < OUTER else (two, at - OUTER)
            out[b, at] = nu[p] * lap - (u - above) - 0.5 * (u - before)


def add_kernel(one, two, after, out):
    out[...] = one[...] + two[...]


def edge_kernel(total, orders, one, two, nu, *rest):
    out = rest[-1]
    planes, blocks, rows, lanes = out.shape
    mode = lax.broadcasted_iota(jnp.int32, (planes, MODES), 1)
    position = lax.broadcasted_iota(jnp.int32, (planes, MODES), 0) + lax.axis_index("mesh") * planes
    ghost = jnp.dot(
        turns(position, mode, orders, total),
        one[...] + two[...],
        precision=lax.Precision.HIGHEST,
        preferred_element_type=jnp.float32,
    )
    rotor = lax.axis_index("row") == 0
    hit = lax.broadcasted_iota(jnp.int32, (rows, lanes), 0) == jnp.where(rotor, rows - 1, 0)
    for p in range(planes):
        facing = jnp.where(rotor, nu[p, nu.shape[1] - 1 :, :], nu[p, :1, :] + 1.0)
        for b in range(blocks):
            value = facing * ghost[p : p + 1, b * lanes : (b + 1) * lanes]
            out[p, b] = jnp.where(hit, value, 0.0)


def final_kernel(start, chunk, near, inverse, edge, field, pre, *rest):
    new, residual, new_held, residual_held = rest[-6 - 2 * (not near) : -2 - 2 * (not near)]
    sems_in, sems = rest[-2:]
    count, planes, rows, lanes = field.shape
    size = pre.shape[1]
    base = (start + 1) % planes
    inst = lax.axis_index("inst")
    steps = (0, 1, 3, 2)
    arrivals = []
    if not near:
        held_in, pieces = rest[-4:-2]
    for b in range(0, count, chunk):
        if near:
            arrivals.append([])
            continue
        part = slice(b, b + chunk)
        pairs = [(pre.at[part], held_in.at[part])]
        pairs += [
            (rest[k].at[part], pieces.at[lax.rem(inst + step, 4), part])
            for k, step in enumerate(steps)
        ]
        arrivals.append(
            [
                pltpu.make_async_copy(x, y, sems_in.at[b // chunk, k])
                for k, (x, y) in enumerate(pairs)
            ]
        )
        for one in arrivals[-1]:
            one.start()
    tile = pl.ds(pl.multiple_of((1 - lax.axis_index("row")) * (rows - 8), 8), 8)
    runs = [(0, base, min(size, planes - base))]
    if base + size > planes:
        runs.append((planes - base, 0, base + size - planes))
    copies = []
    for j in range(0, count, 2):
        if j % chunk == 0:
            for one in arrivals[j // chunk]:
                one.wait()
        for p in range(size):
            plane = (base + p) % planes
            for b in (j, j + 1):
                for k, step in enumerate(steps):
                    if near:
                        at = pl.ds(pl.multiple_of(16 * lax.rem(inst + step, 4), 16), 16)
                        residual_held[b, p, at] = pre[b, p, at] - rest[k][b, p]
                    else:
                        at = pl.ds(16 * k, 16)
                        residual_held[b, p, at] = held_in[b, p, at] - pieces[k, b, p]
                residual_held[b, p, tile] = residual_held[b, p, tile] + edge[plane, b]
            high, low = split_bf16(
                jnp.concatenate([residual_held[j, p], residual_held[j + 1, p]], 1)
            )
            change = jnp.dot(
                inverse[...],
                jnp.concatenate([high, high, low], 0),
                preferred_element_type=jnp.float32,
            )
            new_held[j, p] = field[j, plane] + change[:, :lanes]
            new_held[j + 1, p] = field[j + 1, plane] + change[:, lanes:]
        if (j + 2) % chunk == 0:
            part = slice(j + 2 - chunk, j + 2)
            for held, out in ((residual_held, residual), (new_held, new)):
                for source, target, length in runs:
                    copies.append(
                        pltpu.make_async_copy(
                            held.at[part, source : source + length],
                            out.at[part, target : target + length],
                            sems.at[len(copies)],
                        )
                    )
                    copies[-1].start()
    for one in copies:
        one.wait()


def lag_weights(lag):
    delta = jnp.arange(INST).astype(jnp.float32) - lag
    total = 1.0 + jnp.cos(math.pi * delta)
    for k in range(1, INST // 2):
        total = total + 2.0 * jnp.cos(2.0 * math.pi * k / INST * delta)
    return total / INST


def local(state, viscosity, blade_counts, mode_orders):
    _, local_inst, variables, planes, rows, lanes = state.shape
    quarter = rows // 4
    blocks = local_inst * variables
    mesh_count = lax.axis_size("mesh")
    total = planes * mesh_count
    which = lax.axis_index("row")
    inst = lax.axis_index("inst")
    mesh_idx = lax.axis_index("mesh")
    counts = blade_counts.astype(jnp.float32)
    ratio = counts[1 - which] / counts[which]
    angle = 2.0 * math.pi / counts[which]
    field = state.reshape(blocks, planes, rows, lanes)
    nu = viscosity[0]
    first = mesh_idx == 0
    last = mesh_idx == mesh_count - 1

    def along(x, step):
        return lax.ppermute(x, "inst", [(j, (j + step) % 4) for j in range(4)])

    def in_hbm(*arrays):
        return [pltpu.with_memory_space_constraint(x, pltpu.HBM) for x in arrays]

    def in_vmem(*arrays):
        return [pltpu.with_memory_space_constraint(x, pltpu.VMEM) for x in arrays]

    def exchange(up, down, far):
        from_down, from_up, from_far = along(up, 1), along(down, 3), along(far, 2)
        return from_up, from_down, from_far

    packed = pack(field, ((1, planes - 1), (0, 1)))
    gathered = exchange(*packed)

    top, bottom, own = pl.pallas_call(
        edges_kernel,
        out_shape=(shaped(blocks, rows, lanes),) * 2 + (shaped(blocks, planes, quarter, lanes),),
        in_specs=[HBM, VMEM],
        out_specs=(VMEM,) * 3,
        scratch_shapes=[pltpu.SemaphoreType.DMA((3, blocks))],
        compiler_params=params(),
        cost_estimate=cost(),
    )(pltpu.with_memory_space_constraint(field, pltpu.HBM), packed[0])
    low = lax.ppermute(top, "mesh", [(j, j + 1) for j in range(mesh_count - 1)])
    high = lax.ppermute(bottom, "mesh", [(j + 1, j) for j in range(mesh_count - 1)])

    split = (local_inst, variables)
    own, *theirs = (x.reshape(*split, planes, quarter, lanes) for x in (own, *gathered))
    all_quarters = (*in_hbm(own), *in_vmem(*theirs))

    whole = shaped(*field.shape)
    at_once = 2
    slab = pl.BlockSpec((at_once, planes, rows, lanes), lambda b: (b, 0, 0, 0))
    plane = pl.BlockSpec((at_once, rows, lanes), lambda b: (b, 0, 0))
    pre_one, pre_two = pl.pallas_call(
        stencil_kernel,
        grid=(blocks // at_once,),
        out_shape=(
            pltpu.HBM((blocks, OUTER, rows, lanes), jnp.float32),
            pltpu.HBM((blocks, planes - OUTER, rows, lanes), jnp.float32),
        ),
        in_specs=[pl.BlockSpec((planes, rows, lanes), lambda b: (0, 0, 0)), plane, plane, slab],
        out_specs=(
            pl.BlockSpec((at_once, OUTER, rows, lanes), lambda b: (b, 0, 0, 0)),
            pl.BlockSpec((at_once, planes - OUTER, rows, lanes), lambda b: (b, 0, 0, 0)),
        ),
        compiler_params=params(),
        cost_estimate=cost(),
    )(nu, *in_hbm(low, high), field)

    harmonics = pl.pallas_call(
        functools.partial(harmonics_kernel, total),
        out_shape=shaped(MODES, blocks * lanes),
        grid=(1,),
        in_specs=[
            SMEM,
            VMEM,
            pl.BlockSpec((blocks, planes, 8, lanes), lambda b: (0, 0, 0, 0)),
            pl.BlockSpec((blocks, planes, 8, lanes), lambda b: (0, 0, rows // 8 - 1, 0)),
        ],
        out_specs=pl.BlockSpec((MODES, blocks * lanes), lambda b: (0, 0)),
        compiler_params=params(),
        cost_estimate=cost(),
    )(mode_orders, packed[0], field, field)

    def crossing(flip):
        return [
            (r * mesh_count + m, (1 - r) * mesh_count + (m ^ flip))
            for r in range(2)
            for m in range(mesh_count)
        ]

    def doubled(x, flip):
        return x + lax.ppermute(x, "mesh", [(m, m ^ flip) for m in range(mesh_count)])

    two_ways = [lax.ppermute(harmonics, ("row", "mesh"), crossing(flip)) for flip in (0, 1)]
    harmonics = two_ways[0] + two_ways[1]
    early = lax.ppermute(harmonics, "mesh", [(m, m ^ 2) for m in range(mesh_count)])

    def sources(start, size, rims, after=()):
        at_once = 2

        def kernel(*refs):
            inputs, outputs = refs[: -4 - len(after)], refs[-4:]
            source_kernel(bool(rims), start, *inputs, *outputs)

        outs = pl.pallas_call(
            kernel,
            out_shape=(pltpu.HBM((*split, size, quarter, lanes), jnp.float32),) * 4,
            grid=(variables // at_once,),
            in_specs=[
                SMEM,
                pl.BlockSpec((2, at_once, planes, quarter, lanes), lambda b: (0, b, 0, 0, 0)),
            ]
            + [VMEM] * (3 + len(rims))
            + [ANY] * len(after),
            out_specs=(
                pl.BlockSpec((2, at_once, size, quarter, lanes), lambda b: (0, b, 0, 0, 0)),
            )
            * 4,
            compiler_params=params(),
            cost_estimate=cost(),
        )(ratio[None], *all_quarters, *rims, *after)
        own, up, down, far = (x.reshape(blocks, size, quarter, lanes) for x in outs)
        return (own, *exchange(up, down, far))

    one_source = sources(0, OUTER, (), after=(*in_hbm(pre_one), early))

    weights = lag_weights(jnp.where(first, -ratio, ratio))
    turn = jnp.where(first, angle, -angle)
    ghost_shape = shaped(INST // 2, variables, quarter, lanes)

    ghost_out = pl.pallas_call(
        mix_kernel,
        out_shape=(ghost_shape,) * 2,
        grid=(1,),
        in_specs=[
            SMEM,
            pl.BlockSpec((2, variables, 2, quarter, lanes), lambda b: (0, 0, planes // 2 - 1, 0, 0)),
        ]
        + [VMEM] * 3
        + [ANY],
        out_specs=(VMEM,) * 2,
        compiler_params=params(),
        cost_estimate=cost(),
    )(
        jnp.concatenate([weights, jnp.stack([jnp.cos(turn), jnp.sin(turn)])]),
        *all_quarters,
        *in_hbm(one_source[0]),
    )
    ghost = [
        lax.ppermute(part, "mesh", [(mesh_count - 1, 0), (0, mesh_count - 1)]) for part in ghost_out
    ]

    harmonics = pl.pallas_call(
        add_kernel,
        out_shape=harmonics,
        in_specs=[VMEM, VMEM, ANY],
        out_specs=VMEM,
        compiler_params=params(),
        cost_estimate=cost(),
    )(harmonics, early, ghost_out[0])
    harmonics = doubled(harmonics, 4)
    opposite = lax.ppermute(harmonics, "mesh", [(m, m ^ 8) for m in range(mesh_count)])
    two_source = sources(OUTER, planes - OUTER, (*ghost, nu), after=(opposite,))

    edge = pl.pallas_call(
        functools.partial(edge_kernel, total),
        out_shape=shaped(planes, blocks, 8, lanes),
        in_specs=[SMEM, VMEM, VMEM, VMEM] + [ANY] * 3,
        out_specs=VMEM,
        compiler_params=params(),
        cost_estimate=cost(),
    )(
        mode_orders,
        harmonics,
        opposite,
        nu,
        *one_source[1:],
    )

    inverse = jnp.asarray(inverse_parts(rows))
    kept = ()
    for start, size, group, pre in ((0, OUTER, one_source, pre_one), (OUTER, planes - OUTER, two_source, pre_two)):
        given = 4 + len(group)
        near = size < 4
        if near:
            group = in_vmem(*group)
            given_in = (pre, *group)
        else:
            given_in = (*in_hbm(pre, group[0]), *group[1:])
        kept = pl.pallas_call(
            functools.partial(final_kernel, start, 4 if near else 2, near),
            out_shape=(pltpu.HBM(field.shape, jnp.float32),) * 2,
            in_specs=[VMEM] * 3
            + ([VMEM] * 5 if near else [HBM] * 2 + [ANY] * 3)
            + [HBM] * len(kept),
            out_specs=(HBM,) * 2,
            scratch_shapes=[pltpu.VMEM((blocks, size, rows, lanes), jnp.float32)] * (2 + (not near))
            + [pltpu.VMEM((4, blocks, size, quarter, lanes), jnp.float32)] * (not near)
            + [pltpu.SemaphoreType.DMA((blocks, 5)), pltpu.SemaphoreType.DMA((4 * blocks,))],
            input_output_aliases={given: 0, given + 1: 1} if kept else {},
            compiler_params=params(),
            cost_estimate=cost(),
        )(inverse, edge, field, *given_in, *kept)
    new, residual = kept
    return (new.reshape(state.shape), residual.reshape(state.shape))


def solution(mesh):
    spread = P("row", "inst", None, "mesh", None, None)
    return jax.shard_map(
        local,
        mesh=mesh,
        in_specs=(spread, P("row", "mesh", None, None), P(), P()),
        out_specs=(spread, spread),
        check_vma=False,
    )
```

```python
import functools
import math

import numpy as np

import jax
import jax.numpy as jnp
from jax import lax
from jax.experimental import pallas as pl
from jax.experimental.pallas import tpu as pltpu
from jax.sharding import PartitionSpec as P

INST = 8
OUTER = 6
MODES = 24
LIMIT = 14 * 1024 * 1024
VMEM = pl.BlockSpec(memory_space=pltpu.VMEM)
SMEM = pl.BlockSpec(memory_space=pltpu.SMEM)
ANY = pl.BlockSpec(memory_space=pl.ANY)
HBM = pl.BlockSpec(memory_space=pltpu.HBM)
D1 = -0.5 / math.tan(math.pi / 8)
D2 = 0.5 / math.tan(math.pi / 4)
D3 = -0.5 / math.tan(3 * math.pi / 8)


def shaped(*dims):
    return jax.ShapeDtypeStruct(dims, jnp.float32)


def cost():
    return pl.CostEstimate(flops=1, bytes_accessed=1, transcendentals=0)


def inverse_parts(length):
    steps = np.arange(1, length + 1).astype(np.float64)
    basis = math.sqrt(2.0 / (length + 1)) * np.sin(
        math.pi * steps[:, None] * steps[None, :] / (length + 1)
    )
    eigen = 2.0 - np.cos(math.pi * steps / (length + 1))
    inverse = (0.2 * (basis / eigen[None, :]) @ basis.T).astype(np.float32)
    high = inverse.astype(jnp.bfloat16)
    low = (inverse - high.astype(np.float32)).astype(jnp.bfloat16)
    return np.concatenate([high, low, high], axis=1)


def split_bf16(x):
    high = x.astype(jnp.bfloat16)
    return high, (x - high.astype(jnp.float32)).astype(jnp.bfloat16)


def params():
    return pltpu.CompilerParams(vmem_limit_bytes=LIMIT)


def pack_kernel(planes, field, *rest):
    sems = rest[-1]
    copies = []

    def copy(source, target):
        one = pltpu.make_async_copy(source, target, sems.at[len(copies)])
        one.start()
        copies.append(one)

    outs = rest[:3]
    for k, out in zip((1, 3, 2), outs):
        place = lax.rem(lax.axis_index("inst") + k, 4) * 16
        rows = pl.ds(pl.multiple_of(place, 16), 16)
        done = 0
        for start, size in planes:
            for b in range(0, field.shape[0], 4):
                copy(
                    field.at[b : b + 4, start : start + size, rows, :],
                    out.at[b : b + 4, done : done + size],
                )
            done += size
    for one in copies:
        one.wait()


def edges_kernel(field, after, top, bottom, own, sems):
    rows = pl.ds(pl.multiple_of(lax.axis_index("inst") * 16, 16), 16)
    copies = [
        pltpu.make_async_copy(field.at[b, plane], out.at[b], sems.at[k, b])
        for k, (plane, out) in enumerate(((field.shape[1] - 1, top), (0, bottom)))
        for b in range(field.shape[0])
    ]
    last = field.shape[1] - 1
    copies.append(
        pltpu.make_async_copy(field.at[:, 1:, rows, :], own.at[:, :last], sems.at[2, 0])
    )
    copies.append(
        pltpu.make_async_copy(field.at[:, :1, rows, :], own.at[:, last:], sems.at[2, 1])
    )
    for one in copies:
        one.start()
    for one in copies:
        one.wait()


def pack(field, planes):
    blocks, _, rows, lanes = field.shape
    size = sum(size for _, size in planes)
    return pl.pallas_call(
        functools.partial(pack_kernel, planes),
        out_shape=(shaped(blocks, size, rows // 4, lanes),) * 3,
        in_specs=[HBM],
        out_specs=(VMEM,) * 3,
        scratch_shapes=[pltpu.SemaphoreType.DMA((32,))],
        compiler_params=params(),
        cost_estimate=cost(),
    )(pltpu.with_memory_space_constraint(field, pltpu.HBM))


def turns(position, mode, orders, total):
    order = jnp.zeros(mode.shape, jnp.int32)
    count = orders.shape[0]
    for j in range(count):
        order = jnp.where((mode == 1 + j) | (mode == 1 + count + j), orders[j], order)
    phase = lax.rem(position * order, total).astype(jnp.float32) * (2.0 * math.pi / total)
    value = jnp.where(mode <= count, jnp.cos(phase), jnp.sin(phase))
    return jnp.where(mode <= 2 * count, value, 0.0)


def harmonics_kernel(total, orders, after, front, back, out):
    blocks, planes, _, lanes = front.shape
    mode = lax.broadcasted_iota(jnp.int32, (MODES, planes), 0)
    position = lax.broadcasted_iota(jnp.int32, (MODES, planes), 1) + lax.axis_index("mesh") * planes
    basis = turns(position, mode, orders, total) * jnp.where(mode == 0, 1.0 / total, 2.0 / total)
    rotor = lax.axis_index("row") == 0
    for b in range(blocks):
        edge = jnp.where(rotor, back[b, :, 7, :], front[b, :, 0, :])
        out[:, b * lanes : (b + 1) * lanes] = jnp.dot(
            basis, edge, precision=lax.Precision.HIGHEST, preferred_element_type=jnp.float32
        )


def mix_kernel(scalars, own, up, down, far, after, *outs):
    weight = [scalars[k] for k in range(INST)]
    cosine, sine = scalars[INST], scalars[INST + 1]
    at = jnp.where(lax.axis_index("mesh") == 0, 1, 0)

    def mixed(var):
        u = [r[s, var, at] for r in (own, up, far, down) for s in range(2)]
        sums = []
        for a in range(INST):
            total = weight[a % INST] * u[0]
            for b in range(1, INST):
                total = total + weight[(a - b) % INST] * u[b]
            sums.append(total)
        return sums

    half = INST // 2

    def put(var, values):
        for a, value in enumerate(values):
            outs[a // half][a % half, var] = value

    for var in (0, 1, 4, 5):
        put(var, mixed(var))
    v, w = mixed(2), mixed(3)
    put(2, [cosine * x - sine * y for x, y in zip(v, w)])
    put(3, [sine * x + cosine * y for x, y in zip(v, w)])


def source_kernel(rims, scalars, *refs):
    outs, refs = refs[-4:], refs[:-4]
    if rims:
        *ghost, nu = refs[-3:]
        refs = refs[:-3]
    own, up, down, far = refs
    size = up.shape[2]
    ratio = scalars[0]
    c1, c2, c3 = (ratio * D1, ratio * D2, ratio * D3)
    out_own, out_up, out_down, out_far = outs
    order = (out_own, out_up, out_far, out_down)
    for var in range(up.shape[1]):
        for p in range(size):
            u = [r[s, var, p] for r in (own, up, far, down) for s in range(2)]
            near = [u[(n - 1) % INST] - u[(n + 1) % INST] for n in range(INST)]
            second = [c2 * (u[(n - 2) % INST] - u[(n + 2) % INST]) for n in range(4)]
            for n in range(INST):
                s = c1 * near[n] - c3 * near[(n + 4) % INST]
                s = s + second[n] if n < 4 else s - second[n - 4]
                order[n // 2][n % 2, var, p] = s
    if not rims:
        return

    def add_ghost(p, factor):
        for var in range(up.shape[1]):
            for n in range(INST):
                at = (n % 2, var, p)
                order[n // 2][at] = order[n // 2][at] - factor * ghost[n // 4][n % 4, var]

    place = pl.ds(pl.multiple_of(lax.axis_index("inst") * 16, 16), 16)

    @pl.when(lax.axis_index("mesh") == 0)
    def _():
        add_ghost(size - 1, nu[0, place, :] + 0.5)

    @pl.when(lax.axis_index("mesh") == lax.axis_size("mesh") - 1)
    def _():
        add_ghost(size - 2, nu[nu.shape[0] - 1, place, :])


def stencil_kernel(nu, low, high, field, one, two):
    blocks, planes, rows, lanes = field.shape
    lane = lax.broadcasted_iota(jnp.int32, (rows, lanes), 1)
    row = lax.broadcasted_iota(jnp.int32, (rows, lanes), 0)
    for b in range(blocks):
        for p in range(planes):
            u = field[b, p]
            before = low[b] if p == 0 else field[b, p - 1]
            after = high[b] if p == planes - 1 else field[b, p + 1]
            left = jnp.where(lane == 0, 0.0, pltpu.roll(u, 1, 1))
            right = jnp.where(lane == lanes - 1, 0.0, pltpu.roll(u, lanes - 1, 1))
            above = jnp.where(row == 0, 0.0, pltpu.roll(u, 1, 0))
            below = jnp.where(row == rows - 1, 0.0, pltpu.roll(u, rows - 1, 0))
            lap = (before + after) + (above + below) + (left + right) - 6.0 * u
            at = (p - 1) % planes
            out, at = (one, at) if at < OUTER else (two, at - OUTER)
            out[b, at] = nu[p] * lap - (u - above) - 0.5 * (u - before)


def add_kernel(one, two, after, out):
    out[...] = one[...] + two[...]


def edge_kernel(total, orders, one, two, nu, *rest):
    out = rest[-1]
    planes, blocks, rows, lanes = out.shape
    mode = lax.broadcasted_iota(jnp.int32, (planes, MODES), 1)
    position = lax.broadcasted_iota(jnp.int32, (planes, MODES), 0) + lax.axis_index("mesh") * planes
    ghost = jnp.dot(
        turns(position, mode, orders, total),
        one[...] + two[...],
        precision=lax.Precision.HIGHEST,
        preferred_element_type=jnp.float32,
    )
    rotor = lax.axis_index("row") == 0
    hit = lax.broadcasted_iota(jnp.int32, (rows, lanes), 0) == jnp.where(rotor, rows - 1, 0)
    for p in range(planes):
        facing = jnp.where(rotor, nu[p, nu.shape[1] - 1 :, :], nu[p, :1, :] + 1.0)
        for b in range(blocks):
            value = facing * ghost[p : p + 1, b * lanes : (b + 1) * lanes]
            out[p, b] = jnp.where(hit, value, 0.0)


def final_kernel(start, chunk, near, inverse, edge, field, pre, *rest):
    new, residual, new_held, residual_held = rest[-6 - 2 * (not near) : -2 - 2 * (not near)]
    sems_in, sems = rest[-2:]
    count, planes, rows, lanes = field.shape
    size = pre.shape[1]
    base = (start + 1) % planes
    inst = lax.axis_index("inst")
    steps = (0, 1, 3, 2)
    arrivals = []
    if not near:
        held_in, pieces = rest[-4:-2]
    for b in range(0, count, chunk):
        if near:
            arrivals.append([])
            continue
        part = slice(b, b + chunk)
        pairs = [(pre.at[part], held_in.at[part])]
        pairs += [
            (rest[k].at[part], pieces.at[lax.rem(inst + step, 4), part])
            for k, step in enumerate(steps)
        ]
        arrivals.append(
            [
                pltpu.make_async_copy(x, y, sems_in.at[b // chunk, k])
                for k, (x, y) in enumerate(pairs)
            ]
        )
        for one in arrivals[-1]:
            one.start()
    tile = pl.ds(pl.multiple_of((1 - lax.axis_index("row")) * (rows - 8), 8), 8)
    runs = [(0, base, min(size, planes - base))]
    if base + size > planes:
        runs.append((planes - base, 0, base + size - planes))
    copies = []
    for j in range(0, count, 2):
        if j % chunk == 0:
            for one in arrivals[j // chunk]:
                one.wait()
        for p in range(size):
            plane = (base + p) % planes
            for b in (j, j + 1):
                for k, step in enumerate(steps):
                    if near:
                        at = pl.ds(pl.multiple_of(16 * lax.rem(inst + step, 4), 16), 16)
                        residual_held[b, p, at] = pre[b, p, at] - rest[k][b, p]
                    else:
                        at = pl.ds(16 * k, 16)
                        residual_held[b, p, at] = held_in[b, p, at] - pieces[k, b, p]
                residual_held[b, p, tile] = residual_held[b, p, tile] + edge[plane, b]
            high, low = split_bf16(
                jnp.concatenate([residual_held[j, p], residual_held[j + 1, p]], 1)
            )
            change = jnp.dot(
                inverse[...],
                jnp.concatenate([high, high, low], 0),
                preferred_element_type=jnp.float32,
            )
            new_held[j, p] = field[j, plane] + change[:, :lanes]
            new_held[j + 1, p] = field[j + 1, plane] + change[:, lanes:]
        if (j + 2) % chunk == 0:
            part = slice(j + 2 - chunk, j + 2)
            for held, out in ((residual_held, residual), (new_held, new)):
                for source, target, length in runs:
                    copies.append(
                        pltpu.make_async_copy(
                            held.at[part, source : source + length],
                            out.at[part, target : target + length],
                            sems.at[len(copies)],
                        )
                    )
                    copies[-1].start()
    for one in copies:
        one.wait()


def lag_weights(lag):
    delta = jnp.arange(INST).astype(jnp.float32) - lag
    total = 1.0 + jnp.cos(math.pi * delta)
    for k in range(1, INST // 2):
        total = total + 2.0 * jnp.cos(2.0 * math.pi * k / INST * delta)
    return total / INST


def local(state, viscosity, blade_counts, mode_orders):
    _, local_inst, variables, planes, rows, lanes = state.shape
    quarter = rows // 4
    blocks = local_inst * variables
    mesh_count = lax.axis_size("mesh")
    total = planes * mesh_count
    which = lax.axis_index("row")
    inst = lax.axis_index("inst")
    mesh_idx = lax.axis_index("mesh")
    counts = blade_counts.astype(jnp.float32)
    ratio = counts[1 - which] / counts[which]
    angle = 2.0 * math.pi / counts[which]
    field = state.reshape(blocks, planes, rows, lanes)
    nu = viscosity[0]
    first = mesh_idx == 0
    last = mesh_idx == mesh_count - 1

    def along(x, step):
        return lax.ppermute(x, "inst", [(j, (j + step) % 4) for j in range(4)])

    def in_hbm(*arrays):
        return [pltpu.with_memory_space_constraint(x, pltpu.HBM) for x in arrays]

    def exchange(up, down, far):
        from_down, from_up, from_far = along(up, 1), along(down, 3), along(far, 2)
        return from_up, from_down, from_far

    packed = pack(field, ((1, planes - 1), (0, 1)))
    gathered = exchange(*packed)

    top, bottom, own = pl.pallas_call(
        edges_kernel,
        out_shape=(shaped(blocks, rows, lanes),) * 2 + (shaped(blocks, planes, quarter, lanes),),
        in_specs=[HBM, VMEM],
        out_specs=(VMEM,) * 3,
        scratch_shapes=[pltpu.SemaphoreType.DMA((3, blocks))],
        compiler_params=params(),
        cost_estimate=cost(),
    )(pltpu.with_memory_space_constraint(field, pltpu.HBM), packed[0])
    low = lax.ppermute(top, "mesh", [(j, j + 1) for j in range(mesh_count - 1)])
    high = lax.ppermute(bottom, "mesh", [(j + 1, j) for j in range(mesh_count - 1)])

    split = (local_inst, variables)
    all_quarters = in_hbm(*(x.reshape(*split, planes, quarter, lanes) for x in (own, *gathered)))

    whole = shaped(*field.shape)
    at_once = 2
    slab = pl.BlockSpec((at_once, planes, rows, lanes), lambda b: (b, 0, 0, 0))
    plane = pl.BlockSpec((at_once, rows, lanes), lambda b: (b, 0, 0))
    pre_one, pre_two = pl.pallas_call(
        stencil_kernel,
        grid=(blocks // at_once,),
        out_shape=(
            pltpu.HBM((blocks, OUTER, rows, lanes), jnp.float32),
            pltpu.HBM((blocks, planes - OUTER, rows, lanes), jnp.float32),
        ),
        in_specs=[pl.BlockSpec((planes, rows, lanes), lambda b: (0, 0, 0)), plane, plane, slab],
        out_specs=(
            pl.BlockSpec((at_once, OUTER, rows, lanes), lambda b: (b, 0, 0, 0)),
            pl.BlockSpec((at_once, planes - OUTER, rows, lanes), lambda b: (b, 0, 0, 0)),
        ),
        compiler_params=params(),
        cost_estimate=cost(),
    )(nu, *in_hbm(low, high), field)

    harmonics = pl.pallas_call(
        functools.partial(harmonics_kernel, total),
        out_shape=shaped(MODES, blocks * lanes),
        grid=(1,),
        in_specs=[
            SMEM,
            VMEM,
            pl.BlockSpec((blocks, planes, 8, lanes), lambda b: (0, 0, 0, 0)),
            pl.BlockSpec((blocks, planes, 8, lanes), lambda b: (0, 0, rows // 8 - 1, 0)),
        ],
        out_specs=pl.BlockSpec((MODES, blocks * lanes), lambda b: (0, 0)),
        compiler_params=params(),
        cost_estimate=cost(),
    )(mode_orders, packed[0], field, field)

    def crossing(flip):
        return [
            (r * mesh_count + m, (1 - r) * mesh_count + (m ^ flip))
            for r in range(2)
            for m in range(mesh_count)
        ]

    def doubled(x, flip):
        return x + lax.ppermute(x, "mesh", [(m, m ^ flip) for m in range(mesh_count)])

    two_ways = [lax.ppermute(harmonics, ("row", "mesh"), crossing(flip)) for flip in (0, 1)]
    harmonics = two_ways[0] + two_ways[1]
    early = lax.ppermute(harmonics, "mesh", [(m, m ^ 2) for m in range(mesh_count)])

    def sources(start, size, rims, after=()):
        at_once = 3
        piece_in = pl.BlockSpec(
            (2, at_once, size, quarter, lanes), lambda b: (0, b, start // size, 0, 0)
        )
        rim_specs = [
            pl.BlockSpec((INST // 2, at_once, quarter, lanes), lambda b: (0, b, 0, 0)),
            pl.BlockSpec((INST // 2, at_once, quarter, lanes), lambda b: (0, b, 0, 0)),
            pl.BlockSpec((planes, rows, lanes), lambda b: (0, 0, 0)),
        ]
        def kernel(*refs):
            inputs, outputs = refs[: -4 - len(after)], refs[-4:]
            source_kernel(bool(rims), *inputs, *outputs)

        outs = pl.pallas_call(
            kernel,
            out_shape=(pltpu.HBM((*split, size, quarter, lanes), jnp.float32),) * 4,
            grid=(variables // at_once,),
            in_specs=[SMEM] + [piece_in] * 4 + rim_specs[: len(rims)] + [ANY] * len(after),
            out_specs=(
                pl.BlockSpec((2, at_once, size, quarter, lanes), lambda b: (0, b, 0, 0, 0)),
            )
            * 4,
            compiler_params=params(),
            cost_estimate=cost(),
        )(ratio[None], *all_quarters, *rims, *after)
        own, up, down, far = (x.reshape(blocks, size, quarter, lanes) for x in outs)
        return (own, *exchange(up, down, far))

    one_source = sources(0, OUTER, (), after=(*in_hbm(pre_one), early))

    weights = lag_weights(jnp.where(first, -ratio, ratio))
    turn = jnp.where(first, angle, -angle)
    ghost_shape = shaped(INST // 2, variables, quarter, lanes)

    outermost = pl.BlockSpec((2, variables, 2, quarter, lanes), lambda b: (0, 0, 3, 0, 0))
    ghost_out = pl.pallas_call(
        mix_kernel,
        out_shape=(ghost_shape,) * 2,
        grid=(1,),
        in_specs=[SMEM] + [outermost] * 4 + [ANY],
        out_specs=(pl.BlockSpec(ghost_shape.shape, lambda b: (0, 0, 0, 0)),) * 2,
        compiler_params=params(),
        cost_estimate=cost(),
    )(
        jnp.concatenate([weights, jnp.stack([jnp.cos(turn), jnp.sin(turn)])]),
        *all_quarters,
        *in_hbm(one_source[0]),
    )
    ghost = [
        lax.ppermute(part, "mesh", [(mesh_count - 1, 0), (0, mesh_count - 1)]) for part in ghost_out
    ]

    harmonics = pl.pallas_call(
        add_kernel,
        out_shape=harmonics,
        in_specs=[VMEM, VMEM, ANY],
        out_specs=VMEM,
        compiler_params=params(),
        cost_estimate=cost(),
    )(harmonics, early, ghost_out[0])
    harmonics = doubled(harmonics, 4)
    opposite = lax.ppermute(harmonics, "mesh", [(m, m ^ 8) for m in range(mesh_count)])
    two_source = sources(OUTER, planes - OUTER, (*ghost, nu), after=(opposite,))

    edge = pl.pallas_call(
        functools.partial(edge_kernel, total),
        out_shape=shaped(planes, blocks, 8, lanes),
        in_specs=[SMEM, VMEM, VMEM, VMEM] + [ANY] * 3,
        out_specs=VMEM,
        compiler_params=params(),
        cost_estimate=cost(),
    )(
        mode_orders,
        harmonics,
        opposite,
        nu,
        *one_source[1:],
    )

    inverse = jnp.asarray(inverse_parts(rows))
    kept = ()
    for start, size, group, pre in ((0, OUTER, one_source, pre_one), (OUTER, planes - OUTER, two_source, pre_two)):
        given = 4 + len(group)
        near = size < 4
        if near:
            group = [pltpu.with_memory_space_constraint(x, pltpu.VMEM) for x in group]
            given_in = (pre, *group)
        else:
            given_in = (*in_hbm(pre, group[0]), *group[1:])
        kept = pl.pallas_call(
            functools.partial(final_kernel, start, 4 if near else 2, near),
            out_shape=(pltpu.HBM(field.shape, jnp.float32),) * 2,
            in_specs=[VMEM] * 3
            + ([VMEM] * 5 if near else [HBM] * 2 + [ANY] * 3)
            + [HBM] * len(kept),
            out_specs=(HBM,) * 2,
            scratch_shapes=[pltpu.VMEM((blocks, size, rows, lanes), jnp.float32)] * (2 + (not near))
            + [pltpu.VMEM((4, blocks, size, quarter, lanes), jnp.float32)] * (not near)
            + [pltpu.SemaphoreType.DMA((blocks, 5)), pltpu.SemaphoreType.DMA((4 * blocks,))],
            input_output_aliases={given: 0, given + 1: 1} if kept else {},
            compiler_params=params(),
            cost_estimate=cost(),
        )(inverse, edge, field, *given_in, *kept)
    new, residual = kept
    return (new.reshape(state.shape), residual.reshape(state.shape))


def solution(mesh):
    spread = P("row", "inst", None, "mesh", None, None)
    return jax.shard_map(
        local,
        mesh=mesh,
        in_specs=(spread, P("row", "mesh", None, None), P(), P()),
        out_specs=(spread, spread),
        check_vma=False,
    )
```

```python
import functools
import math

import numpy as np

import jax
import jax.numpy as jnp
from jax import lax
from jax.experimental import pallas as pl
from jax.experimental.pallas import tpu as pltpu
from jax.sharding import PartitionSpec as P

INST = 8
OUTER = 6
MODES = 24
LIMIT = 14 * 1024 * 1024
VMEM = pl.BlockSpec(memory_space=pltpu.VMEM)
SMEM = pl.BlockSpec(memory_space=pltpu.SMEM)
ANY = pl.BlockSpec(memory_space=pl.ANY)
HBM = pl.BlockSpec(memory_space=pltpu.HBM)
D1 = -0.5 / math.tan(math.pi / 8)
D2 = 0.5 / math.tan(math.pi / 4)
D3 = -0.5 / math.tan(3 * math.pi / 8)


def shaped(*dims):
    return jax.ShapeDtypeStruct(dims, jnp.float32)


def cost():
    return pl.CostEstimate(flops=1, bytes_accessed=1, transcendentals=0)


def inverse_parts(length):
    steps = np.arange(1, length + 1).astype(np.float64)
    basis = math.sqrt(2.0 / (length + 1)) * np.sin(
        math.pi * steps[:, None] * steps[None, :] / (length + 1)
    )
    eigen = 2.0 - np.cos(math.pi * steps / (length + 1))
    inverse = (0.2 * (basis / eigen[None, :]) @ basis.T).astype(np.float32)
    high = inverse.astype(jnp.bfloat16)
    low = (inverse - high.astype(np.float32)).astype(jnp.bfloat16)
    return np.concatenate([high, low, high], axis=1)


def split_bf16(x):
    high = x.astype(jnp.bfloat16)
    return high, (x - high.astype(jnp.float32)).astype(jnp.bfloat16)


def params():
    return pltpu.CompilerParams(vmem_limit_bytes=LIMIT)


def pack_kernel(planes, field, *rest):
    sems = rest[-1]
    copies = []

    def copy(source, target):
        one = pltpu.make_async_copy(source, target, sems.at[len(copies)])
        one.start()
        copies.append(one)

    outs = rest[:3]
    for k, out in zip((1, 3, 2), outs):
        place = lax.rem(lax.axis_index("inst") + k, 4) * 16
        rows = pl.ds(pl.multiple_of(place, 16), 16)
        done = 0
        for start, size in planes:
            for b in range(0, field.shape[0], 4):
                copy(
                    field.at[b : b + 4, start : start + size, rows, :],
                    out.at[b : b + 4, done : done + size],
                )
            done += size
    for one in copies:
        one.wait()


def edges_kernel(field, after, top, bottom, own, sems):
    rows = pl.ds(pl.multiple_of(lax.axis_index("inst") * 16, 16), 16)
    copies = [
        pltpu.make_async_copy(field.at[b, plane], out.at[b], sems.at[k, b])
        for k, (plane, out) in enumerate(((field.shape[1] - 1, top), (0, bottom)))
        for b in range(field.shape[0])
    ]
    last = field.shape[1] - 1
    copies.append(
        pltpu.make_async_copy(field.at[:, 1:, rows, :], own.at[:, :last], sems.at[2, 0])
    )
    copies.append(
        pltpu.make_async_copy(field.at[:, :1, rows, :], own.at[:, last:], sems.at[2, 1])
    )
    for one in copies:
        one.start()
    for one in copies:
        one.wait()


def pack(field, planes):
    blocks, _, rows, lanes = field.shape
    size = sum(size for _, size in planes)
    return pl.pallas_call(
        functools.partial(pack_kernel, planes),
        out_shape=(shaped(blocks, size, rows // 4, lanes),) * 3,
        in_specs=[HBM],
        out_specs=(VMEM,) * 3,
        scratch_shapes=[pltpu.SemaphoreType.DMA((32,))],
        compiler_params=params(),
        cost_estimate=cost(),
    )(pltpu.with_memory_space_constraint(field, pltpu.HBM))


def turns(position, mode, orders, total):
    order = jnp.zeros(mode.shape, jnp.int32)
    count = orders.shape[0]
    for j in range(count):
        order = jnp.where((mode == 1 + j) | (mode == 1 + count + j), orders[j], order)
    phase = lax.rem(position * order, total).astype(jnp.float32) * (2.0 * math.pi / total)
    value = jnp.where(mode <= count, jnp.cos(phase), jnp.sin(phase))
    return jnp.where(mode <= 2 * count, value, 0.0)


def harmonics_kernel(total, orders, after, front, back, out):
    blocks, planes, _, lanes = front.shape
    mode = lax.broadcasted_iota(jnp.int32, (MODES, planes), 0)
    position = lax.broadcasted_iota(jnp.int32, (MODES, planes), 1) + lax.axis_index("mesh") * planes
    basis = turns(position, mode, orders, total) * jnp.where(mode == 0, 1.0 / total, 2.0 / total)
    rotor = lax.axis_index("row") == 0
    for b in range(blocks):
        edge = jnp.where(rotor, back[b, :, 7, :], front[b, :, 0, :])
        out[:, b * lanes : (b + 1) * lanes] = jnp.dot(
            basis, edge, precision=lax.Precision.HIGHEST, preferred_element_type=jnp.float32
        )


def mix_kernel(scalars, own, up, down, far, after, *outs):
    weight = [scalars[k] for k in range(INST)]
    cosine, sine = scalars[INST], scalars[INST + 1]
    at = jnp.where(lax.axis_index("mesh") == 0, 1, 0)

    def mixed(var):
        u = [r[s, var, at] for r in (own, up, far, down) for s in range(2)]
        sums = []
        for a in range(INST):
            total = weight[a % INST] * u[0]
            for b in range(1, INST):
                total = total + weight[(a - b) % INST] * u[b]
            sums.append(total)
        return sums

    half = INST // 2

    def put(var, values):
        for a, value in enumerate(values):
            outs[a // half][a % half, var] = value

    for var in (0, 1, 4, 5):
        put(var, mixed(var))
    v, w = mixed(2), mixed(3)
    put(2, [cosine * x - sine * y for x, y in zip(v, w)])
    put(3, [sine * x + cosine * y for x, y in zip(v, w)])


def source_kernel(rims, scalars, *refs):
    outs, refs = refs[-4:], refs[:-4]
    if rims:
        *ghost, nu = refs[-3:]
        refs = refs[:-3]
    own, up, down, far = refs
    size = up.shape[2]
    ratio = scalars[0]
    c1, c2, c3 = (ratio * D1, ratio * D2, ratio * D3)
    out_own, out_up, out_down, out_far = outs
    order = (out_own, out_up, out_far, out_down)
    for var in range(up.shape[1]):
        for p in range(size):
            u = [r[s, var, p] for r in (own, up, far, down) for s in range(2)]
            near = [u[(n - 1) % INST] - u[(n + 1) % INST] for n in range(INST)]
            second = [c2 * (u[(n - 2) % INST] - u[(n + 2) % INST]) for n in range(4)]
            for n in range(INST):
                s = c1 * near[n] - c3 * near[(n + 4) % INST]
                s = s + second[n] if n < 4 else s - second[n - 4]
                order[n // 2][n % 2, var, p] = s
    if not rims:
        return

    def add_ghost(p, factor):
        for var in range(up.shape[1]):
            for n in range(INST):
                at = (n % 2, var, p)
                order[n // 2][at] = order[n // 2][at] - factor * ghost[n // 4][n % 4, var]

    place = pl.ds(pl.multiple_of(lax.axis_index("inst") * 16, 16), 16)

    @pl.when(lax.axis_index("mesh") == 0)
    def _():
        add_ghost(size - 1, nu[0, place, :] + 0.5)

    @pl.when(lax.axis_index("mesh") == lax.axis_size("mesh") - 1)
    def _():
        add_ghost(size - 2, nu[nu.shape[0] - 1, place, :])


def stencil_kernel(nu, low, high, field, one, two):
    blocks, planes, rows, lanes = field.shape
    lane = lax.broadcasted_iota(jnp.int32, (rows, lanes), 1)
    row = lax.broadcasted_iota(jnp.int32, (rows, lanes), 0)
    for b in range(blocks):
        for p in range(planes):
            u = field[b, p]
            before = low[b] if p == 0 else field[b, p - 1]
            after = high[b] if p == planes - 1 else field[b, p + 1]
            left = jnp.where(lane == 0, 0.0, pltpu.roll(u, 1, 1))
            right = jnp.where(lane == lanes - 1, 0.0, pltpu.roll(u, lanes - 1, 1))
            above = jnp.where(row == 0, 0.0, pltpu.roll(u, 1, 0))
            below = jnp.where(row == rows - 1, 0.0, pltpu.roll(u, rows - 1, 0))
            lap = (before + after) + (above + below) + (left + right) - 6.0 * u
            at = (p - 1) % planes
            out, at = (one, at) if at < OUTER else (two, at - OUTER)
            out[b, at] = nu[p] * lap - (u - above) - 0.5 * (u - before)


def add_kernel(one, two, after, out):
    out[...] = one[...] + two[...]


def edge_kernel(total, orders, one, two, nu, *rest):
    out = rest[-1]
    planes, blocks, rows, lanes = out.shape
    mode = lax.broadcasted_iota(jnp.int32, (planes, MODES), 1)
    position = lax.broadcasted_iota(jnp.int32, (planes, MODES), 0) + lax.axis_index("mesh") * planes
    ghost = jnp.dot(
        turns(position, mode, orders, total),
        one[...] + two[...],
        precision=lax.Precision.HIGHEST,
        preferred_element_type=jnp.float32,
    )
    rotor = lax.axis_index("row") == 0
    hit = lax.broadcasted_iota(jnp.int32, (rows, lanes), 0) == jnp.where(rotor, rows - 1, 0)
    for p in range(planes):
        facing = jnp.where(rotor, nu[p, nu.shape[1] - 1 :, :], nu[p, :1, :] + 1.0)
        for b in range(blocks):
            value = facing * ghost[p : p + 1, b * lanes : (b + 1) * lanes]
            out[p, b] = jnp.where(hit, value, 0.0)


def final_kernel(start, chunk, near, inverse, edge, field, pre, *rest):
    new, residual, new_held, residual_held = rest[-6 - 2 * (not near) : -2 - 2 * (not near)]
    sems_in, sems = rest[-2:]
    count, planes, rows, lanes = field.shape
    size = pre.shape[1]
    base = (start + 1) % planes
    inst = lax.axis_index("inst")
    steps = (0, 1, 3, 2)
    arrivals = []
    if not near:
        held_in, pieces = rest[-4:-2]
    for b in range(0, count, chunk):
        if near:
            arrivals.append([])
            continue
        part = slice(b, b + chunk)
        pairs = [(pre.at[part], held_in.at[part])]
        pairs += [
            (rest[k].at[part], pieces.at[lax.rem(inst + step, 4), part])
            for k, step in enumerate(steps)
        ]
        arrivals.append(
            [
                pltpu.make_async_copy(x, y, sems_in.at[b // chunk, k])
                for k, (x, y) in enumerate(pairs)
            ]
        )
        for one in arrivals[-1]:
            one.start()
    tile = pl.ds(pl.multiple_of((1 - lax.axis_index("row")) * (rows - 8), 8), 8)
    runs = [(0, base, min(size, planes - base))]
    if base + size > planes:
        runs.append((planes - base, 0, base + size - planes))
    copies = []
    for j in range(0, count, 2):
        if j % chunk == 0:
            for one in arrivals[j // chunk]:
                one.wait()
        for p in range(size):
            plane = (base + p) % planes
            for b in (j, j + 1):
                for k, step in enumerate(steps):
                    if near:
                        at = pl.ds(pl.multiple_of(16 * lax.rem(inst + step, 4), 16), 16)
                        residual_held[b, p, at] = pre[b, p, at] - rest[k][b, p]
                    else:
                        at = pl.ds(16 * k, 16)
                        residual_held[b, p, at] = held_in[b, p, at] - pieces[k, b, p]
                residual_held[b, p, tile] = residual_held[b, p, tile] + edge[plane, b]
            high, low = split_bf16(
                jnp.concatenate([residual_held[j, p], residual_held[j + 1, p]], 1)
            )
            change = jnp.dot(
                inverse[...],
                jnp.concatenate([high, high, low], 0),
                preferred_element_type=jnp.float32,
            )
            new_held[j, p] = field[j, plane] + change[:, :lanes]
            new_held[j + 1, p] = field[j + 1, plane] + change[:, lanes:]
        if (j + 2) % chunk == 0:
            part = slice(j + 2 - chunk, j + 2)
            for held, out in ((residual_held, residual), (new_held, new)):
                for source, target, length in runs:
                    copies.append(
                        pltpu.make_async_copy(
                            held.at[part, source : source + length],
                            out.at[part, target : target + length],
                            sems.at[len(copies)],
                        )
                    )
                    copies[-1].start()
    for one in copies:
        one.wait()


def lag_weights(lag):
    delta = jnp.arange(INST).astype(jnp.float32) - lag
    total = 1.0 + jnp.cos(math.pi * delta)
    for k in range(1, INST // 2):
        total = total + 2.0 * jnp.cos(2.0 * math.pi * k / INST * delta)
    return total / INST


def local(state, viscosity, blade_counts, mode_orders):
    _, local_inst, variables, planes, rows, lanes = state.shape
    quarter = rows // 4
    blocks = local_inst * variables
    mesh_count = lax.axis_size("mesh")
    total = planes * mesh_count
    which = lax.axis_index("row")
    inst = lax.axis_index("inst")
    mesh_idx = lax.axis_index("mesh")
    counts = blade_counts.astype(jnp.float32)
    ratio = counts[1 - which] / counts[which]
    angle = 2.0 * math.pi / counts[which]
    field = state.reshape(blocks, planes, rows, lanes)
    nu = viscosity[0]
    first = mesh_idx == 0
    last = mesh_idx == mesh_count - 1

    def along(x, step):
        return lax.ppermute(x, "inst", [(j, (j + step) % 4) for j in range(4)])

    def in_hbm(*arrays):
        return [pltpu.with_memory_space_constraint(x, pltpu.HBM) for x in arrays]

    def exchange(up, down, far):
        from_down, from_up, from_far = along(up, 1), along(down, 3), along(far, 2)
        return from_up, from_down, from_far

    packed = pack(field, ((1, planes - 1), (0, 1)))
    gathered = exchange(*packed)

    top, bottom, own = pl.pallas_call(
        edges_kernel,
        out_shape=(shaped(blocks, rows, lanes),) * 2 + (shaped(blocks, planes, quarter, lanes),),
        in_specs=[HBM, VMEM],
        out_specs=(VMEM,) * 3,
        scratch_shapes=[pltpu.SemaphoreType.DMA((3, blocks))],
        compiler_params=params(),
        cost_estimate=cost(),
    )(pltpu.with_memory_space_constraint(field, pltpu.HBM), packed[0])
    low = lax.ppermute(top, "mesh", [(j, j + 1) for j in range(mesh_count - 1)])
    high = lax.ppermute(bottom, "mesh", [(j + 1, j) for j in range(mesh_count - 1)])

    split = (local_inst, variables)
    all_quarters = in_hbm(*(x.reshape(*split, planes, quarter, lanes) for x in (own, *gathered)))

    whole = shaped(*field.shape)
    at_once = 2
    slab = pl.BlockSpec((at_once, planes, rows, lanes), lambda b: (b, 0, 0, 0))
    plane = pl.BlockSpec((at_once, rows, lanes), lambda b: (b, 0, 0))
    pre_one, pre_two = pl.pallas_call(
        stencil_kernel,
        grid=(blocks // at_once,),
        out_shape=(
            pltpu.HBM((blocks, OUTER, rows, lanes), jnp.float32),
            pltpu.HBM((blocks, planes - OUTER, rows, lanes), jnp.float32),
        ),
        in_specs=[pl.BlockSpec((planes, rows, lanes), lambda b: (0, 0, 0)), plane, plane, slab],
        out_specs=(
            pl.BlockSpec((at_once, OUTER, rows, lanes), lambda b: (b, 0, 0, 0)),
            pl.BlockSpec((at_once, planes - OUTER, rows, lanes), lambda b: (b, 0, 0, 0)),
        ),
        compiler_params=params(),
        cost_estimate=cost(),
    )(nu, *in_hbm(low, high), field)

    harmonics = pl.pallas_call(
        functools.partial(harmonics_kernel, total),
        out_shape=shaped(MODES, blocks * lanes),
        grid=(1,),
        in_specs=[
            SMEM,
            VMEM,
            pl.BlockSpec((blocks, planes, 8, lanes), lambda b: (0, 0, 0, 0)),
            pl.BlockSpec((blocks, planes, 8, lanes), lambda b: (0, 0, rows // 8 - 1, 0)),
        ],
        out_specs=pl.BlockSpec((MODES, blocks * lanes), lambda b: (0, 0)),
        compiler_params=params(),
        cost_estimate=cost(),
    )(mode_orders, packed[0], field, field)

    def crossing(flip):
        return [
            (r * mesh_count + m, (1 - r) * mesh_count + (m ^ flip))
            for r in range(2)
            for m in range(mesh_count)
        ]

    def doubled(x, flip):
        return x + lax.ppermute(x, "mesh", [(m, m ^ flip) for m in range(mesh_count)])

    two_ways = [lax.ppermute(harmonics, ("row", "mesh"), crossing(flip)) for flip in (0, 1)]
    harmonics = two_ways[0] + two_ways[1]
    early = lax.ppermute(harmonics, "mesh", [(m, m ^ 2) for m in range(mesh_count)])

    def sources(start, size, rims, after=()):
        at_once = 3
        piece_in = pl.BlockSpec(
            (2, at_once, size, quarter, lanes), lambda b: (0, b, start // size, 0, 0)
        )
        rim_specs = [
            pl.BlockSpec((INST // 2, at_once, quarter, lanes), lambda b: (0, b, 0, 0)),
            pl.BlockSpec((INST // 2, at_once, quarter, lanes), lambda b: (0, b, 0, 0)),
            pl.BlockSpec((planes, rows, lanes), lambda b: (0, 0, 0)),
        ]
        def kernel(*refs):
            inputs, outputs = refs[: -4 - len(after)], refs[-4:]
            source_kernel(bool(rims), *inputs, *outputs)

        outs = pl.pallas_call(
            kernel,
            out_shape=(pltpu.HBM((*split, size, quarter, lanes), jnp.float32),) * 4,
            grid=(variables // at_once,),
            in_specs=[SMEM] + [piece_in] * 4 + rim_specs[: len(rims)] + [ANY] * len(after),
            out_specs=(
                pl.BlockSpec((2, at_once, size, quarter, lanes), lambda b: (0, b, 0, 0, 0)),
            )
            * 4,
            compiler_params=params(),
            cost_estimate=cost(),
        )(ratio[None], *all_quarters, *rims, *after)
        own, up, down, far = (x.reshape(blocks, size, quarter, lanes) for x in outs)
        return (own, *exchange(up, down, far))

    weights = lag_weights(jnp.where(first, -ratio, ratio))
    turn = jnp.where(first, angle, -angle)
    mixing = jnp.concatenate([weights, jnp.stack([jnp.cos(turn), jnp.sin(turn)])])
    one_source = sources(0, OUTER, (), after=(*in_hbm(pre_one), early, mixing))

    ghost_shape = shaped(INST // 2, variables, quarter, lanes)

    outermost = pl.BlockSpec((2, variables, 2, quarter, lanes), lambda b: (0, 0, 3, 0, 0))
    ghost_out = pl.pallas_call(
        mix_kernel,
        out_shape=(ghost_shape,) * 2,
        grid=(1,),
        in_specs=[SMEM] + [outermost] * 4 + [ANY],
        out_specs=(pl.BlockSpec(ghost_shape.shape, lambda b: (0, 0, 0, 0)),) * 2,
        compiler_params=params(),
        cost_estimate=cost(),
    )(
        mixing,
        *all_quarters,
        *in_hbm(one_source[0]),
    )
    ghost = [
        lax.ppermute(part, "mesh", [(mesh_count - 1, 0), (0, mesh_count - 1)]) for part in ghost_out
    ]

    harmonics = pl.pallas_call(
        add_kernel,
        out_shape=harmonics,
        in_specs=[VMEM, VMEM, ANY],
        out_specs=VMEM,
        compiler_params=params(),
        cost_estimate=cost(),
    )(harmonics, early, ghost_out[0])
    harmonics = doubled(harmonics, 4)
    opposite = lax.ppermute(harmonics, "mesh", [(m, m ^ 8) for m in range(mesh_count)])
    two_source = sources(OUTER, planes - OUTER, (*ghost, nu), after=(opposite,))

    edge = pl.pallas_call(
        functools.partial(edge_kernel, total),
        out_shape=shaped(planes, blocks, 8, lanes),
        in_specs=[SMEM, VMEM, VMEM, VMEM] + [ANY] * 3,
        out_specs=VMEM,
        compiler_params=params(),
        cost_estimate=cost(),
    )(
        mode_orders,
        harmonics,
        opposite,
        nu,
        *one_source[1:],
    )

    inverse = jnp.asarray(inverse_parts(rows))
    kept = ()
    for start, size, group, pre in ((0, OUTER, one_source, pre_one), (OUTER, planes - OUTER, two_source, pre_two)):
        given = 4 + len(group)
        near = size < 4
        if near:
            group = [pltpu.with_memory_space_constraint(x, pltpu.VMEM) for x in group]
            given_in = (pre, *group)
        else:
            given_in = (*in_hbm(pre, group[0]), *group[1:])
        kept = pl.pallas_call(
            functools.partial(final_kernel, start, 4 if near else 2, near),
            out_shape=(pltpu.HBM(field.shape, jnp.float32),) * 2,
            in_specs=[VMEM] * 3
            + ([VMEM] * 5 if near else [HBM] * 2 + [ANY] * 3)
            + [HBM] * len(kept),
            out_specs=(HBM,) * 2,
            scratch_shapes=[pltpu.VMEM((blocks, size, rows, lanes), jnp.float32)] * (2 + (not near))
            + [pltpu.VMEM((4, blocks, size, quarter, lanes), jnp.float32)] * (not near)
            + [pltpu.SemaphoreType.DMA((blocks, 5)), pltpu.SemaphoreType.DMA((4 * blocks,))],
            input_output_aliases={given: 0, given + 1: 1} if kept else {},
            compiler_params=params(),
            cost_estimate=cost(),
        )(inverse, edge, field, *given_in, *kept)
    new, residual = kept
    return (new.reshape(state.shape), residual.reshape(state.shape))


def solution(mesh):
    spread = P("row", "inst", None, "mesh", None, None)
    return jax.shard_map(
        local,
        mesh=mesh,
        in_specs=(spread, P("row", "mesh", None, None), P(), P()),
        out_specs=(spread, spread),
        check_vma=False,
    )
```

```python
import functools
import math

import numpy as np

import jax
import jax.numpy as jnp
from jax import lax
from jax.experimental import pallas as pl
from jax.experimental.pallas import tpu as pltpu
from jax.sharding import PartitionSpec as P

INST = 8
OUTER = 6
MODES = 24
LIMIT = 14 * 1024 * 1024
VMEM = pl.BlockSpec(memory_space=pltpu.VMEM)
SMEM = pl.BlockSpec(memory_space=pltpu.SMEM)
ANY = pl.BlockSpec(memory_space=pl.ANY)
HBM = pl.BlockSpec(memory_space=pltpu.HBM)
D1 = -0.5 / math.tan(math.pi / 8)
D2 = 0.5 / math.tan(math.pi / 4)
D3 = -0.5 / math.tan(3 * math.pi / 8)


def shaped(*dims):
    return jax.ShapeDtypeStruct(dims, jnp.float32)


def cost():
    return pl.CostEstimate(flops=1, bytes_accessed=1, transcendentals=0)


def inverse_parts(length):
    steps = np.arange(1, length + 1).astype(np.float64)
    basis = math.sqrt(2.0 / (length + 1)) * np.sin(
        math.pi * steps[:, None] * steps[None, :] / (length + 1)
    )
    eigen = 2.0 - np.cos(math.pi * steps / (length + 1))
    inverse = (0.2 * (basis / eigen[None, :]) @ basis.T).astype(np.float32)
    high = inverse.astype(jnp.bfloat16)
    low = (inverse - high.astype(np.float32)).astype(jnp.bfloat16)
    return np.concatenate([high, low, high], axis=1)


def split_bf16(x):
    high = x.astype(jnp.bfloat16)
    return high, (x - high.astype(jnp.float32)).astype(jnp.bfloat16)


def params():
    return pltpu.CompilerParams(vmem_limit_bytes=LIMIT)


def pack_kernel(planes, field, *rest):
    sems = rest[-1]
    copies = []

    def copy(source, target):
        one = pltpu.make_async_copy(source, target, sems.at[len(copies)])
        one.start()
        copies.append(one)

    outs = rest[:3]
    for k, out in zip((1, 3, 2), outs):
        place = lax.rem(lax.axis_index("inst") + k, 4) * 16
        rows = pl.ds(pl.multiple_of(place, 16), 16)
        done = 0
        for start, size in planes:
            for b in range(0, field.shape[0], 4):
                copy(
                    field.at[b : b + 4, start : start + size, rows, :],
                    out.at[b : b + 4, done : done + size],
                )
            done += size
    for one in copies:
        one.wait()


def edges_kernel(field, after, top, bottom, own, sems):
    rows = pl.ds(pl.multiple_of(lax.axis_index("inst") * 16, 16), 16)
    copies = [
        pltpu.make_async_copy(field.at[b, plane], out.at[b], sems.at[k, b])
        for k, (plane, out) in enumerate(((field.shape[1] - 1, top), (0, bottom)))
        for b in range(field.shape[0])
    ]
    last = field.shape[1] - 1
    copies.append(
        pltpu.make_async_copy(field.at[:, 1:, rows, :], own.at[:, :last], sems.at[2, 0])
    )
    copies.append(
        pltpu.make_async_copy(field.at[:, :1, rows, :], own.at[:, last:], sems.at[2, 1])
    )
    for one in copies:
        one.start()
    for one in copies:
        one.wait()


def pack(field, planes):
    blocks, _, rows, lanes = field.shape
    size = sum(size for _, size in planes)
    return pl.pallas_call(
        functools.partial(pack_kernel, planes),
        out_shape=(shaped(blocks, size, rows // 4, lanes),) * 3,
        in_specs=[HBM],
        out_specs=(VMEM,) * 3,
        scratch_shapes=[pltpu.SemaphoreType.DMA((32,))],
        compiler_params=params(),
        cost_estimate=cost(),
    )(pltpu.with_memory_space_constraint(field, pltpu.HBM))


def turns(position, mode, orders, total):
    order = jnp.zeros(mode.shape, jnp.int32)
    count = orders.shape[0]
    for j in range(count):
        order = jnp.where((mode == 1 + j) | (mode == 1 + count + j), orders[j], order)
    phase = lax.rem(position * order, total).astype(jnp.float32) * (2.0 * math.pi / total)
    value = jnp.where(mode <= count, jnp.cos(phase), jnp.sin(phase))
    return jnp.where(mode <= 2 * count, value, 0.0)


def harmonics_kernel(total, orders, after, front, back, out):
    blocks, planes, _, lanes = front.shape
    mode = lax.broadcasted_iota(jnp.int32, (MODES, planes), 0)
    position = lax.broadcasted_iota(jnp.int32, (MODES, planes), 1) + lax.axis_index("mesh") * planes
    basis = turns(position, mode, orders, total) * jnp.where(mode == 0, 1.0 / total, 2.0 / total)
    rotor = lax.axis_index("row") == 0
    for b in range(blocks):
        edge = jnp.where(rotor, back[b, :, 7, :], front[b, :, 0, :])
        out[:, b * lanes : (b + 1) * lanes] = jnp.dot(
            basis, edge, precision=lax.Precision.HIGHEST, preferred_element_type=jnp.float32
        )


def mix_kernel(counts, own, up, down, far, after, *outs):
    lanes = own.shape[-1]
    which, low_end = lax.axis_index("row"), lax.axis_index("mesh") == 0
    mine, other = (
        jnp.full((1, lanes), counts[k], jnp.int32).astype(jnp.float32) for k in (which, 1 - which)
    )
    ratio, angle = other / mine, 2.0 * math.pi / mine
    lag, turn = jnp.where(low_end, -ratio, ratio), jnp.where(low_end, angle, -angle)
    delta = lax.broadcasted_iota(jnp.int32, (1, lanes), 1).astype(jnp.float32) - lag
    weights = lag_weights(delta)
    weight = [weights[:, k : k + 1] for k in range(INST)]
    cosine, sine = jnp.cos(turn), jnp.sin(turn)
    at = jnp.where(lax.axis_index("mesh") == 0, 1, 0)

    def mixed(var):
        u = [r[s, var, at] for r in (own, up, far, down) for s in range(2)]
        sums = []
        for a in range(INST):
            total = weight[a % INST] * u[0]
            for b in range(1, INST):
                total = total + weight[(a - b) % INST] * u[b]
            sums.append(total)
        return sums

    half = INST // 2

    def put(var, values):
        for a, value in enumerate(values):
            outs[a // half][a % half, var] = value

    for var in (0, 1, 4, 5):
        put(var, mixed(var))
    v, w = mixed(2), mixed(3)
    put(2, [cosine * x - sine * y for x, y in zip(v, w)])
    put(3, [sine * x + cosine * y for x, y in zip(v, w)])


def source_kernel(rims, scalars, *refs):
    outs, refs = refs[-4:], refs[:-4]
    if rims:
        *ghost, nu = refs[-3:]
        refs = refs[:-3]
    own, up, down, far = refs
    size = up.shape[2]
    ratio = scalars[0]
    c1, c2, c3 = (ratio * D1, ratio * D2, ratio * D3)
    out_own, out_up, out_down, out_far = outs
    order = (out_own, out_up, out_far, out_down)
    for var in range(up.shape[1]):
        for p in range(size):
            u = [r[s, var, p] for r in (own, up, far, down) for s in range(2)]
            near = [u[(n - 1) % INST] - u[(n + 1) % INST] for n in range(INST)]
            second = [c2 * (u[(n - 2) % INST] - u[(n + 2) % INST]) for n in range(4)]
            for n in range(INST):
                s = c1 * near[n] - c3 * near[(n + 4) % INST]
                s = s + second[n] if n < 4 else s - second[n - 4]
                order[n // 2][n % 2, var, p] = s
    if not rims:
        return

    def add_ghost(p, factor):
        for var in range(up.shape[1]):
            for n in range(INST):
                at = (n % 2, var, p)
                order[n // 2][at] = order[n // 2][at] - factor * ghost[n // 4][n % 4, var]

    place = pl.ds(pl.multiple_of(lax.axis_index("inst") * 16, 16), 16)

    @pl.when(lax.axis_index("mesh") == 0)
    def _():
        add_ghost(size - 1, nu[0, place, :] + 0.5)

    @pl.when(lax.axis_index("mesh") == lax.axis_size("mesh") - 1)
    def _():
        add_ghost(size - 2, nu[nu.shape[0] - 1, place, :])


def stencil_kernel(nu, low, high, field, one, two):
    blocks, planes, rows, lanes = field.shape
    lane = lax.broadcasted_iota(jnp.int32, (rows, lanes), 1)
    row = lax.broadcasted_iota(jnp.int32, (rows, lanes), 0)
    for b in range(blocks):
        for p in range(planes):
            u = field[b, p]
            before = low[b] if p == 0 else field[b, p - 1]
            after = high[b] if p == planes - 1 else field[b, p + 1]
            left = jnp.where(lane == 0, 0.0, pltpu.roll(u, 1, 1))
            right = jnp.where(lane == lanes - 1, 0.0, pltpu.roll(u, lanes - 1, 1))
            above = jnp.where(row == 0, 0.0, pltpu.roll(u, 1, 0))
            below = jnp.where(row == rows - 1, 0.0, pltpu.roll(u, rows - 1, 0))
            lap = (before + after) + (above + below) + (left + right) - 6.0 * u
            at = (p - 1) % planes
            out, at = (one, at) if at < OUTER else (two, at - OUTER)
            out[b, at] = nu[p] * lap - (u - above) - 0.5 * (u - before)


def add_kernel(one, two, after, out):
    out[...] = one[...] + two[...]


def edge_kernel(total, orders, one, two, nu, *rest):
    out = rest[-1]
    planes, blocks, rows, lanes = out.shape
    mode = lax.broadcasted_iota(jnp.int32, (planes, MODES), 1)
    position = lax.broadcasted_iota(jnp.int32, (planes, MODES), 0) + lax.axis_index("mesh") * planes
    ghost = jnp.dot(
        turns(position, mode, orders, total),
        one[...] + two[...],
        precision=lax.Precision.HIGHEST,
        preferred_element_type=jnp.float32,
    )
    rotor = lax.axis_index("row") == 0
    hit = lax.broadcasted_iota(jnp.int32, (rows, lanes), 0) == jnp.where(rotor, rows - 1, 0)
    for p in range(planes):
        facing = jnp.where(rotor, nu[p, nu.shape[1] - 1 :, :], nu[p, :1, :] + 1.0)
        for b in range(blocks):
            value = facing * ghost[p : p + 1, b * lanes : (b + 1) * lanes]
            out[p, b] = jnp.where(hit, value, 0.0)


def final_kernel(start, chunk, near, inverse, edge, field, pre, *rest):
    new, residual, new_held, residual_held = rest[-6 - 2 * (not near) : -2 - 2 * (not near)]
    sems_in, sems = rest[-2:]
    count, planes, rows, lanes = field.shape
    size = pre.shape[1]
    base = (start + 1) % planes
    inst = lax.axis_index("inst")
    steps = (0, 1, 3, 2)
    arrivals = []
    if not near:
        held_in, pieces = rest[-4:-2]
    for b in range(0, count, chunk):
        if near:
            arrivals.append([])
            continue
        part = slice(b, b + chunk)
        pairs = [(pre.at[part], held_in.at[part])]
        pairs += [
            (rest[k].at[part], pieces.at[lax.rem(inst + step, 4), part])
            for k, step in enumerate(steps)
        ]
        arrivals.append(
            [
                pltpu.make_async_copy(x, y, sems_in.at[b // chunk, k])
                for k, (x, y) in enumerate(pairs)
            ]
        )
        for one in arrivals[-1]:
            one.start()
    tile = pl.ds(pl.multiple_of((1 - lax.axis_index("row")) * (rows - 8), 8), 8)
    runs = [(0, base, min(size, planes - base))]
    if base + size > planes:
        runs.append((planes - base, 0, base + size - planes))
    copies = []
    for j in range(0, count, 2):
        if j % chunk == 0:
            for one in arrivals[j // chunk]:
                one.wait()
        for p in range(size):
            plane = (base + p) % planes
            for b in (j, j + 1):
                for k, step in enumerate(steps):
                    if near:
                        at = pl.ds(pl.multiple_of(16 * lax.rem(inst + step, 4), 16), 16)
                        residual_held[b, p, at] = pre[b, p, at] - rest[k][b, p]
                    else:
                        at = pl.ds(16 * k, 16)
                        residual_held[b, p, at] = held_in[b, p, at] - pieces[k, b, p]
                residual_held[b, p, tile] = residual_held[b, p, tile] + edge[plane, b]
            high, low = split_bf16(
                jnp.concatenate([residual_held[j, p], residual_held[j + 1, p]], 1)
            )
            change = jnp.dot(
                inverse[...],
                jnp.concatenate([high, high, low], 0),
                preferred_element_type=jnp.float32,
            )
            new_held[j, p] = field[j, plane] + change[:, :lanes]
            new_held[j + 1, p] = field[j + 1, plane] + change[:, lanes:]
        if (j + 2) % chunk == 0:
            part = slice(j + 2 - chunk, j + 2)
            for held, out in ((residual_held, residual), (new_held, new)):
                for source, target, length in runs:
                    copies.append(
                        pltpu.make_async_copy(
                            held.at[part, source : source + length],
                            out.at[part, target : target + length],
                            sems.at[len(copies)],
                        )
                    )
                    copies[-1].start()
    for one in copies:
        one.wait()


def lag_weights(delta):
    total = 1.0 + jnp.cos(math.pi * delta)
    for k in range(1, INST // 2):
        total = total + 2.0 * jnp.cos(2.0 * math.pi * k / INST * delta)
    return total / INST


def local(state, viscosity, blade_counts, mode_orders):
    _, local_inst, variables, planes, rows, lanes = state.shape
    quarter = rows // 4
    blocks = local_inst * variables
    mesh_count = lax.axis_size("mesh")
    total = planes * mesh_count
    which = lax.axis_index("row")
    inst = lax.axis_index("inst")
    mesh_idx = lax.axis_index("mesh")
    counts = blade_counts.astype(jnp.float32)
    ratio = counts[1 - which] / counts[which]
    angle = 2.0 * math.pi / counts[which]
    field = state.reshape(blocks, planes, rows, lanes)
    nu = viscosity[0]
    first = mesh_idx == 0
    last = mesh_idx == mesh_count - 1

    def along(x, step):
        return lax.ppermute(x, "inst", [(j, (j + step) % 4) for j in range(4)])

    def in_hbm(*arrays):
        return [pltpu.with_memory_space_constraint(x, pltpu.HBM) for x in arrays]

    def exchange(up, down, far):
        from_down, from_up, from_far = along(up, 1), along(down, 3), along(far, 2)
        return from_up, from_down, from_far

    packed = pack(field, ((1, planes - 1), (0, 1)))
    gathered = exchange(*packed)

    top, bottom, own = pl.pallas_call(
        edges_kernel,
        out_shape=(shaped(blocks, rows, lanes),) * 2 + (shaped(blocks, planes, quarter, lanes),),
        in_specs=[HBM, VMEM],
        out_specs=(VMEM,) * 3,
        scratch_shapes=[pltpu.SemaphoreType.DMA((3, blocks))],
        compiler_params=params(),
        cost_estimate=cost(),
    )(pltpu.with_memory_space_constraint(field, pltpu.HBM), packed[0])
    low = lax.ppermute(top, "mesh", [(j, j + 1) for j in range(mesh_count - 1)])
    high = lax.ppermute(bottom, "mesh", [(j + 1, j) for j in range(mesh_count - 1)])

    split = (local_inst, variables)
    all_quarters = in_hbm(*(x.reshape(*split, planes, quarter, lanes) for x in (own, *gathered)))

    whole = shaped(*field.shape)
    at_once = 2
    slab = pl.BlockSpec((at_once, planes, rows, lanes), lambda b: (b, 0, 0, 0))
    plane = pl.BlockSpec((at_once, rows, lanes), lambda b: (b, 0, 0))
    pre_one, pre_two = pl.pallas_call(
        stencil_kernel,
        grid=(blocks // at_once,),
        out_shape=(
            pltpu.HBM((blocks, OUTER, rows, lanes), jnp.float32),
            pltpu.HBM((blocks, planes - OUTER, rows, lanes), jnp.float32),
        ),
        in_specs=[pl.BlockSpec((planes, rows, lanes), lambda b: (0, 0, 0)), plane, plane, slab],
        out_specs=(
            pl.BlockSpec((at_once, OUTER, rows, lanes), lambda b: (b, 0, 0, 0)),
            pl.BlockSpec((at_once, planes - OUTER, rows, lanes), lambda b: (b, 0, 0, 0)),
        ),
        compiler_params=params(),
        cost_estimate=cost(),
    )(nu, *in_hbm(low, high), field)

    harmonics = pl.pallas_call(
        functools.partial(harmonics_kernel, total),
        out_shape=shaped(MODES, blocks * lanes),
        grid=(1,),
        in_specs=[
            SMEM,
            VMEM,
            pl.BlockSpec((blocks, planes, 8, lanes), lambda b: (0, 0, 0, 0)),
            pl.BlockSpec((blocks, planes, 8, lanes), lambda b: (0, 0, rows // 8 - 1, 0)),
        ],
        out_specs=pl.BlockSpec((MODES, blocks * lanes), lambda b: (0, 0)),
        compiler_params=params(),
        cost_estimate=cost(),
    )(mode_orders, packed[0], field, field)

    def crossing(flip):
        return [
            (r * mesh_count + m, (1 - r) * mesh_count + (m ^ flip))
            for r in range(2)
            for m in range(mesh_count)
        ]

    def doubled(x, flip):
        return x + lax.ppermute(x, "mesh", [(m, m ^ flip) for m in range(mesh_count)])

    two_ways = [lax.ppermute(harmonics, ("row", "mesh"), crossing(flip)) for flip in (0, 1)]
    harmonics = two_ways[0] + two_ways[1]
    early = lax.ppermute(harmonics, "mesh", [(m, m ^ 2) for m in range(mesh_count)])

    def sources(start, size, rims, after=()):
        at_once = 3
        piece_in = pl.BlockSpec(
            (2, at_once, size, quarter, lanes), lambda b: (0, b, start // size, 0, 0)
        )
        rim_specs = [
            pl.BlockSpec((INST // 2, at_once, quarter, lanes), lambda b: (0, b, 0, 0)),
            pl.BlockSpec((INST // 2, at_once, quarter, lanes), lambda b: (0, b, 0, 0)),
            pl.BlockSpec((planes, rows, lanes), lambda b: (0, 0, 0)),
        ]
        def kernel(*refs):
            inputs, outputs = refs[: -4 - len(after)], refs[-4:]
            source_kernel(bool(rims), *inputs, *outputs)

        outs = pl.pallas_call(
            kernel,
            out_shape=(pltpu.HBM((*split, size, quarter, lanes), jnp.float32),) * 4,
            grid=(variables // at_once,),
            in_specs=[SMEM] + [piece_in] * 4 + rim_specs[: len(rims)] + [ANY] * len(after),
            out_specs=(
                pl.BlockSpec((2, at_once, size, quarter, lanes), lambda b: (0, b, 0, 0, 0)),
            )
            * 4,
            compiler_params=params(),
            cost_estimate=cost(),
        )(ratio[None], *all_quarters, *rims, *after)
        own, up, down, far = (x.reshape(blocks, size, quarter, lanes) for x in outs)
        return (own, *exchange(up, down, far))

    one_source = sources(0, OUTER, (), after=(*in_hbm(pre_one), early))

    ghost_shape = shaped(INST // 2, variables, quarter, lanes)

    outermost = pl.BlockSpec((2, variables, 2, quarter, lanes), lambda b: (0, 0, 3, 0, 0))
    ghost_out = pl.pallas_call(
        mix_kernel,
        out_shape=(ghost_shape,) * 2,
        grid=(1,),
        in_specs=[SMEM] + [outermost] * 4 + [ANY],
        out_specs=(pl.BlockSpec(ghost_shape.shape, lambda b: (0, 0, 0, 0)),) * 2,
        compiler_params=params(),
        cost_estimate=cost(),
    )(
        blade_counts,
        *all_quarters,
        *in_hbm(one_source[0]),
    )
    ghost = [
        lax.ppermute(part, "mesh", [(mesh_count - 1, 0), (0, mesh_count - 1)]) for part in ghost_out
    ]

    harmonics = pl.pallas_call(
        add_kernel,
        out_shape=harmonics,
        in_specs=[VMEM, VMEM, ANY],
        out_specs=VMEM,
        compiler_params=params(),
        cost_estimate=cost(),
    )(harmonics, early, ghost_out[0])
    harmonics = doubled(harmonics, 4)
    opposite = lax.ppermute(harmonics, "mesh", [(m, m ^ 8) for m in range(mesh_count)])
    two_source = sources(OUTER, planes - OUTER, (*ghost, nu), after=(opposite,))

    edge = pl.pallas_call(
        functools.partial(edge_kernel, total),
        out_shape=shaped(planes, blocks, 8, lanes),
        in_specs=[SMEM, VMEM, VMEM, VMEM] + [ANY] * 3,
        out_specs=VMEM,
        compiler_params=params(),
        cost_estimate=cost(),
    )(
        mode_orders,
        harmonics,
        opposite,
        nu,
        *one_source[1:],
    )

    inverse = jnp.asarray(inverse_parts(rows))
    kept = ()
    for start, size, group, pre in ((0, OUTER, one_source, pre_one), (OUTER, planes - OUTER, two_source, pre_two)):
        given = 4 + len(group)
        near = size < 4
        if near:
            group = [pltpu.with_memory_space_constraint(x, pltpu.VMEM) for x in group]
            given_in = (pre, *group)
        else:
            given_in = (*in_hbm(pre, group[0]), *group[1:])
        kept = pl.pallas_call(
            functools.partial(final_kernel, start, 4 if near else 2, near),
            out_shape=(pltpu.HBM(field.shape, jnp.float32),) * 2,
            in_specs=[VMEM] * 3
            + ([VMEM] * 5 if near else [HBM] * 2 + [ANY] * 3)
            + [HBM] * len(kept),
            out_specs=(HBM,) * 2,
            scratch_shapes=[pltpu.VMEM((blocks, size, rows, lanes), jnp.float32)] * (2 + (not near))
            + [pltpu.VMEM((4, blocks, size, quarter, lanes), jnp.float32)] * (not near)
            + [pltpu.SemaphoreType.DMA((blocks, 5)), pltpu.SemaphoreType.DMA((4 * blocks,))],
            input_output_aliases={given: 0, given + 1: 1} if kept else {},
            compiler_params=params(),
            cost_estimate=cost(),
        )(inverse, edge, field, *given_in, *kept)
    new, residual = kept
    return (new.reshape(state.shape), residual.reshape(state.shape))


def solution(mesh):
    spread = P("row", "inst", None, "mesh", None, None)
    return jax.shard_map(
        local,
        mesh=mesh,
        in_specs=(spread, P("row", "mesh", None, None), P(), P()),
        out_specs=(spread, spread),
        check_vma=False,
    )
```

```python
import functools
import math

import numpy as np

import jax
import jax.numpy as jnp
from jax import lax
from jax.experimental import pallas as pl
from jax.experimental.pallas import tpu as pltpu
from jax.sharding import PartitionSpec as P

INST = 8
OUTER = 6
MODES = 24
LIMIT = 14 * 1024 * 1024
VMEM = pl.BlockSpec(memory_space=pltpu.VMEM)
SMEM = pl.BlockSpec(memory_space=pltpu.SMEM)
ANY = pl.BlockSpec(memory_space=pl.ANY)
HBM = pl.BlockSpec(memory_space=pltpu.HBM)
D1 = -0.5 / math.tan(math.pi / 8)
D2 = 0.5 / math.tan(math.pi / 4)
D3 = -0.5 / math.tan(3 * math.pi / 8)


def shaped(*dims):
    return jax.ShapeDtypeStruct(dims, jnp.float32)


def cost():
    return pl.CostEstimate(flops=1, bytes_accessed=1, transcendentals=0)


def inverse_parts(length):
    steps = np.arange(1, length + 1).astype(np.float64)
    basis = math.sqrt(2.0 / (length + 1)) * np.sin(
        math.pi * steps[:, None] * steps[None, :] / (length + 1)
    )
    eigen = 2.0 - np.cos(math.pi * steps / (length + 1))
    inverse = (0.2 * (basis / eigen[None, :]) @ basis.T).astype(np.float32)
    high = inverse.astype(jnp.bfloat16)
    low = (inverse - high.astype(np.float32)).astype(jnp.bfloat16)
    return np.concatenate([high, low, high], axis=1)


def split_bf16(x):
    high = x.astype(jnp.bfloat16)
    return high, (x - high.astype(jnp.float32)).astype(jnp.bfloat16)


def params():
    return pltpu.CompilerParams(vmem_limit_bytes=LIMIT)


def pack_kernel(planes, field, *rest):
    sems = rest[-1]
    copies = []

    def copy(source, target):
        one = pltpu.make_async_copy(source, target, sems.at[len(copies)])
        one.start()
        copies.append(one)

    outs = rest[:3]
    for k, out in zip((1, 3, 2), outs):
        place = lax.rem(lax.axis_index("inst") + k, 4) * 16
        rows = pl.ds(pl.multiple_of(place, 16), 16)
        done = 0
        for start, size in planes:
            for b in range(0, field.shape[0], 4):
                copy(
                    field.at[b : b + 4, start : start + size, rows, :],
                    out.at[b : b + 4, done : done + size],
                )
            done += size
    for one in copies:
        one.wait()


def edges_kernel(field, after, top, bottom, own, sems):
    rows = pl.ds(pl.multiple_of(lax.axis_index("inst") * 16, 16), 16)
    copies = [
        pltpu.make_async_copy(field.at[b, plane], out.at[b], sems.at[k, b])
        for k, (plane, out) in enumerate(((field.shape[1] - 1, top), (0, bottom)))
        for b in range(field.shape[0])
    ]
    last = field.shape[1] - 1
    copies.append(
        pltpu.make_async_copy(field.at[:, 1:, rows, :], own.at[:, :last], sems.at[2, 0])
    )
    copies.append(
        pltpu.make_async_copy(field.at[:, :1, rows, :], own.at[:, last:], sems.at[2, 1])
    )
    for one in copies:
        one.start()
    for one in copies:
        one.wait()


def pack(field, planes):
    blocks, _, rows, lanes = field.shape
    size = sum(size for _, size in planes)
    return pl.pallas_call(
        functools.partial(pack_kernel, planes),
        out_shape=(shaped(blocks, size, rows // 4, lanes),) * 3,
        in_specs=[HBM],
        out_specs=(VMEM,) * 3,
        scratch_shapes=[pltpu.SemaphoreType.DMA((32,))],
        compiler_params=params(),
        cost_estimate=cost(),
    )(pltpu.with_memory_space_constraint(field, pltpu.HBM))


def turns(position, mode, orders, total):
    order = jnp.zeros(mode.shape, jnp.int32)
    count = orders.shape[0]
    for j in range(count):
        order = jnp.where((mode == 1 + j) | (mode == 1 + count + j), orders[j], order)
    phase = lax.rem(position * order, total).astype(jnp.float32) * (2.0 * math.pi / total)
    value = jnp.where(mode <= count, jnp.cos(phase), jnp.sin(phase))
    return jnp.where(mode <= 2 * count, value, 0.0)


def harmonics_kernel(total, orders, after, front, back, out):
    blocks, planes, _, lanes = front.shape
    mode = lax.broadcasted_iota(jnp.int32, (MODES, planes), 0)
    position = lax.broadcasted_iota(jnp.int32, (MODES, planes), 1) + lax.axis_index("mesh") * planes
    basis = turns(position, mode, orders, total) * jnp.where(mode == 0, 1.0 / total, 2.0 / total)
    rotor = lax.axis_index("row") == 0
    for b in range(blocks):
        edge = jnp.where(rotor, back[b, :, 7, :], front[b, :, 0, :])
        out[:, b * lanes : (b + 1) * lanes] = jnp.dot(
            basis, edge, precision=lax.Precision.HIGHEST, preferred_element_type=jnp.float32
        )


def mix_kernel(counts, own, up, down, far, after, *outs):
    lanes = own.shape[-1]
    which, low_end = lax.axis_index("row"), lax.axis_index("mesh") == 0
    mine, other = (
        jnp.full((1, lanes), counts[k], jnp.int32).astype(jnp.float32) for k in (which, 1 - which)
    )
    ratio, angle = other / mine, 2.0 * math.pi / mine
    lag, turn = jnp.where(low_end, -ratio, ratio), jnp.where(low_end, angle, -angle)
    delta = lax.broadcasted_iota(jnp.int32, (1, lanes), 1).astype(jnp.float32) - lag
    weights = lag_weights(delta)
    weight = [weights[:, k : k + 1] for k in range(INST)]
    cosine, sine = jnp.cos(turn), jnp.sin(turn)
    at = jnp.where(lax.axis_index("mesh") == 0, 1, 0)

    def mixed(var):
        u = [r[s, var, at] for r in (own, up, far, down) for s in range(2)]
        sums = []
        for a in range(INST):
            total = weight[a % INST] * u[0]
            for b in range(1, INST):
                total = total + weight[(a - b) % INST] * u[b]
            sums.append(total)
        return sums

    half = INST // 2

    def put(var, values):
        for a, value in enumerate(values):
            outs[a // half][a % half, var] = value

    for var in (0, 1, 4, 5):
        put(var, mixed(var))
    v, w = mixed(2), mixed(3)
    put(2, [cosine * x - sine * y for x, y in zip(v, w)])
    put(3, [sine * x + cosine * y for x, y in zip(v, w)])


def source_kernel(rims, scalars, *refs):
    outs, refs = refs[-4:], refs[:-4]
    if rims:
        *ghost, nu = refs[-3:]
        refs = refs[:-3]
    own, up, down, far = refs
    size = up.shape[2]
    ratio = scalars[0]
    c1, c2, c3 = (ratio * D1, ratio * D2, ratio * D3)
    out_own, out_up, out_down, out_far = outs
    order = (out_own, out_up, out_far, out_down)
    for var in range(up.shape[1]):
        for p in range(size):
            u = [r[s, var, p] for r in (own, up, far, down) for s in range(2)]
            near = [u[(n - 1) % INST] - u[(n + 1) % INST] for n in range(INST)]
            second = [c2 * (u[(n - 2) % INST] - u[(n + 2) % INST]) for n in range(4)]
            for n in range(INST):
                s = c1 * near[n] - c3 * near[(n + 4) % INST]
                s = s + second[n] if n < 4 else s - second[n - 4]
                order[n // 2][n % 2, var, p] = s
    if not rims:
        return

    def add_ghost(p, factor):
        for var in range(up.shape[1]):
            for n in range(INST):
                at = (n % 2, var, p)
                order[n // 2][at] = order[n // 2][at] - factor * ghost[n // 4][n % 4, var]

    place = pl.ds(pl.multiple_of(lax.axis_index("inst") * 16, 16), 16)

    @pl.when(lax.axis_index("mesh") == 0)
    def _():
        add_ghost(size - 1, nu[0, place, :] + 0.5)

    @pl.when(lax.axis_index("mesh") == lax.axis_size("mesh") - 1)
    def _():
        add_ghost(size - 2, nu[nu.shape[0] - 1, place, :])


def stencil_kernel(nu, low, high, field, one, two):
    blocks, planes, rows, lanes = field.shape
    lane = lax.broadcasted_iota(jnp.int32, (rows, lanes), 1)
    row = lax.broadcasted_iota(jnp.int32, (rows, lanes), 0)
    for b in range(blocks):
        for p in range(planes):
            u = field[b, p]
            before = low[b] if p == 0 else field[b, p - 1]
            after = high[b] if p == planes - 1 else field[b, p + 1]
            left = jnp.where(lane == 0, 0.0, pltpu.roll(u, 1, 1))
            right = jnp.where(lane == lanes - 1, 0.0, pltpu.roll(u, lanes - 1, 1))
            above = jnp.where(row == 0, 0.0, pltpu.roll(u, 1, 0))
            below = jnp.where(row == rows - 1, 0.0, pltpu.roll(u, rows - 1, 0))
            lap = (before + after) + (above + below) + (left + right) - 6.0 * u
            at = (p - 1) % planes
            out, at = (one, at) if at < OUTER else (two, at - OUTER)
            out[b, at] = nu[p] * lap - (u - above) - 0.5 * (u - before)


def add_kernel(one, two, after, out):
    out[...] = one[...] + two[...]


def edge_kernel(total, orders, one, two, nu, *rest):
    out = rest[-1]
    planes, blocks, rows, lanes = out.shape
    mode = lax.broadcasted_iota(jnp.int32, (planes, MODES), 1)
    position = lax.broadcasted_iota(jnp.int32, (planes, MODES), 0) + lax.axis_index("mesh") * planes
    ghost = jnp.dot(
        turns(position, mode, orders, total),
        one[...] + two[...],
        precision=lax.Precision.HIGHEST,
        preferred_element_type=jnp.float32,
    )
    rotor = lax.axis_index("row") == 0
    hit = lax.broadcasted_iota(jnp.int32, (rows, lanes), 0) == jnp.where(rotor, rows - 1, 0)
    for p in range(planes):
        facing = jnp.where(rotor, nu[p, nu.shape[1] - 1 :, :], nu[p, :1, :] + 1.0)
        for b in range(blocks):
            value = facing * ghost[p : p + 1, b * lanes : (b + 1) * lanes]
            out[p, b] = jnp.where(hit, value, 0.0)


def final_kernel(start, chunk, near, inverse, edge, field, pre, *rest):
    new, residual, new_held, residual_held = rest[-6 - 2 * (not near) : -2 - 2 * (not near)]
    sems_in, sems = rest[-2:]
    count, planes, rows, lanes = field.shape
    size = pre.shape[1]
    base = (start + 1) % planes
    inst = lax.axis_index("inst")
    steps = (0, 1, 3, 2)
    arrivals = []
    if not near:
        held_in, pieces = rest[-4:-2]
    for b in range(0, count, chunk):
        if near:
            arrivals.append([])
            continue
        part = slice(b, b + chunk)
        pairs = [(pre.at[part], held_in.at[part])]
        pairs += [
            (rest[k].at[part], pieces.at[lax.rem(inst + step, 4), part])
            for k, step in enumerate(steps)
        ]
        arrivals.append(
            [
                pltpu.make_async_copy(x, y, sems_in.at[b // chunk, k])
                for k, (x, y) in enumerate(pairs)
            ]
        )
        for one in arrivals[-1]:
            one.start()
    tile = pl.ds(pl.multiple_of((1 - lax.axis_index("row")) * (rows - 8), 8), 8)
    runs = [(0, base, min(size, planes - base))]
    if base + size > planes:
        runs.append((planes - base, 0, base + size - planes))
    copies = []
    for j in range(0, count, 2):
        if j % chunk == 0:
            for one in arrivals[j // chunk]:
                one.wait()
        for p in range(size):
            plane = (base + p) % planes
            for b in (j, j + 1):
                for k, step in enumerate(steps):
                    if near:
                        at = pl.ds(pl.multiple_of(16 * lax.rem(inst + step, 4), 16), 16)
                        residual_held[b, p, at] = pre[b, p, at] - rest[k][b, p]
                    else:
                        at = pl.ds(16 * k, 16)
                        residual_held[b, p, at] = held_in[b, p, at] - pieces[k, b, p]
                residual_held[b, p, tile] = residual_held[b, p, tile] + edge[plane, b]
            high, low = split_bf16(
                jnp.concatenate([residual_held[j, p], residual_held[j + 1, p]], 1)
            )
            change = jnp.dot(
                inverse[...],
                jnp.concatenate([high, high, low], 0),
                preferred_element_type=jnp.float32,
            )
            new_held[j, p] = field[j, plane] + change[:, :lanes]
            new_held[j + 1, p] = field[j + 1, plane] + change[:, lanes:]
        if (j + 2) % chunk == 0:
            part = slice(j + 2 - chunk, j + 2)
            for held, out in ((residual_held, residual), (new_held, new)):
                for source, target, length in runs:
                    copies.append(
                        pltpu.make_async_copy(
                            held.at[part, source : source + length],
                            out.at[part, target : target + length],
                            sems.at[len(copies)],
                        )
                    )
                    copies[-1].start()
    for one in copies:
        one.wait()


def lag_weights(delta):
    total = 1.0 + jnp.cos(math.pi * delta)
    for k in range(1, INST // 2):
        total = total + 2.0 * jnp.cos(2.0 * math.pi * k / INST * delta)
    return total / INST


def local(state, viscosity, blade_counts, mode_orders):
    _, local_inst, variables, planes, rows, lanes = state.shape
    quarter = rows // 4
    blocks = local_inst * variables
    mesh_count = lax.axis_size("mesh")
    total = planes * mesh_count
    which = lax.axis_index("row")
    inst = lax.axis_index("inst")
    mesh_idx = lax.axis_index("mesh")
    counts = blade_counts.astype(jnp.float32)
    ratio = counts[1 - which] / counts[which]
    angle = 2.0 * math.pi / counts[which]
    field = state.reshape(blocks, planes, rows, lanes)
    nu = viscosity[0]
    first = mesh_idx == 0
    last = mesh_idx == mesh_count - 1

    def along(x, step):
        return lax.ppermute(x, "inst", [(j, (j + step) % 4) for j in range(4)])

    def in_hbm(*arrays):
        return [pltpu.with_memory_space_constraint(x, pltpu.HBM) for x in arrays]

    def exchange(up, down, far):
        from_down, from_up, from_far = along(up, 1), along(down, 3), along(far, 2)
        return from_up, from_down, from_far

    packed = pack(field, ((1, planes - 1), (0, 1)))
    gathered = exchange(*packed)

    top, bottom, own = pl.pallas_call(
        edges_kernel,
        out_shape=(shaped(blocks, rows, lanes),) * 2 + (shaped(blocks, planes, quarter, lanes),),
        in_specs=[HBM, VMEM],
        out_specs=(VMEM,) * 3,
        scratch_shapes=[pltpu.SemaphoreType.DMA((3, blocks))],
        compiler_params=params(),
        cost_estimate=cost(),
    )(pltpu.with_memory_space_constraint(field, pltpu.HBM), packed[0])
    low = lax.ppermute(top, "mesh", [(j, j + 1) for j in range(mesh_count - 1)])
    high = lax.ppermute(bottom, "mesh", [(j + 1, j) for j in range(mesh_count - 1)])

    split = (local_inst, variables)
    all_quarters = in_hbm(*(x.reshape(*split, planes, quarter, lanes) for x in (own, *gathered)))

    whole = shaped(*field.shape)
    at_once = 2
    slab = pl.BlockSpec((at_once, planes, rows, lanes), lambda b: (b, 0, 0, 0))
    plane = pl.BlockSpec((at_once, rows, lanes), lambda b: (b, 0, 0))
    pre_one, pre_two = pl.pallas_call(
        stencil_kernel,
        grid=(blocks // at_once,),
        out_shape=(
            pltpu.HBM((blocks, OUTER, rows, lanes), jnp.float32),
            pltpu.HBM((blocks, planes - OUTER, rows, lanes), jnp.float32),
        ),
        in_specs=[pl.BlockSpec((planes, rows, lanes), lambda b: (0, 0, 0)), plane, plane, slab],
        out_specs=(
            pl.BlockSpec((at_once, OUTER, rows, lanes), lambda b: (b, 0, 0, 0)),
            pl.BlockSpec((at_once, planes - OUTER, rows, lanes), lambda b: (b, 0, 0, 0)),
        ),
        compiler_params=params(),
        cost_estimate=cost(),
    )(nu, *in_hbm(low, high), field)

    harmonics = pl.pallas_call(
        functools.partial(harmonics_kernel, total),
        out_shape=shaped(MODES, blocks * lanes),
        grid=(1,),
        in_specs=[
            SMEM,
            VMEM,
            pl.BlockSpec((blocks, planes, 8, lanes), lambda b: (0, 0, 0, 0)),
            pl.BlockSpec((blocks, planes, 8, lanes), lambda b: (0, 0, rows // 8 - 1, 0)),
        ],
        out_specs=pl.BlockSpec((MODES, blocks * lanes), lambda b: (0, 0)),
        compiler_params=params(),
        cost_estimate=cost(),
    )(mode_orders, packed[0], field, field)

    def crossing(flip):
        return [
            (r * mesh_count + m, (1 - r) * mesh_count + (m ^ flip))
            for r in range(2)
            for m in range(mesh_count)
        ]

    def doubled(x, flip):
        return x + lax.ppermute(x, "mesh", [(m, m ^ flip) for m in range(mesh_count)])

    two_ways = [lax.ppermute(harmonics, ("row", "mesh"), crossing(flip)) for flip in (0, 1)]
    harmonics = two_ways[0] + two_ways[1]
    early = lax.ppermute(harmonics, "mesh", [(m, m ^ 2) for m in range(mesh_count)])

    def sources(start, size, rims, after=()):
        at_once = 3
        piece_in = pl.BlockSpec(
            (2, at_once, size, quarter, lanes), lambda b: (0, b, start // size, 0, 0)
        )
        rim_specs = [
            pl.BlockSpec((INST // 2, at_once, quarter, lanes), lambda b: (0, b, 0, 0)),
            pl.BlockSpec((INST // 2, at_once, quarter, lanes), lambda b: (0, b, 0, 0)),
            pl.BlockSpec((planes, rows, lanes), lambda b: (0, 0, 0)),
        ]
        def kernel(*refs):
            inputs, outputs = refs[: -4 - len(after)], refs[-4:]
            source_kernel(bool(rims), *inputs, *outputs)

        outs = pl.pallas_call(
            kernel,
            out_shape=(pltpu.HBM((*split, size, quarter, lanes), jnp.float32),) * 4,
            grid=(variables // at_once,),
            in_specs=[SMEM] + [piece_in] * 4 + rim_specs[: len(rims)] + [ANY] * len(after),
            out_specs=(
                pl.BlockSpec((2, at_once, size, quarter, lanes), lambda b: (0, b, 0, 0, 0)),
            )
            * 4,
            compiler_params=params(),
            cost_estimate=cost(),
        )(ratio[None], *all_quarters, *rims, *after)
        own, up, down, far = (x.reshape(blocks, size, quarter, lanes) for x in outs)
        return (own, *exchange(up, down, far))

    one_source = sources(0, OUTER, (), after=(*in_hbm(pre_one), early))

    ghost_shape = shaped(INST // 2, variables, quarter, lanes)

    outermost = pl.BlockSpec((2, variables, 2, quarter, lanes), lambda b: (0, 0, 3, 0, 0))
    ghost_out = pl.pallas_call(
        mix_kernel,
        out_shape=(ghost_shape,) * 2,
        grid=(1,),
        in_specs=[SMEM] + [outermost] * 4 + [ANY],
        out_specs=(pl.BlockSpec(ghost_shape.shape, lambda b: (0, 0, 0, 0)),) * 2,
        compiler_params=params(),
        cost_estimate=cost(),
    )(
        blade_counts,
        *all_quarters,
        *in_hbm(one_source[0]),
    )
    ghost = [
        lax.ppermute(part, "mesh", [(mesh_count - 1, 0), (0, mesh_count - 1)]) for part in ghost_out
    ]

    harmonics = pl.pallas_call(
        add_kernel,
        out_shape=harmonics,
        in_specs=[VMEM, VMEM, ANY],
        out_specs=VMEM,
        compiler_params=params(),
        cost_estimate=cost(),
    )(harmonics, early, ghost_out[0])
    harmonics = doubled(harmonics, 4)
    opposite = lax.ppermute(harmonics, "mesh", [(m, m ^ 8) for m in range(mesh_count)])
    two_source = sources(OUTER, planes - OUTER, (*ghost, nu), after=(opposite,))

    edge = pl.pallas_call(
        functools.partial(edge_kernel, total),
        out_shape=shaped(planes, blocks, 8, lanes),
        in_specs=[SMEM, VMEM, VMEM, VMEM] + [ANY] * 3,
        out_specs=VMEM,
        compiler_params=params(),
        cost_estimate=cost(),
    )(
        mode_orders,
        harmonics,
        opposite,
        nu,
        *one_source[1:],
    )

    inverse = jnp.asarray(inverse_parts(rows))
    kept = ()
    for start, size, group, pre in ((0, OUTER, one_source, pre_one), (OUTER, planes - OUTER, two_source, pre_two)):
        given = 4 + len(group)
        near = size < 4
        if near:
            group = [pltpu.with_memory_space_constraint(x, pltpu.VMEM) for x in group]
            given_in = (pre, *group)
        else:
            given_in = (*in_hbm(pre, group[0]), *group[1:])
        kept = pl.pallas_call(
            functools.partial(final_kernel, start, 2, near),
            out_shape=(pltpu.HBM(field.shape, jnp.float32),) * 2,
            in_specs=[VMEM] * 3
            + ([VMEM] * 5 if near else [HBM] * 2 + [ANY] * 3)
            + [HBM] * len(kept),
            out_specs=(HBM,) * 2,
            scratch_shapes=[pltpu.VMEM((blocks, size, rows, lanes), jnp.float32)] * (2 + (not near))
            + [pltpu.VMEM((4, blocks, size, quarter, lanes), jnp.float32)] * (not near)
            + [pltpu.SemaphoreType.DMA((blocks, 5)), pltpu.SemaphoreType.DMA((4 * blocks,))],
            input_output_aliases={given: 0, given + 1: 1} if kept else {},
            compiler_params=params(),
            cost_estimate=cost(),
        )(inverse, edge, field, *given_in, *kept)
    new, residual = kept
    return (new.reshape(state.shape), residual.reshape(state.shape))


def solution(mesh):
    spread = P("row", "inst", None, "mesh", None, None)
    return jax.shard_map(
        local,
        mesh=mesh,
        in_specs=(spread, P("row", "mesh", None, None), P(), P()),
        out_specs=(spread, spread),
        check_vma=False,
    )
```
